32 devices in a mesh: rows: 4 (over y, x), cols: 8 (over z, core).
Axes of the slice: x: 2, y: 2, z: 4, core: 2. Of those that a mesh axis runs over, the one named last changes fastest.
Arguments:
- left_image: bfloat16 [32, 2048], P(('rows', 'cols')), may hold values from -8 to 8, as said below
- right_image: bfloat16 [32, 2048], P(('rows', 'cols')), may hold values from -8 to 8, as said below
- ranges: int32 [8, 2], replicated, may hold values from 0 to 63, as said below
Outputs:
- best_score: float32 [32, 2048], P('rows', 'cols')
The draws below stay inside these ranges and needn't reach their ends.
Inputs may be any that keep to these rules, and one draw needn't show every extreme that they name: `left_image`: pixel values. `right_image`: pixel values. `ranges`: row t holds tile t's first disparity (column 0, 0 to 63) and its number of blocks of 128 disparities (column 1, 1 to 2); some tile has 2 blocks, some tile starts at 0 and some at 63.
All inputs are finite; a program needn't handle non-finite values.
Results may differ from the reference program's by a relative error of at most 0.0003.
Values may be sent and summed in bfloat16 or wider, within the bound.
No kernel may reach another device: no remote copies, remote signals or barrier semaphores. Data moves between devices by JAX's collectives and lax.ppermute only.
A program may use at most 128 MiB of HBM per device.

```python
import math
import jax
import jax.numpy as jnp
from jax import lax

TW = 256
DB = 128
MAXB = 2
SMAX = 64
TILES = 8
H = 32
W = 2048


def texture(key):
    amp_key, noise_key = jax.random.split(jax.random.fold_in(key, 11))
    levels = jnp.exp(jax.random.uniform(amp_key, (H // 8, W // 8), jnp.float32, math.log(0.03), math.log(1.0)))
    grain = jnp.clip(jax.random.normal(noise_key, (H, W), jnp.float32), -4.0, 4.0)
    scale = jnp.repeat(jnp.repeat(levels, 8, axis=0), 8, axis=1)
    return (scale * grain, scale)


def draw_left_image(key, part):
    pattern, scale = texture(key)
    return pattern.astype(jnp.bfloat16)


def draw_right_image(key, part):
    pattern, scale = texture(key)
    shifts = jax.random.randint(jax.random.fold_in(key, 13), (H // 8,), 0, SMAX + DB * MAXB, jnp.int32)
    per_row = jnp.repeat(shifts, 8)
    columns = jnp.arange(W, dtype=jnp.int32)[None, :] + per_row[:, None]
    inside = columns < W
    moved = jnp.take_along_axis(pattern, jnp.minimum(columns, W - 1), axis=1)
    moved = jnp.where(inside, moved, 0.0)
    grain = jnp.clip(jax.random.normal(jax.random.fold_in(key, 17), (H, W), jnp.float32), -4.0, 4.0)
    return (0.8 * moved + 0.4 * scale * grain).astype(jnp.bfloat16)


def draw_ranges(key, part):
    first_key, count_key, pick_key = jax.random.split(jax.random.fold_in(key, 19), 3)
    starts = jax.random.randint(first_key, (TILES,), 0, SMAX, jnp.int32)
    counts = jax.random.randint(count_key, (TILES,), 1, MAXB + 1, jnp.int32)
    heavy = jax.random.randint(pick_key, (), 0, TILES, jnp.int32)
    tile_ids = jnp.arange(TILES, dtype=jnp.int32)
    counts = jnp.where(tile_ids == heavy, MAXB, counts)
    starts = jnp.where(tile_ids == heavy, 0, starts)
    starts = jnp.where(tile_ids == (heavy + 1) % TILES, SMAX - 1, starts)
    return jnp.stack([starts, counts], axis=1)


def setup_inputs(seed: int = 0) -> dict:
    splits = jax.random.split(jax.random.key(seed), 4)
    return {
        "left_image": draw_left_image(jax.random.fold_in(splits[3], 71), 0),
        "right_image": draw_right_image(jax.random.fold_in(splits[3], 71), 0),
        "ranges": draw_ranges(jax.random.fold_in(splits[3], 71), 0),
    }


def box_sum(values, along):
    length = values.shape[along] - 6
    running = lax.slice_in_dim(values, 0, length, axis=along)
    for offset in range(1, 7):
        running = running + lax.slice_in_dim(values, offset, offset + length, axis=along)
    return running

def window_sums(values):
    return box_sum(box_sum(values, values.ndim - 1), values.ndim - 2)

def moments(pixels):
    average = window_sums(pixels) / 49.0
    spread = jnp.maximum(window_sums(pixels * pixels) / 49.0 - average * average, 0.01)
    return (average, spread)

def skewed(values, columns, lanes):
    lead = values.shape[:-1]
    length = values.shape[-1]
    tiled = jnp.broadcast_to(values[..., None, :], lead + (lanes + 1, length))
    flat = tiled.reshape(lead + ((lanes + 1) * length,))
    sheared = flat[..., :lanes * (length + 1)].reshape(lead + (lanes, length + 1))
    sheared = jnp.flip(sheared[..., :columns], axis=-2)
    return jnp.swapaxes(sheared, -1, -2)

def best_scores(left_pad, right_pad, block_count):
    height = left_pad.shape[0] - 6
    tile_width = left_pad.shape[1] - 6
    left_mean, left_spread = moments(left_pad)
    right_mean, right_spread = moments(right_pad)
    right_stats = jnp.stack([right_mean, right_spread])
    col_block = 256 if tile_width % 256 == 0 else 128
    col_blocks = tile_width // col_block

    def visitor(step_index, current):
        block_id = step_index // col_blocks
        col_start = step_index % col_blocks * col_block
        source_at = col_start + 61 + DB * (MAXB - block_id) - (DB - 1)
        right_cut = lax.dynamic_slice_in_dim(right_pad, source_at, col_block + 6 + DB - 1, 1)
        right_lanes = skewed(right_cut, col_block + 6, DB)
        left_cut = lax.dynamic_slice_in_dim(left_pad, col_start, col_block + 6, 1)
        product = left_cut[:, :, None] * right_lanes
        cross_term = box_sum(box_sum(product, 1), 0) / 49.0
        stats_cut = lax.dynamic_slice_in_dim(right_stats, source_at, col_block + DB - 1, 2)
        stats_lanes = skewed(stats_cut, col_block, DB)
        mean_l = lax.dynamic_slice_in_dim(left_mean, col_start, col_block, 1)[:, :, None]
        spread_l = lax.dynamic_slice_in_dim(left_spread, col_start, col_block, 1)[:, :, None]
        scores = (cross_term - mean_l * stats_lanes[0]) / jnp.sqrt(spread_l * stats_lanes[1])
        best = lax.optimization_barrier(jnp.max(scores, axis=-1))
        old = lax.dynamic_slice_in_dim(current, col_start, col_block, 1)
        return lax.dynamic_update_slice_in_dim(current, jnp.maximum(old, best), col_start, 1)
    initial = jnp.full((height, tile_width), -2.0, jnp.float32)
    return lax.fori_loop(0, block_count * col_blocks, visitor, initial)

def reference(left_image, right_image, ranges):
    lead_pad = SMAX + DB * MAXB + 64
    window_width = TW + DB * (MAXB + 1)
    left_full = jnp.pad(left_image.astype(jnp.float32), 3)
    right_full = jnp.pad(right_image.astype(jnp.float32), ((3, 3), (lead_pad, 64)))

    def per_tile(tile_id):
        left_pad = lax.dynamic_slice_in_dim(left_full, tile_id * TW, TW + 6, 1)
        window_at = tile_id * TW - ranges[tile_id, 0] + SMAX
        right_pad = lax.dynamic_slice_in_dim(right_full, window_at, window_width, 1)
        return best_scores(left_pad, right_pad, ranges[tile_id, 1])
    tiles_out = lax.map(per_tile, jnp.arange(TILES, dtype=jnp.int32))
    return jnp.transpose(tiles_out, (1, 0, 2)).reshape(H, W)
```

```python
import functools

import jax
import jax.numpy as jnp
from jax import lax
from jax.experimental import pallas as pl
from jax.experimental.pallas import tpu as pltpu
from jax.sharding import PartitionSpec as P

DB = 128
MAXB = 2
LANES = 128
LEFT_TILES = 3
RIGHT_TILES = 5
TILES = LEFT_TILES + RIGHT_TILES
LEAD = 3
GROUP = 8
FAR = 3.0e37
VMEM = pl.BlockSpec(memory_space=pltpu.VMEM)
SMEM = pl.BlockSpec(memory_space=pltpu.SMEM)


def pack_kernel(bands, tiles, left_ref, right_ref, ranges_ref, out_ref, low_ref, left_rows, right_rows):
    strip, width = left_ref.shape
    per_tile = width // tiles // LANES
    lane = lax.broadcasted_iota(jnp.int32, (8, LANES), 1)
    low = MAXB * DB - DB * ranges_ref[lax.axis_index("cols"), 1]
    low_ref[...] = jnp.full(low_ref.shape, low, jnp.int32)
    left_rows[...] = jnp.zeros_like(left_rows)
    right_rows[...] = jnp.zeros_like(right_rows)
    for line in range(strip):
        for chunk in range(width // LANES):
            cut = slice(chunk * LANES, (chunk + 1) * LANES)
            left_rows[LEAD + chunk : LEAD + chunk + 1, :] = left_ref[line : line + 1, cut].astype(jnp.float32)
            right_rows[LEAD + chunk : LEAD + chunk + 1, :] = right_ref[line : line + 1, cut].astype(jnp.float32)

        def shifted(rows, begin):
            first = begin // LANES
            offset = begin - first * LANES
            here = pltpu.roll(rows[pl.ds(first, 8), :], LANES - offset, 1)
            after = pltpu.roll(rows[pl.ds(first + 1, 8), :], LANES - offset, 1)
            return jnp.where(lane < LANES - offset, here, after)

        for tile in range(tiles):
            base = (LEAD + tile * per_tile) * LANES
            left_part = shifted(left_rows, base - 3)[:LEFT_TILES]
            right_part = shifted(right_rows, base - 3 - (MAXB * DB - 1) - ranges_ref[tile, 0])[:RIGHT_TILES]
            piece = jnp.concatenate([left_part, right_part], 0).astype(jnp.bfloat16)
            for band in range(bands):
                out_ref[band * tiles + tile, line] = piece


def pack(left, right, ranges, bands, tiles):
    strip, width = left.shape
    rows = LEAD + width // LANES + 13
    return pl.pallas_call(
        functools.partial(pack_kernel, bands, tiles),
        out_shape=[
            jax.ShapeDtypeStruct((bands * tiles, strip, TILES, LANES), jnp.bfloat16),
            jax.ShapeDtypeStruct((8, LANES), jnp.int32),
        ],
        in_specs=[VMEM, VMEM, SMEM],
        out_specs=[VMEM, VMEM],
        scratch_shapes=[pltpu.VMEM((rows, LANES), jnp.float32), pltpu.VMEM((rows, LANES), jnp.float32)],
        compiler_params=pltpu.CompilerParams(vmem_limit_bytes=8 * 2**20),
    )(left, right, ranges)


def ahead(values, by, axis):
    return pltpu.roll(values, values.shape[axis] - by, axis)


def box(values, axis):
    two = values + ahead(values, 1, axis)
    four = two + ahead(two, 2, axis)
    return four + ahead(two, 4, axis) + ahead(values, 6, axis)


def moments(pixels):
    total = box(box(pixels, 1), 0)[:GROUP]
    mean = total / 49.0
    spread = jnp.maximum(box(box(pixels * pixels, 1), 0)[:GROUP] / 49.0 - mean * mean, 0.01)
    return total, mean, spread


def parts(values):
    high = values.astype(jnp.bfloat16)
    rest = values - high.astype(jnp.float32)
    middle = rest.astype(jnp.bfloat16)
    low = (rest - middle.astype(jnp.float32)).astype(jnp.bfloat16)
    return [p.astype(jnp.float32) for p in (high, middle, low)]


def score_kernel(height, lines_ref, low_ref, out_ref, rows):
    band_rows, tile_width = out_ref.shape
    row = lax.broadcasted_iota(jnp.int32, (16, 1), 0)
    row8 = lax.broadcasted_iota(jnp.int32, (GROUP, 1), 0)
    span = MAXB * DB + LANES
    past = lax.broadcasted_iota(jnp.int32, (span, LANES), 0) - lax.broadcasted_iota(jnp.int32, (span, LANES), 1)
    inside = (past >= low_ref[0:1, :]) & (past < MAXB * DB)
    cap = jnp.where(inside, FAR, -FAR)
    rows[...] = jnp.zeros_like(rows)
    for group in range(band_rows // GROUP):
        first = lax.axis_index("rows") * band_rows + group * GROUP - 3
        for i in range(GROUP + 6):
            y = first + i
            valid = ((y >= 0) & (y < height)).astype(jnp.float32)
            line = lines_ref[jnp.clip(y, 0, height - 1)].astype(jnp.float32)
            rows[i * TILES : (i + 1) * TILES, :] = line * valid
        tiles = [rows[pl.ds(t, 16, stride=TILES), :] for t in range(TILES)]
        left = jnp.concatenate(tiles[:LEFT_TILES], 1)
        right = jnp.concatenate(tiles[LEFT_TILES:], 1)
        left_total, _, left_spread = moments(left)
        _, right_mean, right_spread = moments(right)
        reach = tile_width + MAXB * DB
        left_scale = lax.rsqrt(left_spread[:, :tile_width]) * (1.0 / 49.0)
        right_scale = jnp.transpose(lax.rsqrt(right_spread[:, :reach]))
        left_parts = parts(-left_total[:, :tile_width])
        right_parts = parts(right_mean[:, :reach])
        shifted_left = [(left if j == 0 else ahead(left, j, 1))[:, :tile_width] for j in range(7)]
        shifted_right = [(right if j == 0 else ahead(right, j, 1))[:, :reach] for j in range(7)]
        right_side = jnp.concatenate(shifted_right + [b for _ in range(3) for b in right_parts], 0)
        right_side = jnp.transpose(right_side).astype(jnp.bfloat16)
        result = []
        for y in range(GROUP):
            window = ((row >= y) & (row < y + 7)).astype(jnp.float32)
            only = (row8 == y).astype(jnp.float32)
            left_side = [v * window for v in shifted_left] + [a * only for a in left_parts for _ in range(3)]
            left_side = jnp.concatenate(left_side, 0).astype(jnp.bfloat16)
            halves = []
            for block in range(tile_width // LANES):
                at = block * LANES
                products = jnp.dot(
                    right_side[at : at + span],
                    left_side[:, at : at + LANES],
                    preferred_element_type=jnp.float32,
                )
                scaled = products * right_scale[at : at + span, y : y + 1]
                halves.append(jnp.max(jnp.minimum(scaled, cap), axis=0, keepdims=True))
            result.append(jnp.concatenate(halves, 1))
        best = jnp.concatenate(result, 0) * left_scale
        out_ref[group * GROUP : (group + 1) * GROUP, :] = jnp.maximum(best, -2.0)


def score(lines, low, band_rows, tile_width):
    return pl.pallas_call(
        functools.partial(score_kernel, lines.shape[0]),
        out_shape=jax.ShapeDtypeStruct((band_rows, tile_width), jnp.float32),
        in_specs=[VMEM, VMEM],
        out_specs=VMEM,
        scratch_shapes=[pltpu.VMEM((16 * TILES, LANES), jnp.float32)],
        compiler_params=pltpu.CompilerParams(vmem_limit_bytes=16 * 2**20),
    )(lines, low)


def on_device(left_image, right_image, ranges):
    bands, tiles = lax.axis_size("rows"), lax.axis_size("cols")
    strip, width = left_image.shape
    pieces, low = pack(left_image, right_image, ranges, bands, tiles)
    lines = lax.all_to_all(pieces, ("rows", "cols"), split_axis=0, concat_axis=0, tiled=True)
    lines = lines.reshape(bands * tiles * strip, TILES, LANES)
    return score(lines, low, strip * tiles, width // tiles)


def solution(mesh):
    return jax.shard_map(
        on_device,
        mesh=mesh,
        in_specs=(P(("rows", "cols"), None), P(("rows", "cols"), None), P()),
        out_specs=P("rows", "cols"),
        check_vma=False,
    )
```

```python
import functools

import jax
import jax.numpy as jnp
from jax import lax
from jax.experimental import pallas as pl
from jax.experimental.pallas import tpu as pltpu
from jax.sharding import PartitionSpec as P

DB = 128
MAXB = 2
LANES = 128
LEFT_TILES = 3
RIGHT_TILES = 5
TILES = LEFT_TILES + RIGHT_TILES
LEAD = 3
GROUP = 8
FAR = 3.0e37
VMEM = pl.BlockSpec(memory_space=pltpu.VMEM)
HBM = pl.BlockSpec(memory_space=pltpu.HBM)


def pack_kernel(bands, tiles, left_hbm, right_hbm, ranges_hbm, out_ref, low_ref, left_ref, right_ref, ranges_ref, left_rows, right_rows, sems):
    copies = [
        pltpu.make_async_copy(source, target, sems.at[i])
        for i, (source, target) in enumerate(
            [(ranges_hbm, ranges_ref), (left_hbm, left_ref), (right_hbm, right_ref)]
        )
    ]
    for copy in copies:
        copy.start()
    strip, width = left_ref.shape
    chunks = width // LANES
    per_tile = chunks // tiles
    lane = lax.broadcasted_iota(jnp.int32, (8, LANES), 1)
    left_rows[...] = jnp.zeros_like(left_rows)
    right_rows[...] = jnp.zeros_like(right_rows)
    for copy in copies:
        copy.wait()
    low = MAXB * DB - DB * ranges_ref[1, lax.axis_index("cols")]
    low_ref[...] = jnp.full(low_ref.shape, low, jnp.int32)

    def shifted(rows, first, by):
        here = pltpu.roll(rows[first : first + 8, :], by, 1)
        after = pltpu.roll(rows[first + 1 : first + 9, :], by, 1)
        return jnp.where(lane < by, here, after)

    for line in range(strip):
        for chunk in range(chunks):
            cut = slice(chunk * LANES, (chunk + 1) * LANES)
            at = slice(LEAD + chunk, LEAD + chunk + 1)
            left_rows[at, :] = left_ref[line : line + 1, cut].astype(jnp.float32)
            right_rows[at, :] = right_ref[line : line + 1, cut].astype(jnp.float32)
        for tile in range(tiles):
            first = LEAD + tile * per_tile
            left_part = shifted(left_rows, first - 1, 3)[:LEFT_TILES]
            right_part = shifted(right_rows, first - 3, 2 + ranges_ref[0, tile])[:RIGHT_TILES]
            piece = jnp.concatenate([left_part, right_part], 0).astype(jnp.bfloat16)
            for band in range(bands):
                out_ref[band * tiles + tile, line] = piece


def pack(left, right, ranges, bands, tiles):
    strip, width = left.shape
    rows = LEAD + width // LANES + 13
    return pl.pallas_call(
        functools.partial(pack_kernel, bands, tiles),
        out_shape=[
            jax.ShapeDtypeStruct((bands * tiles, strip, TILES, LANES), jnp.bfloat16),
            jax.ShapeDtypeStruct((8, LANES), jnp.int32),
        ],
        in_specs=[HBM, HBM, HBM],
        out_specs=[VMEM, VMEM],
        scratch_shapes=[
            pltpu.VMEM(left.shape, left.dtype),
            pltpu.VMEM(right.shape, right.dtype),
            pltpu.SMEM((2, tiles), jnp.int32),
            pltpu.VMEM((rows, LANES), jnp.float32),
            pltpu.VMEM((rows, LANES), jnp.float32),
            pltpu.SemaphoreType.DMA((3,)),
        ],
        compiler_params=pltpu.CompilerParams(vmem_limit_bytes=8 * 2**20),
    )(*[pltpu.with_memory_space_constraint(v, pltpu.HBM) for v in (left, right, ranges.T)])


def ahead(values, by, axis):
    return pltpu.roll(values, values.shape[axis] - by, axis)


def box(values, axis):
    two = values + ahead(values, 1, axis)
    four = two + ahead(two, 2, axis)
    return four + ahead(two, 4, axis) + ahead(values, 6, axis)


def moments(pixels):
    total = box(box(pixels, 1), 0)[:GROUP]
    mean = total / 49.0
    spread = jnp.maximum(box(box(pixels * pixels, 1), 0)[:GROUP] / 49.0 - mean * mean, 0.01)
    return total, mean, spread


def parts(values):
    high = values.astype(jnp.bfloat16)
    rest = values - high.astype(jnp.float32)
    middle = rest.astype(jnp.bfloat16)
    low = (rest - middle.astype(jnp.float32)).astype(jnp.bfloat16)
    return [p.astype(jnp.float32) for p in (high, middle, low)]


def score_kernel(height, lines_ref, low_ref, out_ref, rows):
    band_rows, tile_width = out_ref.shape
    row = lax.broadcasted_iota(jnp.int32, (16, 1), 0)
    row8 = lax.broadcasted_iota(jnp.int32, (GROUP, 1), 0)
    span = MAXB * DB + LANES
    past = lax.broadcasted_iota(jnp.int32, (span, LANES), 0) - lax.broadcasted_iota(jnp.int32, (span, LANES), 1)
    inside = (past >= low_ref[0:1, :]) & (past < MAXB * DB)
    cap = jnp.where(inside, FAR, -FAR)
    rows[...] = jnp.zeros_like(rows)
    for group in range(band_rows // GROUP):
        first = lax.axis_index("rows") * band_rows + group * GROUP - 3
        for i in range(GROUP + 6):
            y = first + i
            valid = ((y >= 0) & (y < height)).astype(jnp.float32)
            line = lines_ref[jnp.clip(y, 0, height - 1)].astype(jnp.float32)
            rows[i * TILES : (i + 1) * TILES, :] = line * valid
        tiles = [rows[pl.ds(t, 16, stride=TILES), :] for t in range(TILES)]
        left = jnp.concatenate(tiles[:LEFT_TILES], 1)
        right = jnp.concatenate(tiles[LEFT_TILES:], 1)
        left_total, _, left_spread = moments(left)
        _, right_mean, right_spread = moments(right)
        reach = tile_width + MAXB * DB
        left_scale = lax.rsqrt(left_spread[:, :tile_width]) * (1.0 / 49.0)
        right_scale = jnp.transpose(lax.rsqrt(right_spread[:, :reach]))
        left_parts = parts(-left_total[:, :tile_width])
        right_parts = parts(right_mean[:, :reach])
        shifted_left = [(left if j == 0 else ahead(left, j, 1))[:, :tile_width] for j in range(7)]
        shifted_right = [(right if j == 0 else ahead(right, j, 1))[:, :reach] for j in range(7)]
        right_side = jnp.concatenate(shifted_right + [b for _ in range(3) for b in right_parts], 0)
        right_side = jnp.transpose(right_side).astype(jnp.bfloat16)
        result = []
        for y in range(GROUP):
            window = ((row >= y) & (row < y + 7)).astype(jnp.float32)
            only = (row8 == y).astype(jnp.float32)
            left_side = [v * window for v in shifted_left] + [a * only for a in left_parts for _ in range(3)]
            left_side = jnp.concatenate(left_side, 0).astype(jnp.bfloat16)
            halves = []
            for block in range(tile_width // LANES):
                at = block * LANES
                products = jnp.dot(
                    right_side[at : at + span],
                    left_side[:, at : at + LANES],
                    preferred_element_type=jnp.float32,
                )
                scaled = products * right_scale[at : at + span, y : y + 1]
                halves.append(jnp.max(jnp.minimum(scaled, cap), axis=0, keepdims=True))
            result.append(jnp.concatenate(halves, 1))
        best = jnp.concatenate(result, 0) * left_scale
        out_ref[group * GROUP : (group + 1) * GROUP, :] = jnp.maximum(best, -2.0)


def score(lines, low, band_rows, tile_width):
    return pl.pallas_call(
        functools.partial(score_kernel, lines.shape[0]),
        out_shape=jax.ShapeDtypeStruct((band_rows, tile_width), jnp.float32),
        in_specs=[VMEM, VMEM],
        out_specs=VMEM,
        scratch_shapes=[pltpu.VMEM((16 * TILES, LANES), jnp.float32)],
        compiler_params=pltpu.CompilerParams(vmem_limit_bytes=16 * 2**20),
    )(lines, low)


def on_device(left_image, right_image, ranges):
    bands, tiles = lax.axis_size("rows"), lax.axis_size("cols")
    strip, width = left_image.shape
    pieces, low = pack(left_image, right_image, ranges, bands, tiles)
    lines = lax.all_to_all(pieces, ("rows", "cols"), split_axis=0, concat_axis=0, tiled=True)
    lines = lines.reshape(bands * tiles * strip, TILES, LANES)
    return score(lines, low, strip * tiles, width // tiles)


def solution(mesh):
    return jax.shard_map(
        on_device,
        mesh=mesh,
        in_specs=(P(("rows", "cols"), None), P(("rows", "cols"), None), P()),
        out_specs=P("rows", "cols"),
        check_vma=False,
    )
```

```python
import functools

import jax
import jax.numpy as jnp
from jax import lax
from jax.experimental import pallas as pl
from jax.experimental.pallas import tpu as pltpu
from jax.sharding import PartitionSpec as P

DB = 128
MAXB = 2
LANES = 128
LEFT_TILES = 3
RIGHT_TILES = 5
TILES = LEFT_TILES + RIGHT_TILES
LEAD = 3
GROUP = 8
FAR = 3.0e37
VMEM = pl.BlockSpec(memory_space=pltpu.VMEM)
HBM = pl.BlockSpec(memory_space=pltpu.HBM)


def pack_kernel(bands, tiles, left_hbm, right_hbm, ranges_hbm, out_ref, low_ref, left_ref, right_ref, ranges_ref, left_rows, right_rows, sems):
    copies = [
        pltpu.make_async_copy(source, target, sems.at[i])
        for i, (source, target) in enumerate(
            [(ranges_hbm, ranges_ref), (left_hbm, left_ref), (right_hbm, right_ref)]
        )
    ]
    for copy in copies:
        copy.start()
    strip, width = left_ref.shape
    chunks = width // LANES
    per_tile = chunks // tiles
    lane = lax.broadcasted_iota(jnp.int32, (8, LANES), 1)
    left_rows[...] = jnp.zeros_like(left_rows)
    right_rows[...] = jnp.zeros_like(right_rows)
    for copy in copies:
        copy.wait()
    low = MAXB * DB - DB * ranges_ref[1, lax.axis_index("cols")]
    low_ref[...] = jnp.full(low_ref.shape, low, jnp.int32)

    def shifted(rows, first, by):
        here = pltpu.roll(rows[first : first + 8, :], by, 1)
        after = pltpu.roll(rows[first + 1 : first + 9, :], by, 1)
        return jnp.where(lane < by, here, after)

    for line in range(strip):
        for chunk in range(chunks):
            cut = slice(chunk * LANES, (chunk + 1) * LANES)
            at = slice(LEAD + chunk, LEAD + chunk + 1)
            left_rows[at, :] = left_ref[line : line + 1, cut].astype(jnp.float32)
            right_rows[at, :] = right_ref[line : line + 1, cut].astype(jnp.float32)
        for tile in range(tiles):
            first = LEAD + tile * per_tile
            left_part = shifted(left_rows, first - 1, 3)[:LEFT_TILES]
            right_part = shifted(right_rows, first - 3, 2 + ranges_ref[0, tile])[:RIGHT_TILES]
            piece = jnp.concatenate([left_part, right_part], 0).astype(jnp.bfloat16)
            for band in range(bands):
                out_ref[band * tiles + tile, line] = piece


def pack(left, right, ranges, bands, tiles):
    strip, width = left.shape
    rows = LEAD + width // LANES + 13
    return pl.pallas_call(
        functools.partial(pack_kernel, bands, tiles),
        out_shape=[
            jax.ShapeDtypeStruct((bands * tiles, strip, TILES, LANES), jnp.bfloat16),
            jax.ShapeDtypeStruct((8, LANES), jnp.int32),
        ],
        in_specs=[HBM, HBM, HBM],
        out_specs=[VMEM, VMEM],
        scratch_shapes=[
            pltpu.VMEM(left.shape, left.dtype),
            pltpu.VMEM(right.shape, right.dtype),
            pltpu.SMEM((2, tiles), jnp.int32),
            pltpu.VMEM((rows, LANES), jnp.float32),
            pltpu.VMEM((rows, LANES), jnp.float32),
            pltpu.SemaphoreType.DMA((3,)),
        ],
        compiler_params=pltpu.CompilerParams(vmem_limit_bytes=8 * 2**20),
    )(*[pltpu.with_memory_space_constraint(v, pltpu.HBM) for v in (left, right, ranges.T)])


def ahead(values, by, axis):
    if by == 0:
        return values
    return pltpu.roll(values, values.shape[axis] - by, axis)


def column_sum(values):
    two = values + ahead(values, 1, 0)
    four = two + ahead(two, 2, 0)
    return (four + ahead(two, 4, 0) + ahead(values, 6, 0))[:GROUP]


def moments(shifted):
    total = column_sum(sum(shifted[1:], shifted[0]))
    squares = [v * v for v in shifted]
    mean = total * (1.0 / 49.0)
    spread = column_sum(sum(squares[1:], squares[0])) * (1.0 / 49.0) - mean * mean
    return total, mean, lax.rsqrt(jnp.maximum(spread, 0.01))


def parts(values):
    high = values.astype(jnp.bfloat16)
    rest = values - high.astype(jnp.float32)
    middle = rest.astype(jnp.bfloat16)
    low = (rest - middle.astype(jnp.float32)).astype(jnp.bfloat16)
    return [high, middle, low]


def score_kernel(height, lines_ref, low_ref, out_ref, rows):
    band_rows, tile_width = out_ref.shape
    reach = tile_width + MAXB * DB
    span = MAXB * DB + LANES
    row = lax.broadcasted_iota(jnp.int32, (16, tile_width), 0)
    row8 = lax.broadcasted_iota(jnp.int32, (GROUP, tile_width), 0)
    past = lax.broadcasted_iota(jnp.int32, (span, LANES), 0) - lax.broadcasted_iota(jnp.int32, (span, LANES), 1)
    inside = (past >= low_ref[0:1, :]) & (past < MAXB * DB)
    cap = jnp.where(inside, FAR, -FAR)
    rows[...] = jnp.zeros_like(rows)
    for group in range(band_rows // GROUP):
        first = lax.axis_index("rows") * band_rows + group * GROUP - 3
        for i in range(GROUP + 6):
            y = first + i
            valid = ((y >= 0) & (y < height)).astype(jnp.float32)
            line = lines_ref[jnp.clip(y, 0, height - 1)].astype(jnp.float32)
            rows[i * TILES : (i + 1) * TILES, :] = line * valid
        tiles = [rows[pl.ds(t, 16, stride=TILES), :] for t in range(TILES)]
        left = jnp.concatenate(tiles[:LEFT_TILES], 1)
        right = jnp.concatenate(tiles[LEFT_TILES:], 1)
        shifted_left = [ahead(left, j, 1)[:, :tile_width] for j in range(7)]
        shifted_right = [ahead(right, j, 1)[:, :reach] for j in range(7)]
        left_total, _, left_scale = moments(shifted_left)
        _, right_mean, right_scale = moments(shifted_right)
        right_scale = jnp.transpose(right_scale)
        left_parts = [a for a in parts(-left_total) for _ in range(3)]
        right_side = jnp.concatenate(
            [v.astype(jnp.bfloat16) for v in shifted_right] + 3 * parts(right_mean), 0
        )
        right_side = jnp.transpose(right_side)
        left_all = jnp.concatenate([v.astype(jnp.bfloat16) for v in shifted_left] + left_parts, 0)
        scales = [jnp.broadcast_to(right_scale[:, y : y + 1], (reach, LANES)) for y in range(GROUP)]
        sides = []
        for y in range(GROUP):
            window = jnp.where((row >= y) & (row < y + 7), 1.0, 0.0).astype(jnp.bfloat16)
            only = jnp.where(row8 == y, 1.0, 0.0).astype(jnp.bfloat16)
            sides.append(left_all * jnp.concatenate([window] * 7 + [only] * 9, 0))
        best = [[None] * (tile_width // LANES) for _ in range(GROUP)]
        for y in range(0, GROUP, 2):
            for block in range(tile_width // LANES):
                at = slice(block * LANES, (block + 1) * LANES)
                reached = slice(block * LANES, block * LANES + span)
                products = jnp.dot(
                    right_side[reached],
                    jnp.concatenate([sides[y][:, at], sides[y + 1][:, at]], 1),
                    preferred_element_type=jnp.float32,
                )
                for half in range(2):
                    scaled = products[:, half * LANES : (half + 1) * LANES] * scales[y + half][reached]
                    best[y + half][block] = jnp.max(jnp.minimum(scaled, cap), axis=0, keepdims=True)
        best = jnp.concatenate([jnp.concatenate(b, 1) for b in best], 0)
        best = best * (left_scale * (1.0 / 49.0))
        out_ref[group * GROUP : (group + 1) * GROUP, :] = jnp.maximum(best, -2.0)


def score(lines, low, band_rows, tile_width):
    return pl.pallas_call(
        functools.partial(score_kernel, lines.shape[0]),
        out_shape=jax.ShapeDtypeStruct((band_rows, tile_width), jnp.float32),
        in_specs=[VMEM, VMEM],
        out_specs=VMEM,
        scratch_shapes=[pltpu.VMEM((16 * TILES, LANES), jnp.float32)],
        compiler_params=pltpu.CompilerParams(vmem_limit_bytes=16 * 2**20),
    )(lines, low)


def on_device(left_image, right_image, ranges):
    bands, tiles = lax.axis_size("rows"), lax.axis_size("cols")
    strip, width = left_image.shape
    pieces, low = pack(left_image, right_image, ranges, bands, tiles)
    lines = lax.all_to_all(pieces, ("rows", "cols"), split_axis=0, concat_axis=0, tiled=True)
    lines = lines.reshape(bands * tiles * strip, TILES, LANES)
    return score(lines, low, strip * tiles, width // tiles)


def solution(mesh):
    return jax.shard_map(
        on_device,
        mesh=mesh,
        in_specs=(P(("rows", "cols"), None), P(("rows", "cols"), None), P()),
        out_specs=P("rows", "cols"),
        check_vma=False,
    )
```

```python
import functools

import jax
import jax.numpy as jnp
from jax import lax
from jax.experimental import pallas as pl
from jax.experimental.pallas import tpu as pltpu
from jax.sharding import PartitionSpec as P

DB = 128
MAXB = 2
LANES = 128
LEFT_TILES = 3
RIGHT_TILES = 5
TILES = LEFT_TILES + RIGHT_TILES
LEAD = 3
GROUP = 8
STEP = 32
FAR = 3.0e37
VMEM = pl.BlockSpec(memory_space=pltpu.VMEM)
HBM = pl.BlockSpec(memory_space=pltpu.HBM)


def pack_kernel(bands, tiles, left_hbm, right_hbm, ranges_hbm, out_ref, low_ref, left_ref, right_ref, ranges_ref, left_rows, right_rows, sems):
    copies = [
        pltpu.make_async_copy(source, target, sems.at[i])
        for i, (source, target) in enumerate(
            [(ranges_hbm, ranges_ref), (left_hbm, left_ref), (right_hbm, right_ref)]
        )
    ]
    for copy in copies:
        copy.start()
    strip, width = left_ref.shape
    chunks = width // LANES
    per_tile = chunks // tiles
    lane = lax.broadcasted_iota(jnp.int32, (8, LANES), 1)
    left_rows[...] = jnp.zeros_like(left_rows)
    right_rows[...] = jnp.zeros_like(right_rows)
    for copy in copies:
        copy.wait()
    low = MAXB * DB - DB * ranges_ref[1, lax.axis_index("cols")]
    low_ref[...] = jnp.full(low_ref.shape, low, jnp.int32)

    def shifted(rows, first, by):
        here = pltpu.roll(rows[first : first + 8, :], by, 1)
        after = pltpu.roll(rows[first + 1 : first + 9, :], by, 1)
        return jnp.where(lane < by, here, after)

    for line in range(strip):
        for chunk in range(chunks):
            cut = slice(chunk * LANES, (chunk + 1) * LANES)
            at = slice(LEAD + chunk, LEAD + chunk + 1)
            left_rows[at, :] = left_ref[line : line + 1, cut].astype(jnp.float32)
            right_rows[at, :] = right_ref[line : line + 1, cut].astype(jnp.float32)
        for tile in range(tiles):
            first = LEAD + tile * per_tile
            left_part = shifted(left_rows, first - 1, 3)[:LEFT_TILES]
            right_part = shifted(right_rows, first - 3, 2 + ranges_ref[0, tile])[:RIGHT_TILES]
            piece = jnp.concatenate([left_part, right_part], 0).astype(jnp.bfloat16)
            for band in range(bands):
                out_ref[band * tiles + tile, line] = piece


def pack(left, right, ranges, bands, tiles):
    strip, width = left.shape
    rows = LEAD + width // LANES + 13
    return pl.pallas_call(
        functools.partial(pack_kernel, bands, tiles),
        out_shape=[
            jax.ShapeDtypeStruct((bands * tiles, strip, TILES, LANES), jnp.bfloat16),
            jax.ShapeDtypeStruct((8, LANES), jnp.int32),
        ],
        in_specs=[HBM, HBM, HBM],
        out_specs=[VMEM, VMEM],
        scratch_shapes=[
            pltpu.VMEM(left.shape, left.dtype),
            pltpu.VMEM(right.shape, right.dtype),
            pltpu.SMEM((2, tiles), jnp.int32),
            pltpu.VMEM((rows, LANES), jnp.float32),
            pltpu.VMEM((rows, LANES), jnp.float32),
            pltpu.SemaphoreType.DMA((3,)),
        ],
        compiler_params=pltpu.CompilerParams(vmem_limit_bytes=8 * 2**20),
    )(*[pltpu.with_memory_space_constraint(v, pltpu.HBM) for v in (left, right, ranges.T)])


def ahead(values, by, axis):
    if by == 0:
        return values
    return pltpu.roll(values, values.shape[axis] - by, axis)


def column_sum(values):
    two = values + ahead(values, 1, 0)
    four = two + ahead(two, 2, 0)
    return (four + ahead(two, 4, 0) + ahead(values, 6, 0))[:GROUP]


def moments(shifted):
    shifted = [v.astype(jnp.float32) for v in shifted]
    total = column_sum(sum(shifted[1:], shifted[0]))
    squares = [v * v for v in shifted]
    mean = total * (1.0 / 49.0)
    spread = column_sum(sum(squares[1:], squares[0])) * (1.0 / 49.0) - mean * mean
    return total, mean, lax.rsqrt(jnp.maximum(spread, 0.01))


def parts(values):
    high = values.astype(jnp.bfloat16)
    rest = values - high.astype(jnp.float32)
    middle = rest.astype(jnp.bfloat16)
    low = (rest - middle.astype(jnp.float32)).astype(jnp.bfloat16)
    return [high, middle, low]


def sum_of(values):
    return functools.reduce(lambda a, b: a + b, values)


def fold(values):
    return functools.reduce(jnp.maximum, [values[i : i + 8] for i in range(0, values.shape[0], 8)])


def spread_out(values, lane_group):
    out = []
    for tile in range(values.shape[1] // LANES):
        here = values[:, tile * LANES : (tile + 1) * LANES]
        turned = [here] + [pltpu.roll(here, STEP * k, 1) for k in range(1, LANES // STEP)]
        for g in range(LANES // STEP):
            out.append(sum_of([turned[k] * lane_group[(g + k) % (LANES // STEP)] for k in range(LANES // STEP)]))
    return out


def regroup(found):
    groups = LANES // STEP
    row = lax.broadcasted_iota(jnp.int32, (GROUP, LANES), 0)
    lane = lax.broadcasted_iota(jnp.int32, (GROUP, LANES), 1) // STEP
    halves = [found[:, h * LANES : (h + 1) * LANES] for h in range(2)]
    out = []
    for to in range(2):
        result = jnp.zeros((GROUP, LANES), jnp.float32)
        for half in range(2):
            for k in range(groups):
                turned = halves[half] if k == 0 else pltpu.roll(halves[half], STEP * k, 1)
                for up in sorted({(half - to) * groups - k, (half - to) * groups + (groups - k if k else 0)}):
                    chosen = (row // groups == half) & (row - (to * groups + lane) == up)
                    by = up % GROUP
                    result = jnp.where(chosen, pltpu.roll(turned, by, 0) if by else turned, result)
        out.append(result)
    return jnp.concatenate(out, 1)


def score_kernel(height, lines_ref, low_ref, out_ref, rows):
    band_rows, tile_width = out_ref.shape
    reach = tile_width + MAXB * DB
    span = MAXB * DB + STEP
    taken = GROUP + 6
    row16 = lax.broadcasted_iota(jnp.int32, (16, 2 * LANES), 0)
    owner16 = lax.broadcasted_iota(jnp.int32, (16, 2 * LANES), 1) // STEP
    window = jnp.where((row16 >= owner16) & (row16 < owner16 + 7), 1.0, 0.0).astype(jnp.bfloat16)
    only = jnp.where((row16 & 7) == owner16, 1.0, 0.0)[:GROUP]
    lane16 = lax.broadcasted_iota(jnp.int32, (16, LANES), 1) // STEP
    lane_group = [jnp.where(lane16 == p, 1.0, 0.0) for p in range(LANES // STEP)]
    lane_group8 = [v[:GROUP] for v in lane_group]
    lane_group = [v.astype(jnp.bfloat16) for v in lane_group]
    past = lax.broadcasted_iota(jnp.int32, (span, LANES), 0) - (
        lax.broadcasted_iota(jnp.int32, (span, LANES), 1) & (STEP - 1)
    )
    inside = (past >= low_ref[0:1, :]) & (past < MAXB * DB)
    cap = jnp.where(inside, FAR, -FAR)
    always = (DB + STEP, MAXB * DB)
    rows[...] = jnp.zeros_like(rows)
    for group in range(band_rows // GROUP):
        first = lax.axis_index("rows") * band_rows + group * GROUP - 3
        base = jnp.clip(first, 0, height - taken)
        if group:
            rows[...] = jnp.zeros_like(rows)
        found_lines = lines_ref[pl.ds(base, taken)].astype(jnp.float32)
        rows[pl.ds(base - first + 3, taken)] = found_lines
        flat = rows.reshape(rows.shape[0] * TILES, LANES)
        tiles = [flat[pl.ds(3 * TILES + t, 16, stride=TILES), :] for t in range(TILES)]
        left = jnp.concatenate(tiles[:LEFT_TILES], 1).astype(jnp.bfloat16)
        right = jnp.concatenate(tiles[LEFT_TILES:], 1).astype(jnp.bfloat16)
        shifted_right = [ahead(right, j, 1)[:, :reach] for j in range(7)]
        shifted_left = [ahead(left, j, 1)[:, :tile_width] for j in range(7)]
        blank = jnp.zeros((16, reach), jnp.bfloat16)
        near_side = jnp.transpose(jnp.concatenate(shifted_right + [blank], 0))
        _, right_mean, right_scale = moments(shifted_right)
        left_total, _, left_scale = moments(shifted_left)
        far_side = [p.astype(jnp.float32) for p in 3 * parts(right_mean) + parts(right_scale)]
        far_side = jnp.transpose(jnp.concatenate(far_side, 0).astype(jnp.bfloat16))
        right_side = jnp.concatenate([near_side, far_side], 1)
        depth = right_side.shape[1]
        near = [spread_out(v, lane_group) for v in shifted_left]
        far = [spread_out(p.astype(jnp.float32), lane_group8) for p in parts(-left_total)]
        source = lax.broadcasted_iota(jnp.int32, (depth, 2 * LANES), 0)
        owner = lax.broadcasted_iota(jnp.int32, (depth, 2 * LANES), 1) // STEP
        picked = (source >= 128 + 9 * GROUP) & ((source & 7) == owner)
        picks = jnp.where(picked, 1.0, 0.0).astype(jnp.bfloat16)
        scale = jnp.dot(right_side, picks, preferred_element_type=jnp.float32)
        none = jnp.zeros((16, 2 * LANES), jnp.bfloat16)
        none24 = jnp.zeros((3 * GROUP, 2 * LANES), jnp.float32)
        found = []
        for block in range(tile_width // STEP):
            left_side = [jnp.concatenate([v[block]] * 2, 1) * window for v in near] + [none]
            means = [jnp.concatenate([a[block]] * 2, 1) * only for a in far for _ in range(3)]
            left_side.append(jnp.concatenate(means + [none24], 0).astype(jnp.bfloat16))
            reached = slice(block * STEP, block * STEP + span)
            products = jnp.dot(
                right_side[reached], jnp.concatenate(left_side, 0), preferred_element_type=jnp.float32
            )
            halves = []
            for half in range(2):
                at = slice(half * LANES, (half + 1) * LANES)
                scaled = products[:, at] * scale[reached, at]
                kept = [
                    jnp.minimum(scaled[: always[0]], cap[: always[0]]),
                    scaled[always[0] : always[1]],
                    jnp.minimum(scaled[always[1] :], cap[always[1] :]),
                ]
                halves.append(jnp.max(functools.reduce(jnp.maximum, [fold(v) for v in kept]), axis=0, keepdims=True))
            found.append(jnp.concatenate(halves, 1))
        best = regroup(jnp.concatenate(found, 0)) * (left_scale * (1.0 / 49.0))
        out_ref[group * GROUP : (group + 1) * GROUP, :] = jnp.maximum(best, -2.0)


def score(lines, low, band_rows, tile_width):
    return pl.pallas_call(
        functools.partial(score_kernel, lines.shape[0]),
        out_shape=jax.ShapeDtypeStruct((band_rows, tile_width), jnp.float32),
        in_specs=[VMEM, VMEM],
        out_specs=VMEM,
        scratch_shapes=[pltpu.VMEM((GROUP + 12, TILES, LANES), jnp.float32)],
        compiler_params=pltpu.CompilerParams(vmem_limit_bytes=16 * 2**20),
    )(lines, low)


def on_device(left_image, right_image, ranges):
    bands, tiles = lax.axis_size("rows"), lax.axis_size("cols")
    strip, width = left_image.shape
    pieces, low = pack(left_image, right_image, ranges, bands, tiles)
    lines = lax.all_to_all(pieces, ("rows", "cols"), split_axis=0, concat_axis=0, tiled=True)
    lines = lines.reshape(bands * tiles * strip, TILES, LANES)
    return score(lines, low, strip * tiles, width // tiles)


def solution(mesh):
    return jax.shard_map(
        on_device,
        mesh=mesh,
        in_specs=(P(("rows", "cols"), None), P(("rows", "cols"), None), P()),
        out_specs=P("rows", "cols"),
        check_vma=False,
    )
```

```python
import functools

import jax
import jax.numpy as jnp
from jax import lax
from jax.experimental import pallas as pl
from jax.experimental.pallas import tpu as pltpu
from jax.sharding import PartitionSpec as P

DB = 128
MAXB = 2
LANES = 128
LEFT_TILES = 3
RIGHT_TILES = 5
TILES = LEFT_TILES + RIGHT_TILES
LEAD = 3
RIGHT_LEAD = 67
GROUP = 8
STEP = 32
FAR = 3.0e37
VMEM = pl.BlockSpec(memory_space=pltpu.VMEM)
HBM = pl.BlockSpec(memory_space=pltpu.HBM)


def cut(left_rows, right_rows, first):
    lane = lax.broadcasted_iota(jnp.int32, (8, LANES), 1)

    def shifted(rows, at, by):
        here = pltpu.roll(rows[pl.ds(at, 8), :], by, 1)
        after = pltpu.roll(rows[pl.ds(at + 1, 8), :], by, 1)
        return jnp.where(lane < by, here, after)

    left_part = shifted(left_rows, first - 1, 3)[:LEFT_TILES]
    right_part = shifted(right_rows, first - 3, RIGHT_LEAD)[:RIGHT_TILES]
    return jnp.concatenate([left_part, right_part], 0).astype(jnp.bfloat16)


def cut_all(tiles, left_ref, right_ref, left_rows, right_rows, put):
    strip, width = left_ref.shape
    chunks = width // LANES
    per_tile = chunks // tiles
    core = lax.rem(lax.axis_index("cols"), 2)
    for line in range(strip):
        for chunk in range(chunks):
            span = slice(chunk * LANES, (chunk + 1) * LANES)
            at = slice(LEAD + chunk, LEAD + chunk + 1)
            left_rows[at, :] = left_ref[line : line + 1, span].astype(jnp.float32)
            right_rows[at, :] = right_ref[line : line + 1, span].astype(jnp.float32)
        for pair in range(tiles // 2):
            put(pair, line, cut(left_rows, right_rows, LEAD + (2 * pair + core) * per_tile))


def own_kernel(tiles, left_hbm, right_hbm, ranges_hbm, out_ref, start_ref, low_ref, left_ref, right_ref, ranges_ref, left_rows, right_rows, sems):
    copies = [
        pltpu.make_async_copy(source, target, sems.at[i])
        for i, (source, target) in enumerate(
            [(ranges_hbm, ranges_ref), (left_hbm, left_ref), (right_hbm, right_ref)]
        )
    ]
    for copy in copies:
        copy.start()
    left_rows[...] = jnp.zeros_like(left_rows)
    right_rows[...] = jnp.zeros_like(right_rows)
    for copy in copies:
        copy.wait()
    tile = lax.axis_index("cols")
    start_ref[...] = jnp.full(start_ref.shape, ranges_ref[0, tile], jnp.int32)
    low_ref[...] = jnp.full(low_ref.shape, MAXB * DB - DB * ranges_ref[1, tile], jnp.int32)

    def put(pair, line, piece):
        out_ref[pair, line] = piece

    cut_all(tiles, left_ref, right_ref, left_rows, right_rows, put)


def cut_own(left, right, ranges, tiles):
    strip, width = left.shape
    rows = LEAD + width // LANES + 13
    return pl.pallas_call(
        functools.partial(own_kernel, tiles),
        out_shape=[
            jax.ShapeDtypeStruct((tiles // 2, strip, TILES, LANES), jnp.bfloat16),
            jax.ShapeDtypeStruct((8, LANES), jnp.int32),
            jax.ShapeDtypeStruct((8, LANES), jnp.int32),
        ],
        in_specs=[HBM, HBM, HBM],
        out_specs=[VMEM, VMEM, VMEM],
        scratch_shapes=[
            pltpu.VMEM(left.shape, left.dtype),
            pltpu.VMEM(right.shape, right.dtype),
            pltpu.SMEM((2, tiles), jnp.int32),
            pltpu.VMEM((rows, LANES), jnp.float32),
            pltpu.VMEM((rows, LANES), jnp.float32),
            pltpu.SemaphoreType.DMA((3,)),
        ],
        compiler_params=pltpu.CompilerParams(vmem_limit_bytes=8 * 2**20),
        cost_estimate=pl.CostEstimate(flops=10**6, bytes_accessed=2**16, transcendentals=0),
    )(*[pltpu.with_memory_space_constraint(v, pltpu.HBM) for v in (left, right, ranges.T)])


def pair_kernel(bands, tiles, own_ref, left_ref, right_ref, out_ref, left_rows, right_rows):
    left_rows[...] = jnp.zeros_like(left_rows)
    right_rows[...] = jnp.zeros_like(right_rows)
    core = lax.rem(lax.axis_index("cols"), 2)
    chips = bands * tiles // 2

    def put(pair, line, piece):
        mine = own_ref[pair, line]
        for band in range(bands):
            member = (band * (tiles // 2) + pair + 1) % chips
            out_ref[member, core, line] = mine
            out_ref[member, 1 - core, line] = piece

    cut_all(tiles, left_ref, right_ref, left_rows, right_rows, put)


def cut_pair(own, left, right, bands, tiles):
    strip, width = left.shape
    rows = LEAD + width // LANES + 13
    return pl.pallas_call(
        functools.partial(pair_kernel, bands, tiles),
        out_shape=jax.ShapeDtypeStruct((bands * tiles // 2, 2, strip, TILES, LANES), jnp.bfloat16),
        in_specs=[VMEM, VMEM, VMEM],
        out_specs=VMEM,
        scratch_shapes=[pltpu.VMEM((rows, LANES), jnp.float32), pltpu.VMEM((rows, LANES), jnp.float32)],
        compiler_params=pltpu.CompilerParams(vmem_limit_bytes=8 * 2**20),
    )(own, left, right)


def ahead(values, by, axis):
    if by == 0:
        return values
    return pltpu.roll(values, values.shape[axis] - by, axis)


def column_sum(values):
    two = values + ahead(values, 1, 0)
    four = two + ahead(two, 2, 0)
    return (four + ahead(two, 4, 0) + ahead(values, 6, 0))[:GROUP]


def moments(shifted):
    shifted = [v.astype(jnp.float32) for v in shifted]
    total = column_sum(sum(shifted[1:], shifted[0]))
    squares = [v * v for v in shifted]
    mean = total * (1.0 / 49.0)
    spread = column_sum(sum(squares[1:], squares[0])) * (1.0 / 49.0) - mean * mean
    return total, mean, lax.rsqrt(jnp.maximum(spread, 0.01))


def parts(values):
    high = values.astype(jnp.bfloat16)
    rest = values - high.astype(jnp.float32)
    middle = rest.astype(jnp.bfloat16)
    low = (rest - middle.astype(jnp.float32)).astype(jnp.bfloat16)
    return [high, middle, low]


def sum_of(values):
    return functools.reduce(lambda a, b: a + b, values)


def fold(values):
    return functools.reduce(jnp.maximum, [values[i : i + 8] for i in range(0, values.shape[0], 8)])


def spread_out(values, lane_group):
    out = []
    for tile in range(values.shape[1] // LANES):
        here = values[:, tile * LANES : (tile + 1) * LANES]
        turned = [here] + [pltpu.roll(here, STEP * k, 1) for k in range(1, LANES // STEP)]
        for g in range(LANES // STEP):
            out.append(sum_of([turned[k] * lane_group[(g + k) % (LANES // STEP)] for k in range(LANES // STEP)]))
    return out


def regroup(found):
    groups = LANES // STEP
    row = lax.broadcasted_iota(jnp.int32, (GROUP, LANES), 0)
    lane = lax.broadcasted_iota(jnp.int32, (GROUP, LANES), 1) // STEP
    halves = [found[:, h * LANES : (h + 1) * LANES] for h in range(2)]
    out = []
    for to in range(2):
        result = jnp.zeros((GROUP, LANES), jnp.float32)
        for half in range(2):
            for k in range(groups):
                turned = halves[half] if k == 0 else pltpu.roll(halves[half], STEP * k, 1)
                for up in sorted({(half - to) * groups - k, (half - to) * groups + (groups - k if k else 0)}):
                    chosen = (row // groups == half) & (row - (to * groups + lane) == up)
                    by = up % GROUP
                    result = jnp.where(chosen, pltpu.roll(turned, by, 0) if by else turned, result)
        out.append(result)
    return jnp.concatenate(out, 1)


def score_kernel(height, strip, lines_ref, start_ref, low_ref, out_ref, rows):
    band_rows, tile_width = out_ref.shape
    reach = tile_width + MAXB * DB
    span = MAXB * DB + STEP
    taken = GROUP + 6
    row16 = lax.broadcasted_iota(jnp.int32, (16, 2 * LANES), 0)
    owner16 = lax.broadcasted_iota(jnp.int32, (16, 2 * LANES), 1) // STEP
    window = jnp.where((row16 >= owner16) & (row16 < owner16 + 7), 1.0, 0.0).astype(jnp.bfloat16)
    only = jnp.where((row16 & 7) == owner16, 1.0, 0.0)[:GROUP]
    lane16 = lax.broadcasted_iota(jnp.int32, (16, LANES), 1) // STEP
    lane_group = [jnp.where(lane16 == p, 1.0, 0.0) for p in range(LANES // STEP)]
    lane_group8 = [v[:GROUP] for v in lane_group]
    lane_group = [v.astype(jnp.bfloat16) for v in lane_group]
    past = lax.broadcasted_iota(jnp.int32, (span, LANES), 0) - (
        lax.broadcasted_iota(jnp.int32, (span, LANES), 1) & (STEP - 1)
    )
    inside = (past >= low_ref[0:1, :]) & (past < MAXB * DB)
    cap = jnp.where(inside, FAR, -FAR)
    always = (DB + STEP, MAXB * DB)
    rows[...] = jnp.zeros_like(rows)
    start = start_ref[0, 0]
    lane = lax.broadcasted_iota(jnp.int32, (16, LANES), 1)

    def moved(pieces, by):
        turned = [pltpu.roll(v, by, 1) for v in pieces]
        ahead_by = [jnp.where(lane < by, a, b) for a, b in zip(turned, turned[1:])]
        return jnp.concatenate(ahead_by, 1).astype(jnp.bfloat16)

    for group in range(band_rows // GROUP):
        first = lax.axis_index("rows") * band_rows + group * GROUP - 3
        base = jnp.clip(first, 0, height - taken)
        if group:
            rows[...] = jnp.zeros_like(rows)
        into = base - first + 3
        for count, at in ((taken - 2, 0), (2, taken - 2)):
            part = lines_ref[pl.ds(lax.rem(base + at + 2 * strip, height), count)].astype(jnp.float32)
            rows[pl.ds(into + at, count)] = part
        flat = rows.reshape(rows.shape[0] * TILES, LANES)
        tiles = [flat[pl.ds(3 * TILES + t, 16, stride=TILES), :] for t in range(TILES)]
        left = jnp.concatenate(tiles[:LEFT_TILES], 1).astype(jnp.bfloat16)
        shifted_right = [moved(tiles[LEFT_TILES:], RIGHT_LEAD - 4 - j + start) for j in range(7)]
        shifted_left = [ahead(left, j, 1)[:, :tile_width] for j in range(7)]
        blank = jnp.zeros((16, reach), jnp.bfloat16)
        near_side = jnp.transpose(jnp.concatenate(shifted_right + [blank], 0))
        _, right_mean, right_scale = moments(shifted_right)
        left_total, _, left_scale = moments(shifted_left)
        far_side = [p.astype(jnp.float32) for p in 3 * parts(right_mean) + parts(right_scale)]
        far_side = jnp.transpose(jnp.concatenate(far_side, 0).astype(jnp.bfloat16))
        right_side = jnp.concatenate([near_side, far_side], 1)
        depth = right_side.shape[1]
        near = [spread_out(v, lane_group) for v in shifted_left]
        far = [spread_out(p.astype(jnp.float32), lane_group8) for p in parts(-left_total)]
        source = lax.broadcasted_iota(jnp.int32, (depth, 2 * LANES), 0)
        owner = lax.broadcasted_iota(jnp.int32, (depth, 2 * LANES), 1) // STEP
        picked = (source >= 128 + 9 * GROUP) & ((source & 7) == owner)
        picks = jnp.where(picked, 1.0, 0.0).astype(jnp.bfloat16)
        scale = jnp.dot(right_side, picks, preferred_element_type=jnp.float32)
        none = jnp.zeros((16, 2 * LANES), jnp.bfloat16)
        none24 = jnp.zeros((3 * GROUP, 2 * LANES), jnp.float32)
        found = []
        for block in range(tile_width // STEP):
            left_side = [jnp.concatenate([v[block]] * 2, 1) * window for v in near] + [none]
            means = [jnp.concatenate([a[block]] * 2, 1) * only for a in far for _ in range(3)]
            left_side.append(jnp.concatenate(means + [none24], 0).astype(jnp.bfloat16))
            reached = slice(block * STEP, block * STEP + span)
            products = jnp.dot(
                right_side[reached], jnp.concatenate(left_side, 0), preferred_element_type=jnp.float32
            )
            halves = []
            for half in range(2):
                at = slice(half * LANES, (half + 1) * LANES)
                scaled = products[:, at] * scale[reached, at]
                kept = [
                    jnp.minimum(scaled[: always[0]], cap[: always[0]]),
                    scaled[always[0] : always[1]],
                    jnp.minimum(scaled[always[1] :], cap[always[1] :]),
                ]
                halves.append(jnp.max(functools.reduce(jnp.maximum, [fold(v) for v in kept]), axis=0, keepdims=True))
            found.append(jnp.concatenate(halves, 1))
        best = regroup(jnp.concatenate(found, 0)) * (left_scale * (1.0 / 49.0))
        out_ref[group * GROUP : (group + 1) * GROUP, :] = jnp.maximum(best, -2.0)


def score(lines, start, low, band_rows, tile_width):
    return pl.pallas_call(
        functools.partial(score_kernel, lines.shape[0], band_rows // lax.axis_size("cols")),
        out_shape=jax.ShapeDtypeStruct((band_rows, tile_width), jnp.float32),
        in_specs=[VMEM, VMEM, VMEM],
        out_specs=VMEM,
        scratch_shapes=[pltpu.VMEM((GROUP + 12, TILES, LANES), jnp.float32)],
        compiler_params=pltpu.CompilerParams(vmem_limit_bytes=16 * 2**20),
    )(lines, start, low)


def on_device(left_image, right_image, ranges):
    bands, tiles = lax.axis_size("rows"), lax.axis_size("cols")
    strip, width = left_image.shape
    chips = bands * tiles // 2
    swap = [(i, i ^ 1) for i in range(tiles)]
    left_other = lax.ppermute(left_image, "cols", swap)
    right_other = lax.ppermute(right_image, "cols", swap)
    own, start, low = cut_own(left_image, right_image, ranges, tiles)
    pieces = cut_pair(own, left_other, right_other, bands, tiles)
    order = [chips - 1] + list(range(chips - 1))
    groups = [[2 * chip + core for chip in order] for core in range(2)]
    lines = lax.all_to_all(
        pieces, ("rows", "cols"), split_axis=0, concat_axis=0, tiled=True, axis_index_groups=groups
    )
    lines = lines.reshape(bands * tiles * strip, TILES, LANES)
    return score(lines, start, low, strip * tiles, width // tiles)


def solution(mesh):
    return jax.shard_map(
        on_device,
        mesh=mesh,
        in_specs=(P(("rows", "cols"), None), P(("rows", "cols"), None), P()),
        out_specs=P("rows", "cols"),
        check_vma=False,
    )
```

```python
import functools

import jax
import jax.numpy as jnp
from jax import lax
from jax.experimental import pallas as pl
from jax.experimental.pallas import tpu as pltpu
from jax.sharding import PartitionSpec as P

DB = 128
MAXB = 2
LANES = 128
LEFT_TILES = 3
RIGHT_TILES = 5
TILES = LEFT_TILES + RIGHT_TILES
LEAD = 3
RIGHT_LEAD = 67
AHEAD = 2
GROUP = 8
STEP = 32
FAR = 3.0e37
VMEM = pl.BlockSpec(memory_space=pltpu.VMEM)
HBM = pl.BlockSpec(memory_space=pltpu.HBM)


def side_of(tile):
    return lax.rem(tile + jnp.where(tile < 2, 1, 0), 2)


def cut(left_rows, right_rows, first):
    lane = lax.broadcasted_iota(jnp.int32, (8, LANES), 1)

    def shifted(rows, at, by):
        here = pltpu.roll(rows[pl.ds(at, 8), :], by, 1)
        after = pltpu.roll(rows[pl.ds(at + 1, 8), :], by, 1)
        return jnp.where(lane < by, here, after)

    left_part = shifted(left_rows, first - 1, 3)[:LEFT_TILES]
    right_part = shifted(right_rows, first - 3, RIGHT_LEAD)[:RIGHT_TILES]
    return jnp.concatenate([left_part, right_part], 0).astype(jnp.bfloat16)


def cut_all(tiles, left_ref, right_ref, left_rows, right_rows, put):
    strip, width = left_ref.shape
    chunks = width // LANES
    per_tile = chunks // tiles
    side = side_of(lax.axis_index("cols"))
    for line in range(strip):
        for chunk in range(chunks):
            span = slice(chunk * LANES, (chunk + 1) * LANES)
            at = slice(LEAD + chunk, LEAD + chunk + 1)
            left_rows[at, :] = left_ref[line : line + 1, span].astype(jnp.float32)
            right_rows[at, :] = right_ref[line : line + 1, span].astype(jnp.float32)
        for pair in range(tiles // 2):
            tile = 2 * pair + (side if pair else 1 - side)
            put(pair, line, cut(left_rows, right_rows, LEAD + tile * per_tile))


def own_kernel(tiles, left_hbm, right_hbm, ranges_hbm, out_ref, start_ref, low_ref, left_ref, right_ref, ranges_ref, left_rows, right_rows, sems):
    copies = [
        pltpu.make_async_copy(source, target, sems.at[i])
        for i, (source, target) in enumerate(
            [(ranges_hbm, ranges_ref), (left_hbm, left_ref), (right_hbm, right_ref)]
        )
    ]
    for copy in copies:
        copy.start()
    left_rows[...] = jnp.zeros_like(left_rows)
    right_rows[...] = jnp.zeros_like(right_rows)
    for copy in copies:
        copy.wait()
    tile = lax.axis_index("cols")
    start_ref[...] = jnp.full(start_ref.shape, ranges_ref[0, tile], jnp.int32)
    low_ref[...] = jnp.full(low_ref.shape, MAXB * DB - DB * ranges_ref[1, tile], jnp.int32)

    def put(pair, line, piece):
        out_ref[pair, line] = piece

    cut_all(tiles, left_ref, right_ref, left_rows, right_rows, put)


def cut_own(left, right, ranges, tiles):
    strip, width = left.shape
    rows = LEAD + width // LANES + 13
    return pl.pallas_call(
        functools.partial(own_kernel, tiles),
        out_shape=[
            jax.ShapeDtypeStruct((tiles // 2, strip, TILES, LANES), jnp.bfloat16),
            jax.ShapeDtypeStruct((8, LANES), jnp.int32),
            jax.ShapeDtypeStruct((8, LANES), jnp.int32),
        ],
        in_specs=[HBM, HBM, HBM],
        out_specs=[VMEM, VMEM, VMEM],
        scratch_shapes=[
            pltpu.VMEM(left.shape, left.dtype),
            pltpu.VMEM(right.shape, right.dtype),
            pltpu.SMEM((2, tiles), jnp.int32),
            pltpu.VMEM((rows, LANES), jnp.float32),
            pltpu.VMEM((rows, LANES), jnp.float32),
            pltpu.SemaphoreType.DMA((3,)),
        ],
        compiler_params=pltpu.CompilerParams(vmem_limit_bytes=8 * 2**20),
        cost_estimate=pl.CostEstimate(flops=10**6, bytes_accessed=2**16, transcendentals=0),
    )(*[pltpu.with_memory_space_constraint(v, pltpu.HBM) for v in (left, right, ranges.T)])


def pair_kernel(bands, tiles, own_ref, left_ref, right_ref, out_ref, left_rows, right_rows):
    left_rows[...] = jnp.zeros_like(left_rows)
    right_rows[...] = jnp.zeros_like(right_rows)
    core = lax.rem(lax.axis_index("cols"), 2)
    chips = bands * tiles // 2

    def put(pair, line, piece):
        mine = own_ref[pair, line]
        for band in range(bands):
            member = (band * (tiles // 2) + pair + AHEAD) % chips
            out_ref[member, core, line] = mine
            out_ref[member, 1 - core, line] = piece

    cut_all(tiles, left_ref, right_ref, left_rows, right_rows, put)


def cut_pair(own, left, right, bands, tiles):
    strip, width = left.shape
    rows = LEAD + width // LANES + 13
    return pl.pallas_call(
        functools.partial(pair_kernel, bands, tiles),
        out_shape=jax.ShapeDtypeStruct((bands * tiles // 2, 2, strip, TILES, LANES), jnp.bfloat16),
        in_specs=[VMEM, VMEM, VMEM],
        out_specs=VMEM,
        scratch_shapes=[pltpu.VMEM((rows, LANES), jnp.float32), pltpu.VMEM((rows, LANES), jnp.float32)],
        compiler_params=pltpu.CompilerParams(vmem_limit_bytes=8 * 2**20),
    )(own, left, right)


def ahead(values, by, axis):
    if by == 0:
        return values
    return pltpu.roll(values, values.shape[axis] - by, axis)


def column_sum(values):
    two = values + ahead(values, 1, 0)
    four = two + ahead(two, 2, 0)
    return (four + ahead(two, 4, 0) + ahead(values, 6, 0))[:GROUP]


def moments(shifted):
    shifted = [v.astype(jnp.float32) for v in shifted]
    total = column_sum(sum(shifted[1:], shifted[0]))
    squares = [v * v for v in shifted]
    mean = total * (1.0 / 49.0)
    spread = column_sum(sum(squares[1:], squares[0])) * (1.0 / 49.0) - mean * mean
    return total, mean, lax.rsqrt(jnp.maximum(spread, 0.01))


def parts(values):
    high = values.astype(jnp.bfloat16)
    rest = values - high.astype(jnp.float32)
    middle = rest.astype(jnp.bfloat16)
    low = (rest - middle.astype(jnp.float32)).astype(jnp.bfloat16)
    return [high, middle, low]


def sum_of(values):
    return functools.reduce(lambda a, b: a + b, values)


def fold(values):
    return functools.reduce(jnp.maximum, [values[i : i + 8] for i in range(0, values.shape[0], 8)])


def spread_out(values, lane_group):
    out = []
    for tile in range(values.shape[1] // LANES):
        here = values[:, tile * LANES : (tile + 1) * LANES]
        turned = [here] + [pltpu.roll(here, STEP * k, 1) for k in range(1, LANES // STEP)]
        for g in range(LANES // STEP):
            out.append(sum_of([turned[k] * lane_group[(g + k) % (LANES // STEP)] for k in range(LANES // STEP)]))
    return out


def regroup(found):
    groups = LANES // STEP
    row = lax.broadcasted_iota(jnp.int32, (GROUP, LANES), 0)
    lane = lax.broadcasted_iota(jnp.int32, (GROUP, LANES), 1) // STEP
    halves = [found[:, h * LANES : (h + 1) * LANES] for h in range(2)]
    out = []
    for to in range(2):
        result = jnp.zeros((GROUP, LANES), jnp.float32)
        for half in range(2):
            for k in range(groups):
                turned = halves[half] if k == 0 else pltpu.roll(halves[half], STEP * k, 1)
                for up in sorted({(half - to) * groups - k, (half - to) * groups + (groups - k if k else 0)}):
                    chosen = (row // groups == half) & (row - (to * groups + lane) == up)
                    by = up % GROUP
                    result = jnp.where(chosen, pltpu.roll(turned, by, 0) if by else turned, result)
        out.append(result)
    return jnp.concatenate(out, 1)


def score_kernel(height, strip, lines_ref, start_ref, low_ref, out_ref, rows):
    band_rows, tile_width = out_ref.shape
    reach = tile_width + MAXB * DB
    span = MAXB * DB + STEP
    taken = GROUP + 6
    row16 = lax.broadcasted_iota(jnp.int32, (16, 2 * LANES), 0)
    owner16 = lax.broadcasted_iota(jnp.int32, (16, 2 * LANES), 1) // STEP
    window = jnp.where((row16 >= owner16) & (row16 < owner16 + 7), 1.0, 0.0).astype(jnp.bfloat16)
    only = jnp.where((row16 & 7) == owner16, 1.0, 0.0)[:GROUP]
    lane16 = lax.broadcasted_iota(jnp.int32, (16, LANES), 1) // STEP
    lane_group = [jnp.where(lane16 == p, 1.0, 0.0) for p in range(LANES // STEP)]
    lane_group8 = [v[:GROUP] for v in lane_group]
    lane_group = [v.astype(jnp.bfloat16) for v in lane_group]
    past = lax.broadcasted_iota(jnp.int32, (span, LANES), 0) - (
        lax.broadcasted_iota(jnp.int32, (span, LANES), 1) & (STEP - 1)
    )
    inside = (past >= low_ref[0:1, :]) & (past < MAXB * DB)
    cap = jnp.where(inside, FAR, -FAR)
    always = (DB + STEP, MAXB * DB)
    rows[...] = jnp.zeros_like(rows)
    start = start_ref[0, 0]
    lane = lax.broadcasted_iota(jnp.int32, (16, LANES), 1)

    def moved(pieces, by):
        turned = [pltpu.roll(v, by, 1) for v in pieces]
        ahead_by = [jnp.where(lane < by, a, b) for a, b in zip(turned, turned[1:])]
        return jnp.concatenate(ahead_by, 1).astype(jnp.bfloat16)

    for group in range(band_rows // GROUP):
        first = lax.axis_index("rows") * band_rows + group * GROUP - 3
        base = jnp.clip(first, 0, height - taken)
        if group:
            rows[...] = jnp.zeros_like(rows)
        into = base - first + 3
        last = 2 * AHEAD * strip
        for count, at in ((taken - last, 0), (last, taken - last)):
            part = lines_ref[pl.ds(lax.rem(base + at + last, height), count)].astype(jnp.float32)
            rows[pl.ds(into + at, count)] = part
        flat = rows.reshape(rows.shape[0] * TILES, LANES)
        tiles = [flat[pl.ds(3 * TILES + t, 16, stride=TILES), :] for t in range(TILES)]
        left = jnp.concatenate(tiles[:LEFT_TILES], 1).astype(jnp.bfloat16)
        shifted_right = [moved(tiles[LEFT_TILES:], RIGHT_LEAD - 4 - j + start) for j in range(7)]
        shifted_left = [ahead(left, j, 1)[:, :tile_width] for j in range(7)]
        blank = jnp.zeros((16, reach), jnp.bfloat16)
        near_side = jnp.transpose(jnp.concatenate(shifted_right + [blank], 0))
        _, right_mean, right_scale = moments(shifted_right)
        left_total, _, left_scale = moments(shifted_left)
        far_side = [p.astype(jnp.float32) for p in 3 * parts(right_mean) + parts(right_scale)]
        far_side = jnp.transpose(jnp.concatenate(far_side, 0).astype(jnp.bfloat16))
        right_side = jnp.concatenate([near_side, far_side], 1)
        depth = right_side.shape[1]
        near = [spread_out(v, lane_group) for v in shifted_left]
        far = [spread_out(p.astype(jnp.float32), lane_group8) for p in parts(-left_total)]
        source = lax.broadcasted_iota(jnp.int32, (depth, 2 * LANES), 0)
        owner = lax.broadcasted_iota(jnp.int32, (depth, 2 * LANES), 1) // STEP
        picked = (source >= 128 + 9 * GROUP) & ((source & 7) == owner)
        picks = jnp.where(picked, 1.0, 0.0).astype(jnp.bfloat16)
        scale = jnp.dot(right_side, picks, preferred_element_type=jnp.float32)
        none = jnp.zeros((16, 2 * LANES), jnp.bfloat16)
        none24 = jnp.zeros((3 * GROUP, 2 * LANES), jnp.float32)
        found = []
        for block in range(tile_width // STEP):
            left_side = [jnp.concatenate([v[block]] * 2, 1) * window for v in near] + [none]
            means = [jnp.concatenate([a[block]] * 2, 1) * only for a in far for _ in range(3)]
            left_side.append(jnp.concatenate(means + [none24], 0).astype(jnp.bfloat16))
            reached = slice(block * STEP, block * STEP + span)
            products = jnp.dot(
                right_side[reached], jnp.concatenate(left_side, 0), preferred_element_type=jnp.float32
            )
            halves = []
            for half in range(2):
                at = slice(half * LANES, (half + 1) * LANES)
                scaled = products[:, at] * scale[reached, at]
                kept = [
                    jnp.minimum(scaled[: always[0]], cap[: always[0]]),
                    scaled[always[0] : always[1]],
                    jnp.minimum(scaled[always[1] :], cap[always[1] :]),
                ]
                halves.append(jnp.max(functools.reduce(jnp.maximum, [fold(v) for v in kept]), axis=0, keepdims=True))
            found.append(jnp.concatenate(halves, 1))
        best = regroup(jnp.concatenate(found, 0)) * (left_scale * (1.0 / 49.0))
        out_ref[group * GROUP : (group + 1) * GROUP, :] = jnp.maximum(best, -2.0)


def score(lines, start, low, band_rows, tile_width):
    return pl.pallas_call(
        functools.partial(score_kernel, lines.shape[0], band_rows // lax.axis_size("cols")),
        out_shape=jax.ShapeDtypeStruct((band_rows, tile_width), jnp.float32),
        in_specs=[VMEM, VMEM, VMEM],
        out_specs=VMEM,
        scratch_shapes=[pltpu.VMEM((GROUP + 12, TILES, LANES), jnp.float32)],
        compiler_params=pltpu.CompilerParams(vmem_limit_bytes=16 * 2**20),
    )(lines, start, low)


def on_device(left_image, right_image, ranges):
    bands, tiles = lax.axis_size("rows"), lax.axis_size("cols")
    strip, width = left_image.shape
    chips = bands * tiles // 2
    swap = [(i, i ^ 1) for i in range(tiles)]
    left_other = lax.ppermute(left_image, "cols", swap)
    right_other = lax.ppermute(right_image, "cols", swap)
    own, start, low = cut_own(left_image, right_image, ranges, tiles)
    pieces = cut_pair(own, left_other, right_other, bands, tiles)
    order = [(place - AHEAD) % chips for place in range(chips)]
    groups = [[2 * chip + (side if chip % (tiles // 2) else 1 - side) for chip in order] for side in range(2)]
    lines = lax.all_to_all(
        pieces, ("rows", "cols"), split_axis=0, concat_axis=0, tiled=True, axis_index_groups=groups
    )
    lines = lines.reshape(bands * tiles * strip, TILES, LANES)
    return score(lines, start, low, strip * tiles, width // tiles)


def solution(mesh):
    return jax.shard_map(
        on_device,
        mesh=mesh,
        in_specs=(P(("rows", "cols"), None), P(("rows", "cols"), None), P()),
        out_specs=P("rows", "cols"),
        check_vma=False,
    )
```

```python
import functools

import jax
import jax.numpy as jnp
from jax import lax
from jax.experimental import pallas as pl
from jax.experimental.pallas import tpu as pltpu
from jax.sharding import PartitionSpec as P

DB = 128
MAXB = 2
LANES = 128
LEFT_TILES = 3
RIGHT_TILES = 5
TILES = LEFT_TILES + RIGHT_TILES
LEAD = 3
RIGHT_LEAD = 67
GROUP = 8
STEP = 32
FAR = 3.0e37
VMEM = pl.BlockSpec(memory_space=pltpu.VMEM)
HBM = pl.BlockSpec(memory_space=pltpu.HBM)


def chip_order(bands, pairs):
    chips = bands * pairs
    leader = chips - 2
    away = {chip: bin(chip // pairs).count("1") + chip % pairs for chip in range(1, chips)}
    far_first = sorted(away, key=lambda chip: (-away[chip], chip != leader, chip))
    steps = list(range(2, chips, 2)) + list(range(1, chips, 2))
    first = -steps[far_first.index(leader)] % chips
    order = [0] * chips
    for step, chip in zip(steps, far_first):
        order[(first + step) % chips] = chip
    return order


def side_of(tile):
    return lax.rem(tile + jnp.where(tile < 2, 1, 0), 2)


def cut(left_rows, right_rows, first):
    lane = lax.broadcasted_iota(jnp.int32, (8, LANES), 1)

    def shifted(rows, at, by):
        here = pltpu.roll(rows[pl.ds(at, 8), :], by, 1)
        after = pltpu.roll(rows[pl.ds(at + 1, 8), :], by, 1)
        return jnp.where(lane < by, here, after)

    left_part = shifted(left_rows, first - 1, 3)[:LEFT_TILES]
    right_part = shifted(right_rows, first - 3, RIGHT_LEAD)[:RIGHT_TILES]
    return jnp.concatenate([left_part, right_part], 0).astype(jnp.bfloat16)


def cut_all(tiles, left_ref, right_ref, left_rows, right_rows, put):
    strip, width = left_ref.shape
    chunks = width // LANES
    per_tile = chunks // tiles
    side = side_of(lax.axis_index("cols"))
    for line in range(strip):
        for chunk in range(chunks):
            span = slice(chunk * LANES, (chunk + 1) * LANES)
            at = slice(LEAD + chunk, LEAD + chunk + 1)
            left_rows[at, :] = left_ref[line : line + 1, span].astype(jnp.float32)
            right_rows[at, :] = right_ref[line : line + 1, span].astype(jnp.float32)
        for pair in range(tiles // 2):
            tile = 2 * pair + (side if pair else 1 - side)
            put(pair, line, cut(left_rows, right_rows, LEAD + tile * per_tile))


def own_kernel(tiles, left_hbm, right_hbm, ranges_hbm, out_ref, start_ref, low_ref, left_ref, right_ref, ranges_ref, left_rows, right_rows, sems):
    copies = [
        pltpu.make_async_copy(source, target, sems.at[i])
        for i, (source, target) in enumerate(
            [(ranges_hbm, ranges_ref), (left_hbm, left_ref), (right_hbm, right_ref)]
        )
    ]
    for copy in copies:
        copy.start()
    left_rows[...] = jnp.zeros_like(left_rows)
    right_rows[...] = jnp.zeros_like(right_rows)
    for copy in copies:
        copy.wait()
    tile = lax.axis_index("cols")
    start_ref[...] = jnp.full(start_ref.shape, ranges_ref[0, tile], jnp.int32)
    low_ref[...] = jnp.full(low_ref.shape, MAXB * DB - DB * ranges_ref[1, tile], jnp.int32)

    def put(pair, line, piece):
        out_ref[pair, line] = piece

    cut_all(tiles, left_ref, right_ref, left_rows, right_rows, put)


def cut_own(left, right, ranges, tiles):
    strip, width = left.shape
    rows = LEAD + width // LANES + 13
    return pl.pallas_call(
        functools.partial(own_kernel, tiles),
        out_shape=[
            jax.ShapeDtypeStruct((tiles // 2, strip, TILES, LANES), jnp.bfloat16),
            jax.ShapeDtypeStruct((8, LANES), jnp.int32),
            jax.ShapeDtypeStruct((8, LANES), jnp.int32),
        ],
        in_specs=[HBM, HBM, HBM],
        out_specs=[VMEM, VMEM, VMEM],
        scratch_shapes=[
            pltpu.VMEM(left.shape, left.dtype),
            pltpu.VMEM(right.shape, right.dtype),
            pltpu.SMEM((2, tiles), jnp.int32),
            pltpu.VMEM((rows, LANES), jnp.float32),
            pltpu.VMEM((rows, LANES), jnp.float32),
            pltpu.SemaphoreType.DMA((3,)),
        ],
        compiler_params=pltpu.CompilerParams(vmem_limit_bytes=8 * 2**20),
        cost_estimate=pl.CostEstimate(flops=10**6, bytes_accessed=2**16, transcendentals=0),
    )(*[pltpu.with_memory_space_constraint(v, pltpu.HBM) for v in (left, right, ranges.T)])


def pair_kernel(bands, tiles, own_ref, left_ref, right_ref, out_ref, left_rows, right_rows):
    left_rows[...] = jnp.zeros_like(left_rows)
    right_rows[...] = jnp.zeros_like(right_rows)
    core = lax.rem(lax.axis_index("cols"), 2)
    order = chip_order(bands, tiles // 2)

    def put(pair, line, piece):
        mine = own_ref[pair, line]
        for band in range(bands):
            member = order.index(band * (tiles // 2) + pair)
            out_ref[member, core, line] = mine
            out_ref[member, 1 - core, line] = piece

    cut_all(tiles, left_ref, right_ref, left_rows, right_rows, put)


def cut_pair(own, left, right, bands, tiles):
    strip, width = left.shape
    rows = LEAD + width // LANES + 13
    return pl.pallas_call(
        functools.partial(pair_kernel, bands, tiles),
        out_shape=jax.ShapeDtypeStruct((bands * tiles // 2, 2, strip, TILES, LANES), jnp.bfloat16),
        in_specs=[VMEM, VMEM, VMEM],
        out_specs=VMEM,
        scratch_shapes=[pltpu.VMEM((rows, LANES), jnp.float32), pltpu.VMEM((rows, LANES), jnp.float32)],
        compiler_params=pltpu.CompilerParams(vmem_limit_bytes=8 * 2**20),
    )(own, left, right)


def ahead(values, by, axis):
    if by == 0:
        return values
    return pltpu.roll(values, values.shape[axis] - by, axis)


def column_sum(values):
    two = values + ahead(values, 1, 0)
    four = two + ahead(two, 2, 0)
    return (four + ahead(two, 4, 0) + ahead(values, 6, 0))[:GROUP]


def moments(shifted):
    shifted = [v.astype(jnp.float32) for v in shifted]
    total = column_sum(sum(shifted[1:], shifted[0]))
    squares = [v * v for v in shifted]
    mean = total * (1.0 / 49.0)
    spread = column_sum(sum(squares[1:], squares[0])) * (1.0 / 49.0) - mean * mean
    return total, mean, lax.rsqrt(jnp.maximum(spread, 0.01))


def parts(values):
    high = values.astype(jnp.bfloat16)
    rest = values - high.astype(jnp.float32)
    middle = rest.astype(jnp.bfloat16)
    low = (rest - middle.astype(jnp.float32)).astype(jnp.bfloat16)
    return [high, middle, low]


def sum_of(values):
    return functools.reduce(lambda a, b: a + b, values)


def fold(values):
    return functools.reduce(jnp.maximum, [values[i : i + 8] for i in range(0, values.shape[0], 8)])


def spread_out(values, lane_group):
    out = []
    for tile in range(values.shape[1] // LANES):
        here = values[:, tile * LANES : (tile + 1) * LANES]
        turned = [here] + [pltpu.roll(here, STEP * k, 1) for k in range(1, LANES // STEP)]
        for g in range(LANES // STEP):
            out.append(sum_of([turned[k] * lane_group[(g + k) % (LANES // STEP)] for k in range(LANES // STEP)]))
    return out


def regroup(found):
    groups = LANES // STEP
    row = lax.broadcasted_iota(jnp.int32, (GROUP, LANES), 0)
    lane = lax.broadcasted_iota(jnp.int32, (GROUP, LANES), 1) // STEP
    halves = [found[:, h * LANES : (h + 1) * LANES] for h in range(2)]
    out = []
    for to in range(2):
        result = jnp.zeros((GROUP, LANES), jnp.float32)
        for half in range(2):
            for k in range(groups):
                turned = halves[half] if k == 0 else pltpu.roll(halves[half], STEP * k, 1)
                for up in sorted({(half - to) * groups - k, (half - to) * groups + (groups - k if k else 0)}):
                    chosen = (row // groups == half) & (row - (to * groups + lane) == up)
                    by = up % GROUP
                    result = jnp.where(chosen, pltpu.roll(turned, by, 0) if by else turned, result)
        out.append(result)
    return jnp.concatenate(out, 1)


def score_kernel(order, lines_ref, start_ref, low_ref, out_ref, rows):
    band_rows, tile_width = out_ref.shape
    reach = tile_width + MAXB * DB
    span = MAXB * DB + STEP
    row16 = lax.broadcasted_iota(jnp.int32, (16, 2 * LANES), 0)
    owner16 = lax.broadcasted_iota(jnp.int32, (16, 2 * LANES), 1) // STEP
    window = jnp.where((row16 >= owner16) & (row16 < owner16 + 7), 1.0, 0.0).astype(jnp.bfloat16)
    only = jnp.where((row16 & 7) == owner16, 1.0, 0.0)[:GROUP]
    lane16 = lax.broadcasted_iota(jnp.int32, (16, LANES), 1) // STEP
    lane_group = [jnp.where(lane16 == p, 1.0, 0.0) for p in range(LANES // STEP)]
    lane_group8 = [v[:GROUP] for v in lane_group]
    lane_group = [v.astype(jnp.bfloat16) for v in lane_group]
    past = lax.broadcasted_iota(jnp.int32, (span, LANES), 0) - (
        lax.broadcasted_iota(jnp.int32, (span, LANES), 1) & (STEP - 1)
    )
    inside = (past >= low_ref[0:1, :]) & (past < MAXB * DB)
    cap = jnp.where(inside, FAR, -FAR)
    always = (DB + STEP, MAXB * DB)
    height = lines_ref.shape[0]
    each = height // len(order)
    rows[:3] = jnp.zeros((3, TILES, LANES), jnp.float32)
    rows[height + 3 :] = jnp.zeros((5, TILES, LANES), jnp.float32)
    for member, chip in enumerate(order):
        for line in range(each):
            rows[3 + chip * each + line] = lines_ref[member * each + line].astype(jnp.float32)
    flat = rows.reshape(rows.shape[0] * TILES, LANES)
    start = start_ref[0, 0]
    lane = lax.broadcasted_iota(jnp.int32, (16, LANES), 1)

    def moved(pieces, by):
        turned = [pltpu.roll(v, by, 1) for v in pieces]
        ahead_by = [jnp.where(lane < by, a, b) for a, b in zip(turned, turned[1:])]
        return jnp.concatenate(ahead_by, 1).astype(jnp.bfloat16)

    for group in range(band_rows // GROUP):
        first = (lax.axis_index("rows") * band_rows + group * GROUP) * TILES
        tiles = [flat[pl.ds(first + t, 16, stride=TILES), :] for t in range(TILES)]
        left = jnp.concatenate(tiles[:LEFT_TILES], 1).astype(jnp.bfloat16)
        shifted_right = [moved(tiles[LEFT_TILES:], RIGHT_LEAD - 4 - j + start) for j in range(7)]
        shifted_left = [ahead(left, j, 1)[:, :tile_width] for j in range(7)]
        blank = jnp.zeros((16, reach), jnp.bfloat16)
        near_side = jnp.transpose(jnp.concatenate(shifted_right + [blank], 0))
        _, right_mean, right_scale = moments(shifted_right)
        left_total, _, left_scale = moments(shifted_left)
        far_side = [p.astype(jnp.float32) for p in 3 * parts(right_mean) + parts(right_scale)]
        far_side = jnp.transpose(jnp.concatenate(far_side, 0).astype(jnp.bfloat16))
        right_side = jnp.concatenate([near_side, far_side], 1)
        depth = right_side.shape[1]
        near = [spread_out(v, lane_group) for v in shifted_left]
        far = [spread_out(p.astype(jnp.float32), lane_group8) for p in parts(-left_total)]
        source = lax.broadcasted_iota(jnp.int32, (depth, 2 * LANES), 0)
        owner = lax.broadcasted_iota(jnp.int32, (depth, 2 * LANES), 1) // STEP
        picked = (source >= 128 + 9 * GROUP) & ((source & 7) == owner)
        picks = jnp.where(picked, 1.0, 0.0).astype(jnp.bfloat16)
        scale = jnp.dot(right_side, picks, preferred_element_type=jnp.float32)
        none = jnp.zeros((16, 2 * LANES), jnp.bfloat16)
        none24 = jnp.zeros((3 * GROUP, 2 * LANES), jnp.float32)
        found = []
        for block in range(tile_width // STEP):
            left_side = [jnp.concatenate([v[block]] * 2, 1) * window for v in near] + [none]
            means = [jnp.concatenate([a[block]] * 2, 1) * only for a in far for _ in range(3)]
            left_side.append(jnp.concatenate(means + [none24], 0).astype(jnp.bfloat16))
            reached = slice(block * STEP, block * STEP + span)
            products = jnp.dot(
                right_side[reached], jnp.concatenate(left_side, 0), preferred_element_type=jnp.float32
            )
            halves = []
            for half in range(2):
                at = slice(half * LANES, (half + 1) * LANES)
                scaled = products[:, at] * scale[reached, at]
                kept = [
                    jnp.minimum(scaled[: always[0]], cap[: always[0]]),
                    scaled[always[0] : always[1]],
                    jnp.minimum(scaled[always[1] :], cap[always[1] :]),
                ]
                halves.append(jnp.max(functools.reduce(jnp.maximum, [fold(v) for v in kept]), axis=0, keepdims=True))
            found.append(jnp.concatenate(halves, 1))
        best = regroup(jnp.concatenate(found, 0)) * (left_scale * (1.0 / 49.0))
        out_ref[group * GROUP : (group + 1) * GROUP, :] = jnp.maximum(best, -2.0)


def score(lines, start, low, order, band_rows, tile_width):
    return pl.pallas_call(
        functools.partial(score_kernel, order),
        out_shape=jax.ShapeDtypeStruct((band_rows, tile_width), jnp.float32),
        in_specs=[VMEM, VMEM, VMEM],
        out_specs=VMEM,
        scratch_shapes=[pltpu.VMEM((lines.shape[0] + 8, TILES, LANES), jnp.float32)],
        compiler_params=pltpu.CompilerParams(vmem_limit_bytes=16 * 2**20),
    )(lines, start, low)


def on_device(left_image, right_image, ranges):
    bands, tiles = lax.axis_size("rows"), lax.axis_size("cols")
    strip, width = left_image.shape
    swap = [(i, i ^ 1) for i in range(tiles)]
    left_other = lax.ppermute(left_image, "cols", swap)
    right_other = lax.ppermute(right_image, "cols", swap)
    own, start, low = cut_own(left_image, right_image, ranges, tiles)
    pieces = cut_pair(own, left_other, right_other, bands, tiles)
    order = chip_order(bands, tiles // 2)
    groups = [[2 * chip + (side if chip % (tiles // 2) else 1 - side) for chip in order] for side in range(2)]
    lines = lax.all_to_all(
        pieces, ("rows", "cols"), split_axis=0, concat_axis=0, tiled=True, axis_index_groups=groups
    )
    lines = lines.reshape(bands * tiles * strip, TILES, LANES)
    return score(lines, start, low, order, strip * tiles, width // tiles)


def solution(mesh):
    return jax.shard_map(
        on_device,
        mesh=mesh,
        in_specs=(P(("rows", "cols"), None), P(("rows", "cols"), None), P()),
        out_specs=P("rows", "cols"),
        check_vma=False,
    )
```

```python
import functools

import jax
import jax.numpy as jnp
from jax import lax
from jax.experimental import pallas as pl
from jax.experimental.pallas import tpu as pltpu
from jax.sharding import PartitionSpec as P

DB = 128
MAXB = 2
LANES = 128
LEFT_TILES = 3
RIGHT_TILES = 5
TILES = LEFT_TILES + RIGHT_TILES
LEAD = 3
RIGHT_LEAD = 67
GROUP = 8
STEP = 32
FAR = 3.0e37
VMEM = pl.BlockSpec(memory_space=pltpu.VMEM)
HBM = pl.BlockSpec(memory_space=pltpu.HBM)


def chip_order(bands, pairs):
    chips = bands * pairs
    leader = chips - 2
    away = {chip: bin(chip // pairs).count("1") + chip % pairs for chip in range(1, chips)}
    far_first = sorted(away, key=lambda chip: (-away[chip], chip != leader, chip))
    steps = list(range(2, chips, 2)) + list(range(1, chips, 2))
    first = -steps[far_first.index(leader)] % chips
    order = [0] * chips
    for step, chip in zip(steps, far_first):
        order[(first + step) % chips] = chip
    return order


def side_of(tile):
    return lax.rem(tile + jnp.where(tile < 2, 1, 0), 2)


def cut(left_rows, right_rows, first):
    lane = lax.broadcasted_iota(jnp.int32, (8, LANES), 1)

    def shifted(rows, at, by):
        here = pltpu.roll(rows[pl.ds(at, 8), :], by, 1)
        after = pltpu.roll(rows[pl.ds(at + 1, 8), :], by, 1)
        return jnp.where(lane < by, here, after)

    left_part = shifted(left_rows, first - 1, 3)[:LEFT_TILES]
    right_part = shifted(right_rows, first - 3, RIGHT_LEAD)[:RIGHT_TILES]
    return jnp.concatenate([left_part, right_part], 0).astype(jnp.bfloat16)


def cut_all(tiles, left_ref, right_ref, left_rows, right_rows, put):
    strip, width = left_ref.shape
    chunks = width // LANES
    per_tile = chunks // tiles
    side = side_of(lax.axis_index("cols"))
    for line in range(strip):
        for chunk in range(chunks):
            span = slice(chunk * LANES, (chunk + 1) * LANES)
            at = slice(LEAD + chunk, LEAD + chunk + 1)
            left_rows[at, :] = left_ref[line : line + 1, span].astype(jnp.float32)
            right_rows[at, :] = right_ref[line : line + 1, span].astype(jnp.float32)
        for pair in range(tiles // 2):
            tile = 2 * pair + (side if pair else 1 - side)
            put(pair, line, cut(left_rows, right_rows, LEAD + tile * per_tile))


def own_kernel(tiles, left_hbm, right_hbm, ranges_hbm, out_ref, start_ref, low_ref, left_ref, right_ref, ranges_ref, left_rows, right_rows, sems):
    copies = [
        pltpu.make_async_copy(source, target, sems.at[i])
        for i, (source, target) in enumerate(
            [(ranges_hbm, ranges_ref), (left_hbm, left_ref), (right_hbm, right_ref)]
        )
    ]
    for copy in copies:
        copy.start()
    left_rows[...] = jnp.zeros_like(left_rows)
    right_rows[...] = jnp.zeros_like(right_rows)
    for copy in copies:
        copy.wait()
    tile = lax.axis_index("cols")
    start_ref[...] = jnp.full(start_ref.shape, ranges_ref[0, tile], jnp.int32)
    low_ref[...] = jnp.full(low_ref.shape, MAXB * DB - DB * ranges_ref[1, tile], jnp.int32)

    def put(pair, line, piece):
        out_ref[pair, line] = piece

    cut_all(tiles, left_ref, right_ref, left_rows, right_rows, put)


def cut_own(left, right, ranges, tiles):
    strip, width = left.shape
    rows = LEAD + width // LANES + 13
    return pl.pallas_call(
        functools.partial(own_kernel, tiles),
        out_shape=[
            jax.ShapeDtypeStruct((tiles // 2, strip, TILES, LANES), jnp.bfloat16),
            jax.ShapeDtypeStruct((8, LANES), jnp.int32),
            jax.ShapeDtypeStruct((8, LANES), jnp.int32),
        ],
        in_specs=[HBM, HBM, HBM],
        out_specs=[VMEM, VMEM, VMEM],
        scratch_shapes=[
            pltpu.VMEM(left.shape, left.dtype),
            pltpu.VMEM(right.shape, right.dtype),
            pltpu.SMEM((2, tiles), jnp.int32),
            pltpu.VMEM((rows, LANES), jnp.float32),
            pltpu.VMEM((rows, LANES), jnp.float32),
            pltpu.SemaphoreType.DMA((3,)),
        ],
        compiler_params=pltpu.CompilerParams(vmem_limit_bytes=8 * 2**20),
        cost_estimate=pl.CostEstimate(flops=10**6, bytes_accessed=2**16, transcendentals=0),
    )(*[pltpu.with_memory_space_constraint(v, pltpu.HBM) for v in (left, right, ranges.T)])


def pair_kernel(bands, tiles, own_ref, left_ref, right_ref, out_ref, left_rows, right_rows):
    left_rows[...] = jnp.zeros_like(left_rows)
    right_rows[...] = jnp.zeros_like(right_rows)
    core = lax.rem(lax.axis_index("cols"), 2)
    order = chip_order(bands, tiles // 2)

    def put(pair, line, piece):
        mine = own_ref[pair, line]
        for band in range(bands):
            member = order.index(band * (tiles // 2) + pair)
            out_ref[member, core, line] = mine
            out_ref[member, 1 - core, line] = piece

    cut_all(tiles, left_ref, right_ref, left_rows, right_rows, put)


def cut_pair(own, left, right, bands, tiles):
    strip, width = left.shape
    rows = LEAD + width // LANES + 13
    return pl.pallas_call(
        functools.partial(pair_kernel, bands, tiles),
        out_shape=jax.ShapeDtypeStruct((bands * tiles // 2, 2, strip, TILES, LANES), jnp.bfloat16),
        in_specs=[VMEM, VMEM, VMEM],
        out_specs=VMEM,
        scratch_shapes=[pltpu.VMEM((rows, LANES), jnp.float32), pltpu.VMEM((rows, LANES), jnp.float32)],
        compiler_params=pltpu.CompilerParams(vmem_limit_bytes=8 * 2**20),
    )(own, left, right)


def ahead(values, by, axis):
    if by == 0:
        return values
    return pltpu.roll(values, values.shape[axis] - by, axis)


def column_sum(values):
    two = values + ahead(values, 1, 0)
    four = two + ahead(two, 2, 0)
    return (four + ahead(two, 4, 0) + ahead(values, 6, 0))[:GROUP]


def moments(shifted):
    shifted = [v.astype(jnp.float32) for v in shifted]
    total = column_sum(sum(shifted[1:], shifted[0]))
    squares = [v * v for v in shifted]
    mean = total * (1.0 / 49.0)
    spread = column_sum(sum(squares[1:], squares[0])) * (1.0 / 49.0) - mean * mean
    return total, mean, lax.rsqrt(jnp.maximum(spread, 0.01))


def parts(values):
    high = values.astype(jnp.bfloat16)
    rest = values - high.astype(jnp.float32)
    middle = rest.astype(jnp.bfloat16)
    low = (rest - middle.astype(jnp.float32)).astype(jnp.bfloat16)
    return [high, middle, low]


def sum_of(values):
    return functools.reduce(lambda a, b: a + b, values)


def fold(values):
    return functools.reduce(jnp.maximum, [values[i : i + 8] for i in range(0, values.shape[0], 8)])


def spread_out(values, lane_group):
    out = []
    for tile in range(values.shape[1] // LANES):
        here = values[:, tile * LANES : (tile + 1) * LANES]
        turned = [here] + [pltpu.roll(here, STEP * k, 1) for k in range(1, LANES // STEP)]
        for g in range(LANES // STEP):
            block = turned[0]
            for k in range(1, LANES // STEP):
                block = jnp.where(lane_group[(g + k) % (LANES // STEP)] > 0, turned[k], block)
            out.append(block)
    return out


def regroup(found):
    groups = LANES // STEP
    row = lax.broadcasted_iota(jnp.int32, (GROUP, LANES), 0)
    lane = lax.broadcasted_iota(jnp.int32, (GROUP, LANES), 1) // STEP
    halves = [found[:, h * LANES : (h + 1) * LANES] for h in range(2)]
    out = []
    for to in range(2):
        result = jnp.zeros((GROUP, LANES), jnp.float32)
        for half in range(2):
            for k in range(groups):
                turned = halves[half] if k == 0 else pltpu.roll(halves[half], STEP * k, 1)
                for up in sorted({(half - to) * groups - k, (half - to) * groups + (groups - k if k else 0)}):
                    chosen = (row // groups == half) & (row - (to * groups + lane) == up)
                    by = up % GROUP
                    result = jnp.where(chosen, pltpu.roll(turned, by, 0) if by else turned, result)
        out.append(result)
    return jnp.concatenate(out, 1)


def score_kernel(order, lines_ref, start_ref, low_ref, out_ref, rows):
    band_rows, tile_width = out_ref.shape
    reach = tile_width + MAXB * DB
    span = MAXB * DB + STEP
    row16 = lax.broadcasted_iota(jnp.int32, (16, 2 * LANES), 0)
    owner16 = lax.broadcasted_iota(jnp.int32, (16, 2 * LANES), 1) // STEP
    window = jnp.where((row16 >= owner16) & (row16 < owner16 + 7), 1.0, 0.0).astype(jnp.bfloat16)
    only = jnp.where((row16 & 7) == owner16, 1.0, 0.0).astype(jnp.bfloat16)
    lane16 = lax.broadcasted_iota(jnp.int32, (16, LANES), 1) // STEP
    lane_group = [jnp.where(lane16 == p, 1.0, 0.0) for p in range(LANES // STEP)]
    lane_group = [v.astype(jnp.bfloat16) for v in lane_group]
    past = lax.broadcasted_iota(jnp.int32, (span, LANES), 0) - (
        lax.broadcasted_iota(jnp.int32, (span, LANES), 1) & (STEP - 1)
    )
    inside = (past >= low_ref[0:1, :]) & (past < MAXB * DB)
    cap = jnp.where(inside, FAR, -FAR)
    always = (DB + STEP, MAXB * DB)
    height = lines_ref.shape[0]
    each = height // len(order)
    rows[: 3 * TILES] = jnp.zeros((3 * TILES, LANES), jnp.float32)
    rows[(height + 3) * TILES :] = jnp.zeros((6 * TILES, LANES), jnp.float32)
    for member, chip in enumerate(order):
        for line in range(each):
            at = (3 + chip * each + line) * TILES
            rows[at : at + TILES] = lines_ref[member * each + line].astype(jnp.float32)
    start = start_ref[0, 0]
    lane = lax.broadcasted_iota(jnp.int32, (16, LANES), 1)

    def moved(pieces, by):
        turned = [pltpu.roll(v, by, 1) for v in pieces]
        ahead_by = [jnp.where(lane < by, a, b) for a, b in zip(turned, turned[1:])]
        return jnp.concatenate(ahead_by, 1).astype(jnp.bfloat16)

    for group in range(band_rows // GROUP):
        first = (lax.axis_index("rows") * band_rows + group * GROUP) * TILES
        tiles = [rows[pl.ds(first + t, 16, stride=TILES), :] for t in range(TILES)]
        left = jnp.concatenate(tiles[:LEFT_TILES], 1).astype(jnp.bfloat16)
        shifted_right = [moved(tiles[LEFT_TILES:], RIGHT_LEAD - 4 - j + start) for j in range(7)]
        shifted_left = [ahead(left, j, 1)[:, :tile_width] for j in range(7)]
        blank = jnp.zeros((16, reach), jnp.bfloat16)
        near_side = jnp.transpose(jnp.concatenate(shifted_right + [blank], 0))
        _, right_mean, right_scale = moments(shifted_right)
        left_total, _, left_scale = moments(shifted_left)
        high, middle, low = [p.astype(jnp.float32) for p in parts(right_mean)]
        far_side = [high, high, middle, middle, low, low, high, middle, low, jnp.zeros_like(low)]
        far_side += [p.astype(jnp.float32) for p in parts(right_scale)] + [jnp.zeros_like(low)]
        far_side = jnp.transpose(jnp.concatenate(far_side, 0).astype(jnp.bfloat16))
        right_side = jnp.concatenate([near_side, far_side], 1)
        depth = right_side.shape[1]
        near = [spread_out(v, lane_group) for v in shifted_left]
        high, middle, low = [p.astype(jnp.float32) for p in parts(-left_total)]
        far = [jnp.concatenate(p, 0).astype(jnp.bfloat16) for p in ((high, middle), (low, low))]
        far = [spread_out(p, lane_group) for p in far]
        source = lax.broadcasted_iota(jnp.int32, (depth, 2 * LANES), 0)
        owner = lax.broadcasted_iota(jnp.int32, (depth, 2 * LANES), 1) // STEP
        picked = (source >= 128 + 10 * GROUP) & ((source & 7) == owner)
        picks = jnp.where(picked, 1.0, 0.0).astype(jnp.bfloat16)
        scale = jnp.dot(right_side, picks, preferred_element_type=jnp.float32)
        none = jnp.zeros((16, 2 * LANES), jnp.bfloat16)
        none32 = jnp.zeros((32, 2 * LANES), jnp.bfloat16)
        found = []
        for block in range(tile_width // STEP):
            left_side = [jnp.concatenate([v[block]] * 2, 1) * window for v in near] + [none]
            two, last = [jnp.concatenate([a[block]] * 2, 1) * only for a in far]
            left_side += [two, two, two, last, last, none32]
            reached = slice(block * STEP, block * STEP + span)
            products = jnp.dot(
                right_side[reached], jnp.concatenate(left_side, 0), preferred_element_type=jnp.float32
            )
            halves = []
            for half in range(2):
                at = slice(half * LANES, (half + 1) * LANES)
                scaled = products[:, at] * scale[reached, at]
                kept = [
                    jnp.minimum(scaled[: always[0]], cap[: always[0]]),
                    scaled[always[0] : always[1]],
                    jnp.minimum(scaled[always[1] :], cap[always[1] :]),
                ]
                halves.append(jnp.max(functools.reduce(jnp.maximum, [fold(v) for v in kept]), axis=0, keepdims=True))
            found.append(jnp.concatenate(halves, 1))
        best = regroup(jnp.concatenate(found, 0)) * (left_scale * (1.0 / 49.0))
        out_ref[group * GROUP : (group + 1) * GROUP, :] = jnp.maximum(best, -2.0)


def score(lines, start, low, order, band_rows, tile_width):
    return pl.pallas_call(
        functools.partial(score_kernel, order),
        out_shape=jax.ShapeDtypeStruct((band_rows, tile_width), jnp.float32),
        in_specs=[VMEM, VMEM, VMEM],
        out_specs=VMEM,
        scratch_shapes=[pltpu.VMEM(((lines.shape[0] + 9) * TILES, LANES), jnp.float32)],
        compiler_params=pltpu.CompilerParams(vmem_limit_bytes=16 * 2**20),
    )(lines, start, low)


def on_device(left_image, right_image, ranges):
    bands, tiles = lax.axis_size("rows"), lax.axis_size("cols")
    strip, width = left_image.shape
    swap = [(i, i ^ 1) for i in range(tiles)]
    left_other = lax.ppermute(left_image, "cols", swap)
    right_other = lax.ppermute(right_image, "cols", swap)
    own, start, low = cut_own(left_image, right_image, ranges, tiles)
    pieces = cut_pair(own, left_other, right_other, bands, tiles)
    order = chip_order(bands, tiles // 2)
    groups = [[2 * chip + (side if chip % (tiles // 2) else 1 - side) for chip in order] for side in range(2)]
    lines = lax.all_to_all(
        pieces, ("rows", "cols"), split_axis=0, concat_axis=0, tiled=True, axis_index_groups=groups
    )
    lines = lines.reshape(bands * tiles * strip, TILES, LANES)
    return score(lines, start, low, order, strip * tiles, width // tiles)


def solution(mesh):
    return jax.shard_map(
        on_device,
        mesh=mesh,
        in_specs=(P(("rows", "cols"), None), P(("rows", "cols"), None), P()),
        out_specs=P("rows", "cols"),
        check_vma=False,
    )
```

```python
import functools

import jax
import jax.numpy as jnp
from jax import lax
from jax.experimental import pallas as pl
from jax.experimental.pallas import tpu as pltpu
from jax.sharding import PartitionSpec as P

DB = 128
MAXB = 2
LANES = 128
LEFT_TILES = 3
RIGHT_TILES = 5
TILES = LEFT_TILES + RIGHT_TILES
LEAD = 3
RIGHT_LEAD = 67
GROUP = 8
STEP = 32
FAR = 3.0e37
VMEM = pl.BlockSpec(memory_space=pltpu.VMEM)
HBM = pl.BlockSpec(memory_space=pltpu.HBM)


def chip_order(bands, pairs):
    chips = bands * pairs
    leader = chips - 2
    away = {chip: bin(chip // pairs).count("1") + chip % pairs for chip in range(1, chips)}
    far_first = sorted(away, key=lambda chip: (-away[chip], chip != leader, chip))
    steps = list(range(2, chips, 2)) + list(range(1, chips, 2))
    first = -steps[far_first.index(leader)] % chips
    order = [0] * chips
    for step, chip in zip(steps, far_first):
        order[(first + step) % chips] = chip
    return order


def side_of(tile):
    return lax.rem(tile + jnp.where(tile < 2, 1, 0), 2)


def cut(left_rows, right_rows, first):
    lane = lax.broadcasted_iota(jnp.int32, (8, LANES), 1)

    def shifted(rows, at, by):
        here = pltpu.roll(rows[pl.ds(at, 8), :], by, 1)
        after = pltpu.roll(rows[pl.ds(at + 1, 8), :], by, 1)
        return jnp.where(lane < by, here, after)

    left_part = shifted(left_rows, first - 1, 3)[:LEFT_TILES]
    right_part = shifted(right_rows, first - 3, RIGHT_LEAD)[:RIGHT_TILES]
    return jnp.concatenate([left_part, right_part], 0).astype(jnp.bfloat16)


def cut_all(tiles, left_ref, right_ref, left_rows, right_rows, put):
    strip, width = left_ref.shape
    chunks = width // LANES
    per_tile = chunks // tiles
    side = side_of(lax.axis_index("cols"))
    for line in range(strip):
        for chunk in range(chunks):
            span = slice(chunk * LANES, (chunk + 1) * LANES)
            at = slice(LEAD + chunk, LEAD + chunk + 1)
            left_rows[at, :] = left_ref[line : line + 1, span].astype(jnp.float32)
            right_rows[at, :] = right_ref[line : line + 1, span].astype(jnp.float32)
        for pair in range(tiles // 2):
            tile = 2 * pair + (side if pair else 1 - side)
            put(pair, line, cut(left_rows, right_rows, LEAD + tile * per_tile))


def own_kernel(tiles, left_hbm, right_hbm, ranges_hbm, out_ref, start_ref, low_ref, left_ref, right_ref, ranges_ref, left_rows, right_rows, sems):
    copies = [
        pltpu.make_async_copy(source, target, sems.at[i])
        for i, (source, target) in enumerate(
            [(ranges_hbm, ranges_ref), (left_hbm, left_ref), (right_hbm, right_ref)]
        )
    ]
    for copy in copies:
        copy.start()
    left_rows[...] = jnp.zeros_like(left_rows)
    right_rows[...] = jnp.zeros_like(right_rows)
    for copy in copies:
        copy.wait()
    tile = lax.axis_index("cols")
    start_ref[...] = jnp.full(start_ref.shape, ranges_ref[0, tile], jnp.int32)
    low_ref[...] = jnp.full(low_ref.shape, MAXB * DB - DB * ranges_ref[1, tile], jnp.int32)

    def put(pair, line, piece):
        out_ref[pair, line] = piece

    cut_all(tiles, left_ref, right_ref, left_rows, right_rows, put)


def cut_own(left, right, ranges, tiles):
    strip, width = left.shape
    rows = LEAD + width // LANES + 13
    return pl.pallas_call(
        functools.partial(own_kernel, tiles),
        out_shape=[
            jax.ShapeDtypeStruct((tiles // 2, strip, TILES, LANES), jnp.bfloat16),
            jax.ShapeDtypeStruct((8, LANES), jnp.int32),
            jax.ShapeDtypeStruct((8, LANES), jnp.int32),
        ],
        in_specs=[HBM, HBM, HBM],
        out_specs=[VMEM, VMEM, VMEM],
        scratch_shapes=[
            pltpu.VMEM(left.shape, left.dtype),
            pltpu.VMEM(right.shape, right.dtype),
            pltpu.SMEM((2, tiles), jnp.int32),
            pltpu.VMEM((rows, LANES), jnp.float32),
            pltpu.VMEM((rows, LANES), jnp.float32),
            pltpu.SemaphoreType.DMA((3,)),
        ],
        compiler_params=pltpu.CompilerParams(vmem_limit_bytes=8 * 2**20),
        cost_estimate=pl.CostEstimate(flops=10**6, bytes_accessed=2**16, transcendentals=0),
    )(*[pltpu.with_memory_space_constraint(v, pltpu.HBM) for v in (left, right, ranges.T)])


def pair_kernel(bands, tiles, own_ref, left_ref, right_ref, out_ref, left_rows, right_rows):
    left_rows[...] = jnp.zeros_like(left_rows)
    right_rows[...] = jnp.zeros_like(right_rows)
    core = lax.rem(lax.axis_index("cols"), 2)
    order = chip_order(bands, tiles // 2)

    def put(pair, line, piece):
        mine = own_ref[pair, line]
        for band in range(bands):
            member = order.index(band * (tiles // 2) + pair)
            out_ref[member, core, line] = mine
            out_ref[member, 1 - core, line] = piece

    cut_all(tiles, left_ref, right_ref, left_rows, right_rows, put)


def cut_pair(own, left, right, bands, tiles):
    strip, width = left.shape
    rows = LEAD + width // LANES + 13
    return pl.pallas_call(
        functools.partial(pair_kernel, bands, tiles),
        out_shape=jax.ShapeDtypeStruct((bands * tiles // 2, 2, strip, TILES, LANES), jnp.bfloat16),
        in_specs=[VMEM, VMEM, VMEM],
        out_specs=VMEM,
        scratch_shapes=[pltpu.VMEM((rows, LANES), jnp.float32), pltpu.VMEM((rows, LANES), jnp.float32)],
        compiler_params=pltpu.CompilerParams(vmem_limit_bytes=8 * 2**20),
    )(own, left, right)


def ahead(values, by, axis):
    if by == 0:
        return values
    return pltpu.roll(values, values.shape[axis] - by, axis)


def column_sum(values):
    two = values + ahead(values, 1, 0)
    four = two + ahead(two, 2, 0)
    return (four + ahead(two, 4, 0) + ahead(values, 6, 0))[:GROUP]


def moments(shifted):
    shifted = [v.astype(jnp.float32) for v in shifted]
    total = column_sum(sum(shifted[1:], shifted[0]))
    squares = [v * v for v in shifted]
    mean = total * (1.0 / 49.0)
    spread = column_sum(sum(squares[1:], squares[0])) * (1.0 / 49.0) - mean * mean
    return total, mean, lax.rsqrt(jnp.maximum(spread, 0.01))


def parts(values):
    high = values.astype(jnp.bfloat16)
    rest = values - high.astype(jnp.float32)
    middle = rest.astype(jnp.bfloat16)
    low = (rest - middle.astype(jnp.float32)).astype(jnp.bfloat16)
    return [high, middle, low]


def sum_of(values):
    return functools.reduce(lambda a, b: a + b, values)


def fold(values):
    return functools.reduce(jnp.maximum, [values[i : i + 8] for i in range(0, values.shape[0], 8)])


def spread_out(values, lane_group):
    out = []
    for tile in range(values.shape[1] // LANES):
        here = values[:, tile * LANES : (tile + 1) * LANES]
        turned = [here] + [pltpu.roll(here, STEP * k, 1) for k in range(1, LANES // STEP)]
        for g in range(LANES // STEP):
            block = turned[0]
            for k in range(1, LANES // STEP):
                block = jnp.where(lane_group[(g + k) % (LANES // STEP)] > 0, turned[k], block)
            out.append(block)
    return out


def regroup(found):
    groups = LANES // STEP
    row = lax.broadcasted_iota(jnp.int32, (GROUP, LANES), 0)
    lane = lax.broadcasted_iota(jnp.int32, (GROUP, LANES), 1) // STEP
    halves = [found[:, h * LANES : (h + 1) * LANES] for h in range(2)]
    out = []
    for to in range(2):
        result = jnp.zeros((GROUP, LANES), jnp.float32)
        for half in range(2):
            for k in range(groups):
                turned = halves[half] if k == 0 else pltpu.roll(halves[half], STEP * k, 1)
                for up in sorted({(half - to) * groups - k, (half - to) * groups + (groups - k if k else 0)}):
                    chosen = (row // groups == half) & (row - (to * groups + lane) == up)
                    by = up % GROUP
                    result = jnp.where(chosen, pltpu.roll(turned, by, 0) if by else turned, result)
        out.append(result)
    return jnp.concatenate(out, 1)


def score_kernel(order, lines_ref, start_ref, low_ref, out_ref, rows):
    band_rows, tile_width = out_ref.shape
    reach = tile_width + MAXB * DB
    span = MAXB * DB + STEP
    row16 = lax.broadcasted_iota(jnp.int32, (16, 2 * LANES), 0)
    owner16 = lax.broadcasted_iota(jnp.int32, (16, 2 * LANES), 1) // STEP
    window = jnp.where((row16 >= owner16) & (row16 < owner16 + 7), 1.0, 0.0).astype(jnp.bfloat16)
    only = jnp.where((row16 & 7) == owner16, 1.0, 0.0).astype(jnp.bfloat16)
    lane16 = lax.broadcasted_iota(jnp.int32, (16, LANES), 1) // STEP
    lane_group = [jnp.where(lane16 == p, 1.0, 0.0) for p in range(LANES // STEP)]
    lane_group = [v.astype(jnp.bfloat16) for v in lane_group]
    past = lax.broadcasted_iota(jnp.int32, (span, LANES), 0) - (
        lax.broadcasted_iota(jnp.int32, (span, LANES), 1) & (STEP - 1)
    )
    inside = (past >= low_ref[0:1, :]) & (past < MAXB * DB)
    cap = jnp.where(inside, FAR, -FAR)
    always = (DB + STEP, MAXB * DB)
    height = lines_ref.shape[0]
    each = height // len(order)
    rows[: 3 * TILES] = jnp.zeros((3 * TILES, LANES), jnp.float32)
    rows[(height + 3) * TILES :] = jnp.zeros((6 * TILES, LANES), jnp.float32)
    for member, chip in enumerate(order):
        for line in range(each):
            at = (3 + chip * each + line) * TILES
            rows[at : at + TILES] = lines_ref[member * each + line].astype(jnp.float32)
    start = start_ref[0, 0]
    lane = lax.broadcasted_iota(jnp.int32, (16, LANES), 1)

    def moved(pieces, by):
        turned = [pltpu.roll(v, by, 1) for v in pieces]
        ahead_by = [jnp.where(lane < by, a, b) for a, b in zip(turned, turned[1:])]
        return jnp.concatenate(ahead_by, 1).astype(jnp.bfloat16)

    for group in range(band_rows // GROUP):
        first = (lax.axis_index("rows") * band_rows + group * GROUP) * TILES
        tiles = [rows[pl.ds(first + t, 16, stride=TILES), :] for t in range(TILES)]
        left = jnp.concatenate(tiles[:LEFT_TILES], 1).astype(jnp.bfloat16)
        shifted_right = [moved(tiles[LEFT_TILES:], RIGHT_LEAD - 4 - j + start) for j in range(7)]
        shifted_left = [ahead(left, j, 1)[:, :tile_width] for j in range(7)]
        blank = jnp.zeros((16, reach), jnp.bfloat16)
        near_side = jnp.transpose(jnp.concatenate(shifted_right + [blank], 0))
        _, right_mean, right_scale = moments(shifted_right)
        left_total, _, left_scale = moments(shifted_left)
        high, middle, low = [p.astype(jnp.float32) for p in parts(right_mean)]
        far_side = [high, high, middle, middle, low, low, high, middle, low, jnp.zeros_like(low)]
        far_side += [p.astype(jnp.float32) for p in parts(right_scale)] + [jnp.zeros_like(low)]
        far_side = jnp.transpose(jnp.concatenate(far_side, 0).astype(jnp.bfloat16))
        right_side = jnp.concatenate([near_side, far_side], 1)
        depth = far_side.shape[1]
        near = [spread_out(v, lane_group) for v in shifted_left]
        high, middle, low = [p.astype(jnp.float32) for p in parts(-left_total)]
        far = [jnp.concatenate(p, 0).astype(jnp.bfloat16) for p in ((high, middle), (low, low))]
        far = [spread_out(p, lane_group) for p in far]
        source = lax.broadcasted_iota(jnp.int32, (depth, 2 * LANES), 0)
        owner = lax.broadcasted_iota(jnp.int32, (depth, 2 * LANES), 1) // STEP
        picked = (source >= 10 * GROUP) & ((source & 7) == owner)
        picks = jnp.where(picked, 1.0, 0.0).astype(jnp.bfloat16)
        scale = jnp.dot(far_side, picks, preferred_element_type=jnp.float32)
        none = jnp.zeros((16, 2 * LANES), jnp.bfloat16)
        none32 = jnp.zeros((32, 2 * LANES), jnp.bfloat16)
        found = []
        for block in range(tile_width // STEP):
            left_side = [jnp.concatenate([v[block]] * 2, 1) * window for v in near] + [none]
            two, last = [jnp.concatenate([a[block]] * 2, 1) * only for a in far]
            left_side += [two, two, two, last, last, none32]
            reached = slice(block * STEP, block * STEP + span)
            products = jnp.dot(
                right_side[reached], jnp.concatenate(left_side, 0), preferred_element_type=jnp.float32
            )
            halves = []
            for half in range(2):
                at = slice(half * LANES, (half + 1) * LANES)
                scaled = products[:, at] * scale[reached, at]
                kept = [
                    jnp.minimum(scaled[: always[0]], cap[: always[0]]),
                    scaled[always[0] : always[1]],
                    jnp.minimum(scaled[always[1] :], cap[always[1] :]),
                ]
                halves.append(jnp.max(functools.reduce(jnp.maximum, [fold(v) for v in kept]), axis=0, keepdims=True))
            found.append(jnp.concatenate(halves, 1))
        best = regroup(jnp.concatenate(found, 0)) * (left_scale * (1.0 / 49.0))
        out_ref[group * GROUP : (group + 1) * GROUP, :] = jnp.maximum(best, -2.0)


def score(lines, start, low, order, band_rows, tile_width):
    return pl.pallas_call(
        functools.partial(score_kernel, order),
        out_shape=jax.ShapeDtypeStruct((band_rows, tile_width), jnp.float32),
        in_specs=[VMEM, VMEM, VMEM],
        out_specs=VMEM,
        scratch_shapes=[pltpu.VMEM(((lines.shape[0] + 9) * TILES, LANES), jnp.float32)],
        compiler_params=pltpu.CompilerParams(vmem_limit_bytes=16 * 2**20),
    )(lines, start, low)


def on_device(left_image, right_image, ranges):
    bands, tiles = lax.axis_size("rows"), lax.axis_size("cols")
    strip, width = left_image.shape
    swap = [(i, i ^ 1) for i in range(tiles)]
    left_other = lax.ppermute(left_image, "cols", swap)
    right_other = lax.ppermute(right_image, "cols", swap)
    own, start, low = cut_own(left_image, right_image, ranges, tiles)
    pieces = cut_pair(own, left_other, right_other, bands, tiles)
    order = chip_order(bands, tiles // 2)
    groups = [[2 * chip + (side if chip % (tiles // 2) else 1 - side) for chip in order] for side in range(2)]
    lines = lax.all_to_all(
        pieces, ("rows", "cols"), split_axis=0, concat_axis=0, tiled=True, axis_index_groups=groups
    )
    lines = lines.reshape(bands * tiles * strip, TILES, LANES)
    return score(lines, start, low, order, strip * tiles, width // tiles)


def solution(mesh):
    return jax.shard_map(
        on_device,
        mesh=mesh,
        in_specs=(P(("rows", "cols"), None), P(("rows", "cols"), None), P()),
        out_specs=P("rows", "cols"),
        check_vma=False,
    )
```

```python
import functools

import jax
import jax.numpy as jnp
from jax import lax
from jax.experimental import pallas as pl
from jax.experimental.pallas import tpu as pltpu
from jax.sharding import PartitionSpec as P

DB = 128
MAXB = 2
LANES = 128
LEFT_TILES = 3
RIGHT_TILES = 5
TILES = LEFT_TILES + RIGHT_TILES
LEAD = 3
RIGHT_LEAD = 67
GROUP = 8
STEP = 32
FAR = 3.0e37
VMEM = pl.BlockSpec(memory_space=pltpu.VMEM)
HBM = pl.BlockSpec(memory_space=pltpu.HBM)


def chip_order(bands, pairs):
    chips = bands * pairs
    leader = chips - 2
    away = {chip: bin(chip // pairs).count("1") + chip % pairs for chip in range(1, chips)}
    far_first = sorted(away, key=lambda chip: (-away[chip], chip != leader, chip))
    steps = list(range(2, chips, 2)) + list(range(1, chips, 2))
    first = -steps[far_first.index(leader)] % chips
    order = [0] * chips
    for step, chip in zip(steps, far_first):
        order[(first + step) % chips] = chip
    return order


def side_of(tile):
    return lax.rem(tile + jnp.where(tile < 2, 1, 0), 2)


def cut(left_rows, right_rows, first):
    lane = lax.broadcasted_iota(jnp.int32, (8, LANES), 1)

    def shifted(rows, at, by):
        here = pltpu.roll(rows[pl.ds(at, 8), :], by, 1)
        after = pltpu.roll(rows[pl.ds(at + 1, 8), :], by, 1)
        return jnp.where(lane < by, here, after)

    left_part = shifted(left_rows, first - 1, 3)[:LEFT_TILES]
    right_part = shifted(right_rows, first - 3, RIGHT_LEAD)[:RIGHT_TILES]
    return jnp.concatenate([left_part, right_part], 0).astype(jnp.bfloat16)


def cut_all(tiles, left_ref, right_ref, left_rows, right_rows, put):
    strip, width = left_ref.shape
    chunks = width // LANES
    per_tile = chunks // tiles
    side = side_of(lax.axis_index("cols"))
    for line in range(strip):
        for chunk in range(chunks):
            span = slice(chunk * LANES, (chunk + 1) * LANES)
            at = slice(LEAD + chunk, LEAD + chunk + 1)
            left_rows[at, :] = left_ref[line : line + 1, span].astype(jnp.float32)
            right_rows[at, :] = right_ref[line : line + 1, span].astype(jnp.float32)
        for pair in range(tiles // 2):
            tile = 2 * pair + (side if pair else 1 - side)
            put(pair, line, cut(left_rows, right_rows, LEAD + tile * per_tile))


def own_kernel(tiles, left_hbm, right_hbm, ranges_hbm, out_ref, start_ref, cap_ref, masks_ref, picks_ref, left_ref, right_ref, ranges_ref, left_rows, right_rows, sems):
    copies = [
        pltpu.make_async_copy(source, target, sems.at[i])
        for i, (source, target) in enumerate(
            [(ranges_hbm, ranges_ref), (left_hbm, left_ref), (right_hbm, right_ref)]
        )
    ]
    for copy in copies:
        copy.start()
    left_rows[...] = jnp.zeros_like(left_rows)
    right_rows[...] = jnp.zeros_like(right_rows)
    row16 = lax.broadcasted_iota(jnp.int32, (16, 2 * LANES), 0)
    owner16 = lax.broadcasted_iota(jnp.int32, (16, 2 * LANES), 1) // STEP
    window = jnp.where((row16 >= owner16) & (row16 < owner16 + 7), 1.0, 0.0)
    masks_ref[0] = window.astype(jnp.bfloat16)
    masks_ref[1] = jnp.where((row16 & 7) == owner16, 1.0, 0.0).astype(jnp.bfloat16)
    source = lax.broadcasted_iota(jnp.int32, picks_ref.shape, 0)
    owner = lax.broadcasted_iota(jnp.int32, picks_ref.shape, 1) // STEP
    picked = (source >= 10 * GROUP) & ((source & 7) == owner)
    picks_ref[...] = jnp.where(picked, 1.0, 0.0).astype(jnp.bfloat16)
    past = lax.broadcasted_iota(jnp.int32, cap_ref.shape, 0) - (
        lax.broadcasted_iota(jnp.int32, cap_ref.shape, 1) & (STEP - 1)
    )
    for copy in copies:
        copy.wait()
    tile = lax.axis_index("cols")
    start_ref[...] = jnp.full(start_ref.shape, ranges_ref[0, tile], jnp.int32)
    inside = (past >= MAXB * DB - DB * ranges_ref[1, tile]) & (past < MAXB * DB)
    cap_ref[...] = jnp.where(inside, FAR, -FAR)

    def put(pair, line, piece):
        out_ref[pair, line] = piece

    cut_all(tiles, left_ref, right_ref, left_rows, right_rows, put)


def cut_own(left, right, ranges, tiles):
    strip, width = left.shape
    rows = LEAD + width // LANES + 13
    return pl.pallas_call(
        functools.partial(own_kernel, tiles),
        out_shape=[
            jax.ShapeDtypeStruct((tiles // 2, strip, TILES, LANES), jnp.bfloat16),
            jax.ShapeDtypeStruct((8, LANES), jnp.int32),
            jax.ShapeDtypeStruct((MAXB * DB + STEP, LANES), jnp.float32),
            jax.ShapeDtypeStruct((2, 16, 2 * LANES), jnp.bfloat16),
            jax.ShapeDtypeStruct((14 * GROUP, 2 * LANES), jnp.bfloat16),
        ],
        in_specs=[HBM, HBM, HBM],
        out_specs=[VMEM] * 5,
        scratch_shapes=[
            pltpu.VMEM(left.shape, left.dtype),
            pltpu.VMEM(right.shape, right.dtype),
            pltpu.SMEM((2, tiles), jnp.int32),
            pltpu.VMEM((rows, LANES), jnp.float32),
            pltpu.VMEM((rows, LANES), jnp.float32),
            pltpu.SemaphoreType.DMA((3,)),
        ],
        compiler_params=pltpu.CompilerParams(vmem_limit_bytes=8 * 2**20),
        cost_estimate=pl.CostEstimate(flops=10**6, bytes_accessed=2**16, transcendentals=0),
    )(*[pltpu.with_memory_space_constraint(v, pltpu.HBM) for v in (left, right, ranges.T)])


def pair_kernel(bands, tiles, own_ref, left_ref, right_ref, out_ref, left_rows, right_rows):
    left_rows[...] = jnp.zeros_like(left_rows)
    right_rows[...] = jnp.zeros_like(right_rows)
    core = lax.rem(lax.axis_index("cols"), 2)
    order = chip_order(bands, tiles // 2)

    def put(pair, line, piece):
        mine = own_ref[pair, line]
        for band in range(bands):
            member = order.index(band * (tiles // 2) + pair)
            out_ref[member, core, line] = mine
            out_ref[member, 1 - core, line] = piece

    cut_all(tiles, left_ref, right_ref, left_rows, right_rows, put)


def cut_pair(own, left, right, bands, tiles):
    strip, width = left.shape
    rows = LEAD + width // LANES + 13
    return pl.pallas_call(
        functools.partial(pair_kernel, bands, tiles),
        out_shape=jax.ShapeDtypeStruct((bands * tiles // 2, 2, strip, TILES, LANES), jnp.bfloat16),
        in_specs=[VMEM, VMEM, VMEM],
        out_specs=VMEM,
        scratch_shapes=[pltpu.VMEM((rows, LANES), jnp.float32), pltpu.VMEM((rows, LANES), jnp.float32)],
        compiler_params=pltpu.CompilerParams(vmem_limit_bytes=8 * 2**20),
    )(own, left, right)


def ahead(values, by, axis):
    if by == 0:
        return values
    return pltpu.roll(values, values.shape[axis] - by, axis)


def column_sum(values):
    two = values + ahead(values, 1, 0)
    four = two + ahead(two, 2, 0)
    return (four + ahead(two, 4, 0) + ahead(values, 6, 0))[:GROUP]


def moments(shifted):
    shifted = [v.astype(jnp.float32) for v in shifted]
    total = column_sum(sum(shifted[1:], shifted[0]))
    squares = [v * v for v in shifted]
    mean = total * (1.0 / 49.0)
    spread = column_sum(sum(squares[1:], squares[0])) * (1.0 / 49.0) - mean * mean
    return total, mean, lax.rsqrt(jnp.maximum(spread, 0.01))


def parts(values):
    high = values.astype(jnp.bfloat16)
    rest = values - high.astype(jnp.float32)
    middle = rest.astype(jnp.bfloat16)
    low = (rest - middle.astype(jnp.float32)).astype(jnp.bfloat16)
    return [high, middle, low]


def sum_of(values):
    return functools.reduce(lambda a, b: a + b, values)


def fold(values):
    return functools.reduce(jnp.maximum, [values[i : i + 8] for i in range(0, values.shape[0], 8)])


def spread_out(values, lane_group):
    out = []
    for tile in range(values.shape[1] // LANES):
        here = values[:, tile * LANES : (tile + 1) * LANES]
        turned = [here] + [pltpu.roll(here, STEP * k, 1) for k in range(1, LANES // STEP)]
        for g in range(LANES // STEP):
            block = turned[0]
            for k in range(1, LANES // STEP):
                block = jnp.where(lane_group[(g + k) % (LANES // STEP)] > 0, turned[k], block)
            out.append(block)
    return out


def regroup(found):
    groups = LANES // STEP
    row = lax.broadcasted_iota(jnp.int32, (GROUP, LANES), 0)
    lane = lax.broadcasted_iota(jnp.int32, (GROUP, LANES), 1) // STEP
    halves = [found[:, h * LANES : (h + 1) * LANES] for h in range(2)]
    out = []
    for to in range(2):
        result = jnp.zeros((GROUP, LANES), jnp.float32)
        for half in range(2):
            for k in range(groups):
                turned = halves[half] if k == 0 else pltpu.roll(halves[half], STEP * k, 1)
                for up in sorted({(half - to) * groups - k, (half - to) * groups + (groups - k if k else 0)}):
                    chosen = (row // groups == half) & (row - (to * groups + lane) == up)
                    by = up % GROUP
                    result = jnp.where(chosen, pltpu.roll(turned, by, 0) if by else turned, result)
        out.append(result)
    return jnp.concatenate(out, 1)


def score_kernel(order, lines_ref, start_ref, cap_ref, masks_ref, picks_ref, out_ref, rows):
    band_rows, tile_width = out_ref.shape
    reach = tile_width + MAXB * DB
    span = MAXB * DB + STEP
    window, only = masks_ref[0], masks_ref[1]
    lane16 = lax.broadcasted_iota(jnp.int32, (16, LANES), 1) // STEP
    lane_group = [jnp.where(lane16 == p, 1.0, 0.0) for p in range(LANES // STEP)]
    lane_group = [v.astype(jnp.bfloat16) for v in lane_group]
    always = (DB + STEP, MAXB * DB)
    height = lines_ref.shape[0]
    each = height // len(order)
    rows[: 3 * TILES] = jnp.zeros((3 * TILES, LANES), jnp.float32)
    rows[(height + 3) * TILES :] = jnp.zeros((6 * TILES, LANES), jnp.float32)
    for member, chip in enumerate(order):
        for line in range(each):
            at = (3 + chip * each + line) * TILES
            rows[at : at + TILES] = lines_ref[member * each + line].astype(jnp.float32)
    start = start_ref[0, 0]
    lane = lax.broadcasted_iota(jnp.int32, (16, LANES), 1)

    def moved(pieces, by):
        turned = [pltpu.roll(v, by, 1) for v in pieces]
        ahead_by = [jnp.where(lane < by, a, b) for a, b in zip(turned, turned[1:])]
        return jnp.concatenate(ahead_by, 1).astype(jnp.bfloat16)

    for group in range(band_rows // GROUP):
        first = (lax.axis_index("rows") * band_rows + group * GROUP) * TILES
        tiles = [rows[pl.ds(first + t, 16, stride=TILES), :] for t in range(TILES)]
        left = jnp.concatenate(tiles[:LEFT_TILES], 1).astype(jnp.bfloat16)
        shifted_right = [moved(tiles[LEFT_TILES:], RIGHT_LEAD - 4 - j + start) for j in range(7)]
        shifted_left = [ahead(left, j, 1)[:, :tile_width] for j in range(7)]
        blank = jnp.zeros((16, reach), jnp.bfloat16)
        near_side = jnp.transpose(jnp.concatenate(shifted_right + [blank], 0))
        _, right_mean, right_scale = moments(shifted_right)
        left_total, _, left_scale = moments(shifted_left)
        high, middle, low = [p.astype(jnp.float32) for p in parts(right_mean)]
        far_side = [high, high, middle, middle, low, low, high, middle, low, jnp.zeros_like(low)]
        far_side += [p.astype(jnp.float32) for p in parts(right_scale)] + [jnp.zeros_like(low)]
        far_side = jnp.transpose(jnp.concatenate(far_side, 0).astype(jnp.bfloat16))
        right_side = jnp.concatenate([near_side, far_side], 1)
        near = [spread_out(v, lane_group) for v in shifted_left]
        high, middle, low = [p.astype(jnp.float32) for p in parts(-left_total)]
        far = [jnp.concatenate(p, 0).astype(jnp.bfloat16) for p in ((high, middle), (low, low))]
        far = [spread_out(p, lane_group) for p in far]
        scale = jnp.dot(far_side, picks_ref[...], preferred_element_type=jnp.float32)
        none = jnp.zeros((16, 2 * LANES), jnp.bfloat16)
        none32 = jnp.zeros((32, 2 * LANES), jnp.bfloat16)
        found = []
        for block in range(tile_width // STEP):
            left_side = [jnp.concatenate([v[block]] * 2, 1) * window for v in near] + [none]
            two, last = [jnp.concatenate([a[block]] * 2, 1) * only for a in far]
            left_side += [two, two, two, last, last, none32]
            reached = slice(block * STEP, block * STEP + span)
            products = jnp.dot(
                right_side[reached], jnp.concatenate(left_side, 0), preferred_element_type=jnp.float32
            )
            halves = []
            for half in range(2):
                at = slice(half * LANES, (half + 1) * LANES)
                scaled = products[:, at] * scale[reached, at]
                kept = [
                    jnp.minimum(scaled[: always[0]], cap_ref[: always[0]]),
                    scaled[always[0] : always[1]],
                    jnp.minimum(scaled[always[1] :], cap_ref[always[1] :]),
                ]
                halves.append(jnp.max(functools.reduce(jnp.maximum, [fold(v) for v in kept]), axis=0, keepdims=True))
            found.append(jnp.concatenate(halves, 1))
        best = regroup(jnp.concatenate(found, 0)) * (left_scale * (1.0 / 49.0))
        out_ref[group * GROUP : (group + 1) * GROUP, :] = jnp.maximum(best, -2.0)


def score(lines, constants, order, band_rows, tile_width):
    return pl.pallas_call(
        functools.partial(score_kernel, order),
        out_shape=jax.ShapeDtypeStruct((band_rows, tile_width), jnp.float32),
        in_specs=[VMEM] * 5,
        out_specs=VMEM,
        scratch_shapes=[pltpu.VMEM(((lines.shape[0] + 9) * TILES, LANES), jnp.float32)],
        compiler_params=pltpu.CompilerParams(vmem_limit_bytes=16 * 2**20),
    )(lines, *constants)


def on_device(left_image, right_image, ranges):
    bands, tiles = lax.axis_size("rows"), lax.axis_size("cols")
    strip, width = left_image.shape
    swap = [(i, i ^ 1) for i in range(tiles)]
    left_other = lax.ppermute(left_image, "cols", swap)
    right_other = lax.ppermute(right_image, "cols", swap)
    own, *constants = cut_own(left_image, right_image, ranges, tiles)
    pieces = cut_pair(own, left_other, right_other, bands, tiles)
    order = chip_order(bands, tiles // 2)
    groups = [[2 * chip + (side if chip % (tiles // 2) else 1 - side) for chip in order] for side in range(2)]
    lines = lax.all_to_all(
        pieces, ("rows", "cols"), split_axis=0, concat_axis=0, tiled=True, axis_index_groups=groups
    )
    lines = lines.reshape(bands * tiles * strip, TILES, LANES)
    return score(lines, constants, order, strip * tiles, width // tiles)


def solution(mesh):
    return jax.shard_map(
        on_device,
        mesh=mesh,
        in_specs=(P(("rows", "cols"), None), P(("rows", "cols"), None), P()),
        out_specs=P("rows", "cols"),
        check_vma=False,
    )
```

```python
import functools

import jax
import jax.numpy as jnp
from jax import lax
from jax.experimental import pallas as pl
from jax.experimental.pallas import tpu as pltpu
from jax.sharding import PartitionSpec as P

DB = 128
MAXB = 2
LANES = 128
LEFT_TILES = 3
RIGHT_TILES = 5
TILES = LEFT_TILES + RIGHT_TILES
LEAD = 3
RIGHT_LEAD = 67
GROUP = 8
STEP = 32
FAR = 3.0e37
VMEM = pl.BlockSpec(memory_space=pltpu.VMEM)
HBM = pl.BlockSpec(memory_space=pltpu.HBM)


def chip_order(bands, pairs):
    chips = bands * pairs
    leader = chips - 2
    away = {chip: bin(chip // pairs).count("1") + chip % pairs for chip in range(1, chips)}
    far_first = sorted(away, key=lambda chip: (-away[chip], chip != leader, chip))
    steps = list(range(2, chips, 2)) + list(range(1, chips, 2))
    first = -steps[far_first.index(leader)] % chips
    order = [0] * chips
    for step, chip in zip(steps, far_first):
        order[(first + step) % chips] = chip
    return order


def side_of(tile):
    return lax.rem(tile + jnp.where(tile < 2, 1, 0), 2)


def cut(left_rows, right_rows, first):
    lane = lax.broadcasted_iota(jnp.int32, (8, LANES), 1)

    def shifted(rows, at, by):
        here = pltpu.roll(rows[pl.ds(at, 8), :], by, 1)
        after = pltpu.roll(rows[pl.ds(at + 1, 8), :], by, 1)
        return jnp.where(lane < by, here, after)

    left_part = shifted(left_rows, first - 1, 3)[:LEFT_TILES]
    right_part = shifted(right_rows, first - 3, RIGHT_LEAD)[:RIGHT_TILES]
    return jnp.concatenate([left_part, right_part], 0).astype(jnp.bfloat16)


def cut_all(tiles, left_ref, right_ref, left_rows, right_rows, put):
    strip, width = left_ref.shape
    chunks = width // LANES
    per_tile = chunks // tiles
    side = side_of(lax.axis_index("cols"))
    for line in range(strip):
        for chunk in range(chunks):
            span = slice(chunk * LANES, (chunk + 1) * LANES)
            at = slice(LEAD + chunk, LEAD + chunk + 1)
            left_rows[at, :] = left_ref[line : line + 1, span].astype(jnp.float32)
            right_rows[at, :] = right_ref[line : line + 1, span].astype(jnp.float32)
        for pair in range(tiles // 2):
            tile = 2 * pair + (side if pair else 1 - side)
            put(pair, line, cut(left_rows, right_rows, LEAD + tile * per_tile))


def own_kernel(tiles, left_hbm, right_hbm, ranges_hbm, out_ref, start_ref, cap_ref, masks_ref, picks_ref, left_ref, right_ref, ranges_ref, left_rows, right_rows, sems):
    copies = [
        pltpu.make_async_copy(source, target, sems.at[i])
        for i, (source, target) in enumerate(
            [(ranges_hbm, ranges_ref), (left_hbm, left_ref), (right_hbm, right_ref)]
        )
    ]
    for copy in copies:
        copy.start()
    left_rows[...] = jnp.zeros_like(left_rows)
    right_rows[...] = jnp.zeros_like(right_rows)
    row16 = lax.broadcasted_iota(jnp.int32, (16, 2 * LANES), 0)
    owner16 = lax.broadcasted_iota(jnp.int32, (16, 2 * LANES), 1) // STEP
    window = jnp.where((row16 >= owner16) & (row16 < owner16 + 7), 1.0, 0.0)
    masks_ref[0] = window.astype(jnp.bfloat16)
    masks_ref[1] = jnp.where((row16 & 7) == owner16, 1.0, 0.0).astype(jnp.bfloat16)
    source = lax.broadcasted_iota(jnp.int32, picks_ref.shape, 0)
    owner = lax.broadcasted_iota(jnp.int32, picks_ref.shape, 1) // STEP
    picked = (source >= 10 * GROUP) & ((source & 7) == owner)
    picks_ref[...] = jnp.where(picked, 1.0, 0.0).astype(jnp.bfloat16)
    past = lax.broadcasted_iota(jnp.int32, cap_ref.shape, 0) - (
        lax.broadcasted_iota(jnp.int32, cap_ref.shape, 1) & (STEP - 1)
    )
    for copy in copies:
        copy.wait()
    tile = lax.axis_index("cols")
    start_ref[...] = jnp.full(start_ref.shape, ranges_ref[0, tile], jnp.int32)
    inside = (past >= MAXB * DB - DB * ranges_ref[1, tile]) & (past < MAXB * DB)
    cap_ref[...] = jnp.where(inside, FAR, -FAR)

    def put(pair, line, piece):
        out_ref[pair, line] = piece

    cut_all(tiles, left_ref, right_ref, left_rows, right_rows, put)


def cut_own(left, right, ranges, tiles):
    strip, width = left.shape
    rows = LEAD + width // LANES + 13
    return pl.pallas_call(
        functools.partial(own_kernel, tiles),
        out_shape=[
            jax.ShapeDtypeStruct((tiles // 2, strip, TILES, LANES), jnp.bfloat16),
            jax.ShapeDtypeStruct((8, LANES), jnp.int32),
            jax.ShapeDtypeStruct((MAXB * DB + STEP, LANES), jnp.float32),
            jax.ShapeDtypeStruct((2, 16, 2 * LANES), jnp.bfloat16),
            jax.ShapeDtypeStruct((14 * GROUP, 2 * LANES), jnp.bfloat16),
        ],
        in_specs=[HBM, HBM, HBM],
        out_specs=[VMEM] * 5,
        scratch_shapes=[
            pltpu.VMEM(left.shape, left.dtype),
            pltpu.VMEM(right.shape, right.dtype),
            pltpu.SMEM((2, tiles), jnp.int32),
            pltpu.VMEM((rows, LANES), jnp.float32),
            pltpu.VMEM((rows, LANES), jnp.float32),
            pltpu.SemaphoreType.DMA((3,)),
        ],
        compiler_params=pltpu.CompilerParams(vmem_limit_bytes=8 * 2**20),
        cost_estimate=pl.CostEstimate(flops=10**6, bytes_accessed=2**16, transcendentals=0),
    )(*[pltpu.with_memory_space_constraint(v, pltpu.HBM) for v in (left, right, ranges.T)])


def pair_kernel(bands, tiles, own_ref, left_ref, right_ref, out_ref, left_rows, right_rows):
    left_rows[...] = jnp.zeros_like(left_rows)
    right_rows[...] = jnp.zeros_like(right_rows)
    core = lax.rem(lax.axis_index("cols"), 2)
    order = chip_order(bands, tiles // 2)

    def put(pair, line, piece):
        mine = own_ref[pair, line]
        for band in range(bands):
            member = order.index(band * (tiles // 2) + pair)
            out_ref[member, core, line] = mine
            out_ref[member, 1 - core, line] = piece

    cut_all(tiles, left_ref, right_ref, left_rows, right_rows, put)


def cut_pair(own, left, right, bands, tiles):
    strip, width = left.shape
    rows = LEAD + width // LANES + 13
    return pl.pallas_call(
        functools.partial(pair_kernel, bands, tiles),
        out_shape=jax.ShapeDtypeStruct((bands * tiles // 2, 2, strip, TILES, LANES), jnp.bfloat16),
        in_specs=[VMEM, VMEM, VMEM],
        out_specs=VMEM,
        scratch_shapes=[pltpu.VMEM((rows, LANES), jnp.float32), pltpu.VMEM((rows, LANES), jnp.float32)],
        compiler_params=pltpu.CompilerParams(vmem_limit_bytes=8 * 2**20),
    )(own, left, right)


def ahead(values, by, axis):
    if by == 0:
        return values
    return pltpu.roll(values, values.shape[axis] - by, axis)


def column_sum(values):
    two = values + ahead(values, 1, 0)
    four = two + ahead(two, 2, 0)
    return (four + ahead(two, 4, 0) + ahead(values, 6, 0))[:GROUP]


def moments(shifted):
    shifted = [v.astype(jnp.float32) for v in shifted]
    total = column_sum(sum(shifted[1:], shifted[0]))
    squares = [v * v for v in shifted]
    mean = total * (1.0 / 49.0)
    spread = column_sum(sum(squares[1:], squares[0])) * (1.0 / 49.0) - mean * mean
    return total, mean, lax.rsqrt(jnp.maximum(spread, 0.01))


def parts(values):
    high = values.astype(jnp.bfloat16)
    rest = values - high.astype(jnp.float32)
    middle = rest.astype(jnp.bfloat16)
    low = (rest - middle.astype(jnp.float32)).astype(jnp.bfloat16)
    return [high, middle, low]


def sum_of(values):
    return functools.reduce(lambda a, b: a + b, values)


def fold(values):
    return functools.reduce(jnp.maximum, [values[i : i + 8] for i in range(0, values.shape[0], 8)])


def spread_out(values, lane_group):
    out = []
    for tile in range(values.shape[1] // LANES):
        here = values[:, tile * LANES : (tile + 1) * LANES]
        turned = [here] + [pltpu.roll(here, STEP * k, 1) for k in range(1, LANES // STEP)]
        for g in range(LANES // STEP):
            block = turned[0]
            for k in range(1, LANES // STEP):
                block = jnp.where(lane_group[(g + k) % (LANES // STEP)] > 0, turned[k], block)
            out.append(block)
    return out


def regroup(found):
    groups = LANES // STEP
    row = lax.broadcasted_iota(jnp.int32, (GROUP, LANES), 0)
    lane = lax.broadcasted_iota(jnp.int32, (GROUP, LANES), 1) // STEP
    halves = [found[:, h * LANES : (h + 1) * LANES] for h in range(2)]
    out = []
    for to in range(2):
        result = jnp.zeros((GROUP, LANES), jnp.float32)
        for half in range(2):
            for k in range(groups):
                turned = halves[half] if k == 0 else pltpu.roll(halves[half], STEP * k, 1)
                for up in sorted({(half - to) * groups - k, (half - to) * groups + (groups - k if k else 0)}):
                    chosen = (row // groups == half) & (row - (to * groups + lane) == up)
                    by = up % GROUP
                    result = jnp.where(chosen, pltpu.roll(turned, by, 0) if by else turned, result)
        out.append(result)
    return jnp.concatenate(out, 1)


def score_kernel(order, lines_ref, start_ref, cap_ref, masks_ref, picks_ref, out_ref, rows):
    band_rows, tile_width = out_ref.shape
    reach = tile_width + MAXB * DB
    span = MAXB * DB + STEP
    window, only = masks_ref[0], masks_ref[1]
    lane16 = lax.broadcasted_iota(jnp.int32, (16, LANES), 1) // STEP
    lane_group = [jnp.where(lane16 == p, 1.0, 0.0) for p in range(LANES // STEP)]
    lane_group = [v.astype(jnp.bfloat16) for v in lane_group]
    always = (DB + STEP, MAXB * DB)
    height = lines_ref.shape[0]
    each = height // len(order)
    rows[: 3 * TILES] = jnp.zeros((3 * TILES, LANES), jnp.float32)
    rows[(height + 3) * TILES :] = jnp.zeros((6 * TILES, LANES), jnp.float32)
    for member, chip in enumerate(order):
        for line in range(each):
            at = (3 + chip * each + line) * TILES
            rows[at : at + TILES] = lines_ref[member * each + line].astype(jnp.float32)
    start = start_ref[0, 0]
    lane = lax.broadcasted_iota(jnp.int32, (16, LANES), 1)

    def moved(pieces, by):
        turned = [pltpu.roll(v, by, 1) for v in pieces]
        ahead_by = [jnp.where(lane < by, a, b) for a, b in zip(turned, turned[1:])]
        return jnp.concatenate(ahead_by, 1)

    for group in range(band_rows // GROUP):
        first = (lax.axis_index("rows") * band_rows + group * GROUP) * TILES
        tiles = [rows[pl.ds(first + t, 16, stride=TILES), :] for t in range(TILES)]
        left = jnp.concatenate(tiles[:LEFT_TILES], 1).astype(jnp.bfloat16)
        shifted_right = [moved(tiles[LEFT_TILES:], RIGHT_LEAD - 4 - j + start) for j in range(7)]
        shifted_left = [ahead(left, j, 1)[:, :tile_width] for j in range(7)]
        blank = jnp.zeros((16, reach), jnp.bfloat16)
        near_side = jnp.transpose(jnp.concatenate([v.astype(jnp.bfloat16) for v in shifted_right] + [blank], 0))
        _, right_mean, right_scale = moments(shifted_right)
        left_total, _, left_scale = moments(shifted_left)
        high, middle, low = [p.astype(jnp.float32) for p in parts(right_mean)]
        far_side = [high, high, middle, middle, low, low, high, middle, low, jnp.zeros_like(low)]
        far_side += [p.astype(jnp.float32) for p in parts(right_scale)] + [jnp.zeros_like(low)]
        far_side = jnp.transpose(jnp.concatenate(far_side, 0).astype(jnp.bfloat16))
        right_side = jnp.concatenate([near_side, far_side], 1)
        near = [spread_out(v, lane_group) for v in shifted_left]
        high, middle, low = [p.astype(jnp.float32) for p in parts(-left_total)]
        far = [jnp.concatenate(p, 0).astype(jnp.bfloat16) for p in ((high, middle), (low, low))]
        far = [spread_out(p, lane_group) for p in far]
        scale = jnp.dot(far_side, picks_ref[...], preferred_element_type=jnp.float32)
        none = jnp.zeros((16, 2 * LANES), jnp.bfloat16)
        none32 = jnp.zeros((32, 2 * LANES), jnp.bfloat16)
        found = []
        for block in range(tile_width // STEP):
            left_side = [jnp.concatenate([v[block]] * 2, 1) * window for v in near] + [none]
            two, last = [jnp.concatenate([a[block]] * 2, 1) * only for a in far]
            left_side += [two, two, two, last, last, none32]
            reached = slice(block * STEP, block * STEP + span)
            products = jnp.dot(
                right_side[reached], jnp.concatenate(left_side, 0), preferred_element_type=jnp.float32
            )
            halves = []
            for half in range(2):
                at = slice(half * LANES, (half + 1) * LANES)
                scaled = products[:, at] * scale[reached, at]
                kept = [
                    jnp.minimum(scaled[: always[0]], cap_ref[: always[0]]),
                    scaled[always[0] : always[1]],
                    jnp.minimum(scaled[always[1] :], cap_ref[always[1] :]),
                ]
                halves.append(jnp.max(functools.reduce(jnp.maximum, [fold(v) for v in kept]), axis=0, keepdims=True))
            found.append(jnp.concatenate(halves, 1))
        best = regroup(jnp.concatenate(found, 0)) * (left_scale * (1.0 / 49.0))
        out_ref[group * GROUP : (group + 1) * GROUP, :] = jnp.maximum(best, -2.0)


def score(lines, constants, order, band_rows, tile_width):
    return pl.pallas_call(
        functools.partial(score_kernel, order),
        out_shape=jax.ShapeDtypeStruct((band_rows, tile_width), jnp.float32),
        in_specs=[VMEM] * 5,
        out_specs=VMEM,
        scratch_shapes=[pltpu.VMEM(((lines.shape[0] + 9) * TILES, LANES), jnp.float32)],
        compiler_params=pltpu.CompilerParams(vmem_limit_bytes=16 * 2**20),
    )(lines, *constants)


def on_device(left_image, right_image, ranges):
    bands, tiles = lax.axis_size("rows"), lax.axis_size("cols")
    strip, width = left_image.shape
    swap = [(i, i ^ 1) for i in range(tiles)]
    left_other = lax.ppermute(left_image, "cols", swap)
    right_other = lax.ppermute(right_image, "cols", swap)
    own, *constants = cut_own(left_image, right_image, ranges, tiles)
    pieces = cut_pair(own, left_other, right_other, bands, tiles)
    order = chip_order(bands, tiles // 2)
    groups = [[2 * chip + (side if chip % (tiles // 2) else 1 - side) for chip in order] for side in range(2)]
    lines = lax.all_to_all(
        pieces, ("rows", "cols"), split_axis=0, concat_axis=0, tiled=True, axis_index_groups=groups
    )
    lines = lines.reshape(bands * tiles * strip, TILES, LANES)
    return score(lines, constants, order, strip * tiles, width // tiles)


def solution(mesh):
    return jax.shard_map(
        on_device,
        mesh=mesh,
        in_specs=(P(("rows", "cols"), None), P(("rows", "cols"), None), P()),
        out_specs=P("rows", "cols"),
        check_vma=False,
    )
```

```python
import functools

import jax
import jax.numpy as jnp
from jax import lax
from jax.experimental import pallas as pl
from jax.experimental.pallas import tpu as pltpu
from jax.sharding import PartitionSpec as P

DB = 128
MAXB = 2
LANES = 128
LEFT_TILES = 3
RIGHT_TILES = 5
TILES = LEFT_TILES + RIGHT_TILES
LEAD = 3
RIGHT_LEAD = 67
GROUP = 8
STEP = 32
FAR = 3.0e37
VMEM = pl.BlockSpec(memory_space=pltpu.VMEM)
HBM = pl.BlockSpec(memory_space=pltpu.HBM)


def chip_order(bands, pairs):
    chips = bands * pairs
    leader = chips - 2
    away = {chip: bin(chip // pairs).count("1") + chip % pairs for chip in range(1, chips)}
    far_first = sorted(away, key=lambda chip: (-away[chip], chip != leader, chip))
    steps = list(range(2, chips, 2)) + list(range(1, chips, 2))
    first = -steps[far_first.index(leader)] % chips
    order = [0] * chips
    for step, chip in zip(steps, far_first):
        order[(first + step) % chips] = chip
    return order


def side_of(tile):
    return lax.rem(tile + jnp.where(tile < 2, 1, 0), 2)


def cut(left_rows, right_rows, first):
    lane = lax.broadcasted_iota(jnp.int32, (8, LANES), 1)

    def shifted(rows, at, by):
        here = pltpu.roll(rows[pl.ds(at, 8), :], by, 1)
        after = pltpu.roll(rows[pl.ds(at + 1, 8), :], by, 1)
        return jnp.where(lane < by, here, after)

    left_part = shifted(left_rows, first - 1, 3)[:LEFT_TILES]
    right_part = shifted(right_rows, first - 3, RIGHT_LEAD)[:RIGHT_TILES]
    return jnp.concatenate([left_part, right_part], 0).astype(jnp.bfloat16)


def cut_all(tiles, left_ref, right_ref, left_rows, right_rows, put):
    strip, width = left_ref.shape
    chunks = width // LANES
    per_tile = chunks // tiles
    side = side_of(lax.axis_index("cols"))
    for line in range(strip):
        for chunk in range(chunks):
            span = slice(chunk * LANES, (chunk + 1) * LANES)
            at = slice(LEAD + chunk, LEAD + chunk + 1)
            left_rows[at, :] = left_ref[line : line + 1, span].astype(jnp.float32)
            right_rows[at, :] = right_ref[line : line + 1, span].astype(jnp.float32)
        for pair in range(tiles // 2):
            tile = 2 * pair + (side if pair else 1 - side)
            put(pair, line, cut(left_rows, right_rows, LEAD + tile * per_tile))


def own_kernel(tiles, left_hbm, right_hbm, ranges_hbm, out_ref, start_ref, cap_ref, masks_ref, picks_ref, left_ref, right_ref, ranges_ref, left_rows, right_rows, sems):
    copies = [
        pltpu.make_async_copy(source, target, sems.at[i])
        for i, (source, target) in enumerate(
            [(ranges_hbm, ranges_ref), (left_hbm, left_ref), (right_hbm, right_ref)]
        )
    ]
    for copy in copies:
        copy.start()
    left_rows[...] = jnp.zeros_like(left_rows)
    right_rows[...] = jnp.zeros_like(right_rows)
    row16 = lax.broadcasted_iota(jnp.int32, (16, 2 * LANES), 0)
    owner16 = lax.broadcasted_iota(jnp.int32, (16, 2 * LANES), 1) // STEP
    window = jnp.where((row16 >= owner16) & (row16 < owner16 + 7), 1.0, 0.0)
    masks_ref[0] = window.astype(jnp.bfloat16)
    masks_ref[1] = jnp.where((row16 & 7) == owner16, 1.0, 0.0).astype(jnp.bfloat16)
    source = lax.broadcasted_iota(jnp.int32, picks_ref.shape, 0)
    owner = lax.broadcasted_iota(jnp.int32, picks_ref.shape, 1) // STEP
    picked = (source >= 10 * GROUP) & ((source & 7) == owner)
    picks_ref[...] = jnp.where(picked, 1.0, 0.0).astype(jnp.bfloat16)
    past = lax.broadcasted_iota(jnp.int32, cap_ref.shape, 0) - (
        lax.broadcasted_iota(jnp.int32, cap_ref.shape, 1) & (STEP - 1)
    )
    for copy in copies:
        copy.wait()
    tile = lax.axis_index("cols")
    start_ref[...] = jnp.full(start_ref.shape, ranges_ref[0, tile], jnp.int32)
    inside = (past >= MAXB * DB - DB * ranges_ref[1, tile]) & (past < MAXB * DB)
    cap_ref[...] = jnp.where(inside, FAR, -FAR)

    def put(pair, line, piece):
        out_ref[pair, line] = piece

    cut_all(tiles, left_ref, right_ref, left_rows, right_rows, put)


def cut_own(left, right, ranges, tiles):
    strip, width = left.shape
    rows = LEAD + width // LANES + 13
    return pl.pallas_call(
        functools.partial(own_kernel, tiles),
        out_shape=[
            jax.ShapeDtypeStruct((tiles // 2, strip, TILES, LANES), jnp.bfloat16),
            jax.ShapeDtypeStruct((8, LANES), jnp.int32),
            jax.ShapeDtypeStruct((MAXB * DB + STEP, LANES), jnp.float32),
            jax.ShapeDtypeStruct((2, 16, 2 * LANES), jnp.bfloat16),
            jax.ShapeDtypeStruct((14 * GROUP, 2 * LANES), jnp.bfloat16),
        ],
        in_specs=[HBM, HBM, HBM],
        out_specs=[VMEM] * 5,
        scratch_shapes=[
            pltpu.VMEM(left.shape, left.dtype),
            pltpu.VMEM(right.shape, right.dtype),
            pltpu.SMEM((2, tiles), jnp.int32),
            pltpu.VMEM((rows, LANES), jnp.float32),
            pltpu.VMEM((rows, LANES), jnp.float32),
            pltpu.SemaphoreType.DMA((3,)),
        ],
        compiler_params=pltpu.CompilerParams(vmem_limit_bytes=8 * 2**20),
        cost_estimate=pl.CostEstimate(flops=10**6, bytes_accessed=2**16, transcendentals=0),
    )(*[pltpu.with_memory_space_constraint(v, pltpu.HBM) for v in (left, right, ranges.T)])


def pair_kernel(bands, tiles, own_ref, left_ref, right_ref, out_ref, left_rows, right_rows):
    left_rows[...] = jnp.zeros_like(left_rows)
    right_rows[...] = jnp.zeros_like(right_rows)
    core = lax.rem(lax.axis_index("cols"), 2)
    order = chip_order(bands, tiles // 2)

    def put(pair, line, piece):
        mine = own_ref[pair, line]
        for band in range(bands):
            member = order.index(band * (tiles // 2) + pair)
            out_ref[member, core, line] = mine
            out_ref[member, 1 - core, line] = piece

    cut_all(tiles, left_ref, right_ref, left_rows, right_rows, put)


def cut_pair(own, left, right, bands, tiles):
    strip, width = left.shape
    rows = LEAD + width // LANES + 13
    return pl.pallas_call(
        functools.partial(pair_kernel, bands, tiles),
        out_shape=jax.ShapeDtypeStruct((bands * tiles // 2, 2, strip, TILES, LANES), jnp.bfloat16),
        in_specs=[VMEM, VMEM, VMEM],
        out_specs=VMEM,
        scratch_shapes=[pltpu.VMEM((rows, LANES), jnp.float32), pltpu.VMEM((rows, LANES), jnp.float32)],
        compiler_params=pltpu.CompilerParams(vmem_limit_bytes=8 * 2**20),
    )(own, left, right)


def ahead(values, by, axis):
    if by == 0:
        return values
    return pltpu.roll(values, values.shape[axis] - by, axis)


def column_sum(values):
    two = values + ahead(values, 1, 0)
    four = two + ahead(two, 2, 0)
    return (four + ahead(two, 4, 0) + ahead(values, 6, 0))[:GROUP]


def moments(shifted):
    shifted = [v.astype(jnp.float32) for v in shifted]
    total = column_sum(sum(shifted[1:], shifted[0]))
    squares = [v * v for v in shifted]
    mean = total * (1.0 / 49.0)
    spread = column_sum(sum(squares[1:], squares[0])) * (1.0 / 49.0) - mean * mean
    return total, mean, lax.rsqrt(jnp.maximum(spread, 0.01))


def parts(values):
    high = values.astype(jnp.bfloat16)
    rest = values - high.astype(jnp.float32)
    middle = rest.astype(jnp.bfloat16)
    low = (rest - middle.astype(jnp.float32)).astype(jnp.bfloat16)
    return [high, middle, low]


def sum_of(values):
    return functools.reduce(lambda a, b: a + b, values)


def fold(values):
    return functools.reduce(jnp.maximum, [values[i : i + 8] for i in range(0, values.shape[0], 8)])


def spread_out(values, lane_group):
    out = []
    for tile in range(values.shape[1] // LANES):
        here = values[:, tile * LANES : (tile + 1) * LANES]
        turned = [here] + [pltpu.roll(here, STEP * k, 1) for k in range(1, LANES // STEP)]
        for g in range(LANES // STEP):
            block = turned[0]
            for k in range(1, LANES // STEP):
                block = jnp.where(lane_group[(g + k) % (LANES // STEP)] > 0, turned[k], block)
            out.append(block)
    return out


def regroup(found):
    groups = LANES // STEP
    row = lax.broadcasted_iota(jnp.int32, (GROUP, LANES), 0)
    lane = lax.broadcasted_iota(jnp.int32, (GROUP, LANES), 1) // STEP
    halves = [found[:, h * LANES : (h + 1) * LANES] for h in range(2)]
    out = []
    for to in range(2):
        result = jnp.zeros((GROUP, LANES), jnp.float32)
        for half in range(2):
            for k in range(groups):
                turned = halves[half] if k == 0 else pltpu.roll(halves[half], STEP * k, 1)
                for up in sorted({(half - to) * groups - k, (half - to) * groups + (groups - k if k else 0)}):
                    chosen = (row // groups == half) & (row - (to * groups + lane) == up)
                    by = up % GROUP
                    result = jnp.where(chosen, pltpu.roll(turned, by, 0) if by else turned, result)
        out.append(result)
    return jnp.concatenate(out, 1)


def score_kernel(order, lines_ref, start_ref, cap_ref, masks_ref, picks_ref, out_ref, rows):
    band_rows, tile_width = out_ref.shape
    reach = tile_width + MAXB * DB
    span = MAXB * DB + STEP
    start = start_ref[0, 0]
    window, only = masks_ref[0], masks_ref[1]
    lane16 = lax.broadcasted_iota(jnp.int32, (16, LANES), 1) // STEP
    lane_group = [jnp.where(lane16 == p, 1.0, 0.0) for p in range(LANES // STEP)]
    lane_group = [v.astype(jnp.bfloat16) for v in lane_group]
    always = (DB + STEP, MAXB * DB)
    height = lines_ref.shape[0]
    each = height // len(order)
    rows[: 3 * TILES] = jnp.zeros((3 * TILES, LANES), jnp.float32)
    rows[(height + 3) * TILES :] = jnp.zeros((6 * TILES, LANES), jnp.float32)
    for member, chip in enumerate(order):
        for line in range(each):
            at = (3 + chip * each + line) * TILES
            rows[at : at + TILES] = lines_ref[member * each + line].astype(jnp.float32)
    lane = lax.broadcasted_iota(jnp.int32, (16, LANES), 1)

    def moved(pieces, by):
        turned = [pltpu.roll(v, by, 1) for v in pieces]
        ahead_by = [jnp.where(lane < by, a, b) for a, b in zip(turned, turned[1:])]
        return jnp.concatenate(ahead_by, 1)

    for group in range(band_rows // GROUP):
        first = (lax.axis_index("rows") * band_rows + group * GROUP) * TILES
        tiles = [rows[pl.ds(first + t, 16, stride=TILES), :] for t in range(TILES)]
        left = jnp.concatenate(tiles[:LEFT_TILES], 1).astype(jnp.bfloat16)
        shifted_right = [moved(tiles[LEFT_TILES:], RIGHT_LEAD - 4 - j + start) for j in range(7)]
        shifted_left = [ahead(left, j, 1)[:, :tile_width] for j in range(7)]
        blank = jnp.zeros((16, reach), jnp.bfloat16)
        near_side = jnp.transpose(jnp.concatenate([v.astype(jnp.bfloat16) for v in shifted_right] + [blank], 0))
        _, right_mean, right_scale = moments(shifted_right)
        left_total, _, left_scale = moments(shifted_left)
        high, middle, low = [p.astype(jnp.float32) for p in parts(right_mean)]
        far_side = [high, high, middle, middle, low, low, high, middle, low, jnp.zeros_like(low)]
        far_side += [p.astype(jnp.float32) for p in parts(right_scale)] + [jnp.zeros_like(low)]
        far_side = jnp.transpose(jnp.concatenate(far_side, 0).astype(jnp.bfloat16))
        right_side = jnp.concatenate([near_side, far_side], 1)
        near = [spread_out(v, lane_group) for v in shifted_left]
        high, middle, low = [p.astype(jnp.float32) for p in parts(-left_total)]
        far = [jnp.concatenate(p, 0).astype(jnp.bfloat16) for p in ((high, middle), (low, low))]
        far = [spread_out(p, lane_group) for p in far]
        scale = jnp.dot(far_side, picks_ref[...], preferred_element_type=jnp.float32)
        none = jnp.zeros((16, 2 * LANES), jnp.bfloat16)
        none32 = jnp.zeros((32, 2 * LANES), jnp.bfloat16)
        found = []
        for block in range(tile_width // STEP):
            left_side = [jnp.concatenate([v[block]] * 2, 1) * window for v in near] + [none]
            two, last = [jnp.concatenate([a[block]] * 2, 1) * only for a in far]
            left_side += [two, two, two, last, last, none32]
            reached = slice(block * STEP, block * STEP + span)
            products = jnp.dot(
                right_side[reached], jnp.concatenate(left_side, 0), preferred_element_type=jnp.float32
            )
            halves = []
            for half in range(2):
                at = slice(half * LANES, (half + 1) * LANES)
                scaled = products[:, at] * scale[reached, at]
                kept = [
                    jnp.minimum(scaled[: always[0]], cap_ref[: always[0]]),
                    scaled[always[0] : always[1]],
                    jnp.minimum(scaled[always[1] :], cap_ref[always[1] :]),
                ]
                halves.append(jnp.max(functools.reduce(jnp.maximum, [fold(v) for v in kept]), axis=0, keepdims=True))
            found.append(jnp.concatenate(halves, 1))
        best = regroup(jnp.concatenate(found, 0)) * (left_scale * (1.0 / 49.0))
        out_ref[group * GROUP : (group + 1) * GROUP, :] = jnp.maximum(best, -2.0)


def score(lines, constants, order, band_rows, tile_width):
    return pl.pallas_call(
        functools.partial(score_kernel, order),
        out_shape=jax.ShapeDtypeStruct((band_rows, tile_width), jnp.float32),
        in_specs=[VMEM] * 5,
        out_specs=VMEM,
        scratch_shapes=[pltpu.VMEM(((lines.shape[0] + 9) * TILES, LANES), jnp.float32)],
        compiler_params=pltpu.CompilerParams(vmem_limit_bytes=16 * 2**20),
    )(lines, *constants)


def on_device(left_image, right_image, ranges):
    bands, tiles = lax.axis_size("rows"), lax.axis_size("cols")
    strip, width = left_image.shape
    swap = [(i, i ^ 1) for i in range(tiles)]
    left_other = lax.ppermute(left_image, "cols", swap)
    right_other = lax.ppermute(right_image, "cols", swap)
    own, *constants = cut_own(left_image, right_image, ranges, tiles)
    pieces = cut_pair(own, left_other, right_other, bands, tiles)
    order = chip_order(bands, tiles // 2)
    groups = [[2 * chip + (side if chip % (tiles // 2) else 1 - side) for chip in order] for side in range(2)]
    lines = lax.all_to_all(
        pieces, ("rows", "cols"), split_axis=0, concat_axis=0, tiled=True, axis_index_groups=groups
    )
    lines = lines.reshape(bands * tiles * strip, TILES, LANES)
    return score(lines, constants, order, strip * tiles, width // tiles)


def solution(mesh):
    return jax.shard_map(
        on_device,
        mesh=mesh,
        in_specs=(P(("rows", "cols"), None), P(("rows", "cols"), None), P()),
        out_specs=P("rows", "cols"),
        check_vma=False,
    )
```

```python
import functools

import jax
import jax.numpy as jnp
from jax import lax
from jax.experimental import pallas as pl
from jax.experimental.pallas import tpu as pltpu
from jax.sharding import PartitionSpec as P

DB = 128
MAXB = 2
LANES = 128
LEFT_TILES = 3
RIGHT_TILES = 5
TILES = LEFT_TILES + RIGHT_TILES
LEAD = 3
RIGHT_LEAD = 67
GROUP = 8
STEP = 32
FAR = 3.0e37
VMEM = pl.BlockSpec(memory_space=pltpu.VMEM)
HBM = pl.BlockSpec(memory_space=pltpu.HBM)


def chip_order(bands, pairs):
    chips = bands * pairs
    leader = chips - 2
    away = {chip: bin(chip // pairs).count("1") + chip % pairs for chip in range(1, chips)}
    far_first = sorted(away, key=lambda chip: (-away[chip], chip != leader, chip))
    steps = list(range(2, chips, 2)) + list(range(1, chips, 2))
    first = -steps[far_first.index(leader)] % chips
    order = [0] * chips
    for step, chip in zip(steps, far_first):
        order[(first + step) % chips] = chip
    return order


def side_of(tile):
    return lax.rem(tile + jnp.where(tile < 2, 1, 0), 2)


def cut(left_rows, right_rows, first):
    lane = lax.broadcasted_iota(jnp.int32, (8, LANES), 1)

    def shifted(rows, at, by):
        here = pltpu.roll(rows[pl.ds(at, 8), :], by, 1)
        after = pltpu.roll(rows[pl.ds(at + 1, 8), :], by, 1)
        return jnp.where(lane < by, here, after)

    left_part = shifted(left_rows, first - 1, 3)[:LEFT_TILES]
    right_part = shifted(right_rows, first - 3, RIGHT_LEAD)[:RIGHT_TILES]
    return jnp.concatenate([left_part, right_part], 0).astype(jnp.bfloat16)


def cut_all(tiles, left_ref, right_ref, left_rows, right_rows, put):
    strip, width = left_ref.shape
    chunks = width // LANES
    per_tile = chunks // tiles
    side = side_of(lax.axis_index("cols"))
    for line in range(strip):
        for chunk in range(chunks):
            span = slice(chunk * LANES, (chunk + 1) * LANES)
            at = slice(LEAD + chunk, LEAD + chunk + 1)
            left_rows[at, :] = left_ref[line : line + 1, span].astype(jnp.float32)
            right_rows[at, :] = right_ref[line : line + 1, span].astype(jnp.float32)
        for pair in range(tiles // 2):
            tile = 2 * pair + (side if pair else 1 - side)
            put(pair, line, cut(left_rows, right_rows, LEAD + tile * per_tile))


def own_kernel(tiles, left_hbm, right_hbm, ranges_hbm, out_ref, start_ref, cap_ref, masks_ref, picks_ref, left_ref, right_ref, ranges_ref, left_rows, right_rows, sems):
    copies = [
        pltpu.make_async_copy(source, target, sems.at[i])
        for i, (source, target) in enumerate(
            [(ranges_hbm, ranges_ref), (left_hbm, left_ref), (right_hbm, right_ref)]
        )
    ]
    for copy in copies:
        copy.start()
    left_rows[...] = jnp.zeros_like(left_rows)
    right_rows[...] = jnp.zeros_like(right_rows)
    row16 = lax.broadcasted_iota(jnp.int32, (16, 2 * LANES), 0)
    owner16 = lax.broadcasted_iota(jnp.int32, (16, 2 * LANES), 1) // STEP
    window = jnp.where((row16 >= owner16) & (row16 < owner16 + 7), 1.0, 0.0)
    masks_ref[0] = window.astype(jnp.bfloat16)
    masks_ref[1] = jnp.where((row16 & 7) == owner16, 1.0, 0.0).astype(jnp.bfloat16)
    source = lax.broadcasted_iota(jnp.int32, picks_ref.shape, 0)
    owner = lax.broadcasted_iota(jnp.int32, picks_ref.shape, 1) // STEP
    picked = (source >= 10 * GROUP) & ((source & 7) == owner)
    picks_ref[...] = jnp.where(picked, 1.0, 0.0).astype(jnp.bfloat16)
    past = lax.broadcasted_iota(jnp.int32, cap_ref.shape, 0) - (
        lax.broadcasted_iota(jnp.int32, cap_ref.shape, 1) & (STEP - 1)
    )
    for copy in copies:
        copy.wait()
    tile = lax.axis_index("cols")
    start_ref[...] = jnp.full(start_ref.shape, ranges_ref[0, tile], jnp.int32)
    inside = (past >= MAXB * DB - DB * ranges_ref[1, tile]) & (past < MAXB * DB)
    cap_ref[...] = jnp.where(inside, FAR, -FAR)

    def put(pair, line, piece):
        out_ref[pair, line] = piece

    cut_all(tiles, left_ref, right_ref, left_rows, right_rows, put)


def cut_own(left, right, ranges, tiles):
    strip, width = left.shape
    rows = LEAD + width // LANES + 13
    return pl.pallas_call(
        functools.partial(own_kernel, tiles),
        out_shape=[
            jax.ShapeDtypeStruct((tiles // 2, strip, TILES, LANES), jnp.bfloat16),
            jax.ShapeDtypeStruct((8, LANES), jnp.int32),
            jax.ShapeDtypeStruct((MAXB * DB + STEP, LANES), jnp.float32),
            jax.ShapeDtypeStruct((2, 16, 2 * LANES), jnp.bfloat16),
            jax.ShapeDtypeStruct((14 * GROUP, 2 * LANES), jnp.bfloat16),
        ],
        in_specs=[HBM, HBM, HBM],
        out_specs=[VMEM] * 5,
        scratch_shapes=[
            pltpu.VMEM(left.shape, left.dtype),
            pltpu.VMEM(right.shape, right.dtype),
            pltpu.SMEM((2, tiles), jnp.int32),
            pltpu.VMEM((rows, LANES), jnp.float32),
            pltpu.VMEM((rows, LANES), jnp.float32),
            pltpu.SemaphoreType.DMA((3,)),
        ],
        compiler_params=pltpu.CompilerParams(vmem_limit_bytes=8 * 2**20),
        cost_estimate=pl.CostEstimate(flops=10**6, bytes_accessed=2**16, transcendentals=0),
    )(*[pltpu.with_memory_space_constraint(v, pltpu.HBM) for v in (left, right, ranges.T)])


def pair_kernel(bands, tiles, own_ref, left_ref, right_ref, out_ref, left_rows, right_rows):
    left_rows[...] = jnp.zeros_like(left_rows)
    right_rows[...] = jnp.zeros_like(right_rows)
    core = lax.rem(lax.axis_index("cols"), 2)
    order = chip_order(bands, tiles // 2)

    def put(pair, line, piece):
        mine = own_ref[pair, line]
        lines = [jnp.where(core == 0, mine, piece), jnp.where(core == 0, piece, mine)]
        for band in range(bands):
            member = order.index(band * (tiles // 2) + pair)
            for row in range(2):
                out_ref[member, row, line] = lines[row]

    cut_all(tiles, left_ref, right_ref, left_rows, right_rows, put)


def cut_pair(own, left, right, bands, tiles):
    strip, width = left.shape
    rows = LEAD + width // LANES + 13
    return pl.pallas_call(
        functools.partial(pair_kernel, bands, tiles),
        out_shape=jax.ShapeDtypeStruct((bands * tiles // 2, 2, strip, TILES, LANES), jnp.bfloat16),
        in_specs=[VMEM, VMEM, VMEM],
        out_specs=VMEM,
        scratch_shapes=[pltpu.VMEM((rows, LANES), jnp.float32), pltpu.VMEM((rows, LANES), jnp.float32)],
        compiler_params=pltpu.CompilerParams(vmem_limit_bytes=8 * 2**20),
    )(own, left, right)


def ahead(values, by, axis):
    if by == 0:
        return values
    return pltpu.roll(values, values.shape[axis] - by, axis)


def column_sum(values):
    two = values + ahead(values, 1, 0)
    four = two + ahead(two, 2, 0)
    return (four + ahead(two, 4, 0) + ahead(values, 6, 0))[:GROUP]


def moments(shifted):
    shifted = [v.astype(jnp.float32) for v in shifted]
    total = column_sum(sum(shifted[1:], shifted[0]))
    squares = [v * v for v in shifted]
    mean = total * (1.0 / 49.0)
    spread = column_sum(sum(squares[1:], squares[0])) * (1.0 / 49.0) - mean * mean
    return total, mean, lax.rsqrt(jnp.maximum(spread, 0.01))


def parts(values):
    high = values.astype(jnp.bfloat16)
    rest = values - high.astype(jnp.float32)
    middle = rest.astype(jnp.bfloat16)
    low = (rest - middle.astype(jnp.float32)).astype(jnp.bfloat16)
    return [high, middle, low]


def sum_of(values):
    return functools.reduce(lambda a, b: a + b, values)


def fold(values):
    return functools.reduce(jnp.maximum, [values[i : i + 8] for i in range(0, values.shape[0], 8)])


def spread_out(values, lane_group):
    out = []
    for tile in range(values.shape[1] // LANES):
        here = values[:, tile * LANES : (tile + 1) * LANES]
        turned = [here] + [pltpu.roll(here, STEP * k, 1) for k in range(1, LANES // STEP)]
        for g in range(LANES // STEP):
            block = turned[0]
            for k in range(1, LANES // STEP):
                block = jnp.where(lane_group[(g + k) % (LANES // STEP)] > 0, turned[k], block)
            out.append(block)
    return out


def regroup(found):
    groups = LANES // STEP
    row = lax.broadcasted_iota(jnp.int32, (GROUP, LANES), 0)
    lane = lax.broadcasted_iota(jnp.int32, (GROUP, LANES), 1) // STEP
    halves = [found[:, h * LANES : (h + 1) * LANES] for h in range(2)]
    out = []
    for to in range(2):
        result = jnp.zeros((GROUP, LANES), jnp.float32)
        for half in range(2):
            for k in range(groups):
                turned = halves[half] if k == 0 else pltpu.roll(halves[half], STEP * k, 1)
                for up in sorted({(half - to) * groups - k, (half - to) * groups + (groups - k if k else 0)}):
                    chosen = (row // groups == half) & (row - (to * groups + lane) == up)
                    by = up % GROUP
                    result = jnp.where(chosen, pltpu.roll(turned, by, 0) if by else turned, result)
        out.append(result)
    return jnp.concatenate(out, 1)


def score_kernel(order, lines_ref, start_ref, cap_ref, masks_ref, picks_ref, out_ref, rows):
    band_rows, tile_width = out_ref.shape
    reach = tile_width + MAXB * DB
    span = MAXB * DB + STEP
    window, only = masks_ref[0], masks_ref[1]
    lane16 = lax.broadcasted_iota(jnp.int32, (16, LANES), 1) // STEP
    lane_group = [jnp.where(lane16 == p, 1.0, 0.0) for p in range(LANES // STEP)]
    lane_group = [v.astype(jnp.bfloat16) for v in lane_group]
    always = (DB + STEP, MAXB * DB)
    height = lines_ref.shape[0]
    each = height // len(order)
    rows[: 3 * TILES] = jnp.zeros((3 * TILES, LANES), jnp.float32)
    rows[(height + 3) * TILES :] = jnp.zeros((6 * TILES, LANES), jnp.float32)
    for member, chip in enumerate(order):
        for line in range(each):
            at = (3 + chip * each + line) * TILES
            rows[at : at + TILES] = lines_ref[member * each + line].astype(jnp.float32)
    start = start_ref[0, 0]
    lane = lax.broadcasted_iota(jnp.int32, (16, LANES), 1)

    def moved(pieces, by):
        turned = [pltpu.roll(v, by, 1) for v in pieces]
        ahead_by = [jnp.where(lane < by, a, b) for a, b in zip(turned, turned[1:])]
        return jnp.concatenate(ahead_by, 1)

    for group in range(band_rows // GROUP):
        first = (lax.axis_index("rows") * band_rows + group * GROUP) * TILES
        tiles = [rows[pl.ds(first + t, 16, stride=TILES), :] for t in range(TILES)]
        left = jnp.concatenate(tiles[:LEFT_TILES], 1).astype(jnp.bfloat16)
        shifted_right = [moved(tiles[LEFT_TILES:], RIGHT_LEAD - 4 - j + start) for j in range(7)]
        shifted_left = [ahead(left, j, 1)[:, :tile_width] for j in range(7)]
        blank = jnp.zeros((16, reach), jnp.bfloat16)
        near_side = jnp.transpose(jnp.concatenate([v.astype(jnp.bfloat16) for v in shifted_right] + [blank], 0))
        _, right_mean, right_scale = moments(shifted_right)
        left_total, _, left_scale = moments(shifted_left)
        high, middle, low = [p.astype(jnp.float32) for p in parts(right_mean)]
        far_side = [high, high, middle, middle, low, low, high, middle, low, jnp.zeros_like(low)]
        far_side += [p.astype(jnp.float32) for p in parts(right_scale)] + [jnp.zeros_like(low)]
        far_side = jnp.transpose(jnp.concatenate(far_side, 0).astype(jnp.bfloat16))
        right_side = jnp.concatenate([near_side, far_side], 1)
        near = [spread_out(v, lane_group) for v in shifted_left]
        high, middle, low = [p.astype(jnp.float32) for p in parts(-left_total)]
        far = [jnp.concatenate(p, 0).astype(jnp.bfloat16) for p in ((high, middle), (low, low))]
        far = [spread_out(p, lane_group) for p in far]
        scale = jnp.dot(far_side, picks_ref[...], preferred_element_type=jnp.float32)
        none = jnp.zeros((16, 2 * LANES), jnp.bfloat16)
        none32 = jnp.zeros((32, 2 * LANES), jnp.bfloat16)
        found = []
        for block in range(tile_width // STEP):
            left_side = [jnp.concatenate([v[block]] * 2, 1) * window for v in near] + [none]
            two, last = [jnp.concatenate([a[block]] * 2, 1) * only for a in far]
            left_side += [two, two, two, last, last, none32]
            reached = slice(block * STEP, block * STEP + span)
            products = jnp.dot(
                right_side[reached], jnp.concatenate(left_side, 0), preferred_element_type=jnp.float32
            )
            halves = []
            for half in range(2):
                at = slice(half * LANES, (half + 1) * LANES)
                scaled = products[:, at] * scale[reached, at]
                kept = [
                    jnp.minimum(scaled[: always[0]], cap_ref[: always[0]]),
                    scaled[always[0] : always[1]],
                    jnp.minimum(scaled[always[1] :], cap_ref[always[1] :]),
                ]
                halves.append(jnp.max(functools.reduce(jnp.maximum, [fold(v) for v in kept]), axis=0, keepdims=True))
            found.append(jnp.concatenate(halves, 1))
        best = regroup(jnp.concatenate(found, 0)) * (left_scale * (1.0 / 49.0))
        out_ref[group * GROUP : (group + 1) * GROUP, :] = jnp.maximum(best, -2.0)


def score(lines, constants, order, band_rows, tile_width):
    return pl.pallas_call(
        functools.partial(score_kernel, order),
        out_shape=jax.ShapeDtypeStruct((band_rows, tile_width), jnp.float32),
        in_specs=[VMEM] * 5,
        out_specs=VMEM,
        scratch_shapes=[pltpu.VMEM(((lines.shape[0] + 9) * TILES, LANES), jnp.float32)],
        compiler_params=pltpu.CompilerParams(vmem_limit_bytes=16 * 2**20),
    )(lines, *constants)


def on_device(left_image, right_image, ranges):
    bands, tiles = lax.axis_size("rows"), lax.axis_size("cols")
    strip, width = left_image.shape
    swap = [(i, i ^ 1) for i in range(tiles)]
    left_other = lax.ppermute(left_image, "cols", swap)
    right_other = lax.ppermute(right_image, "cols", swap)
    own, *constants = cut_own(left_image, right_image, ranges, tiles)
    pieces = cut_pair(own, left_other, right_other, bands, tiles)
    order = chip_order(bands, tiles // 2)
    groups = [[2 * chip + (side if chip % (tiles // 2) else 1 - side) for chip in order] for side in range(2)]
    lines = lax.all_to_all(
        pieces, ("rows", "cols"), split_axis=0, concat_axis=0, tiled=True, axis_index_groups=groups
    )
    lines = lines.reshape(bands * tiles * strip, TILES, LANES)
    return score(lines, constants, order, strip * tiles, width // tiles)


def solution(mesh):
    return jax.shard_map(
        on_device,
        mesh=mesh,
        in_specs=(P(("rows", "cols"), None), P(("rows", "cols"), None), P()),
        out_specs=P("rows", "cols"),
        check_vma=False,
    )
```

```python
import functools

import jax
import jax.numpy as jnp
from jax import lax
from jax.experimental import pallas as pl
from jax.experimental.pallas import tpu as pltpu
from jax.sharding import PartitionSpec as P

DB = 128
MAXB = 2
LANES = 128
LEFT_TILES = 3
RIGHT_TILES = 5
TILES = LEFT_TILES + RIGHT_TILES
LEAD = 3
RIGHT_LEAD = 67
GROUP = 8
STEP = 32
FAR = 3.0e37
VMEM = pl.BlockSpec(memory_space=pltpu.VMEM)
HBM = pl.BlockSpec(memory_space=pltpu.HBM)


def chip_order(bands, pairs):
    chips = bands * pairs
    leader = chips - 2
    away = {chip: bin(chip // pairs).count("1") + chip % pairs for chip in range(1, chips)}
    far_first = sorted(away, key=lambda chip: (-away[chip], chip != leader, chip))
    steps = list(range(2, chips, 2)) + list(range(1, chips, 2))
    first = -steps[far_first.index(leader)] % chips
    order = [0] * chips
    for step, chip in zip(steps, far_first):
        order[(first + step) % chips] = chip
    return order


def side_of(tile):
    return lax.rem(tile + jnp.where(tile < 2, 1, 0), 2)


def cut(left_rows, right_rows, first):
    lane = lax.broadcasted_iota(jnp.int32, (8, LANES), 1)

    def shifted(rows, at, by):
        here = pltpu.roll(rows[pl.ds(at, 8), :], by, 1)
        after = pltpu.roll(rows[pl.ds(at + 1, 8), :], by, 1)
        return jnp.where(lane < by, here, after)

    left_part = shifted(left_rows, first - 1, 3)[:LEFT_TILES]
    right_part = shifted(right_rows, first - 3, RIGHT_LEAD)[:RIGHT_TILES]
    return jnp.concatenate([left_part, right_part], 0).astype(jnp.bfloat16)


def cut_all(tiles, left_ref, right_ref, left_rows, right_rows, put):
    strip, width = left_ref.shape
    chunks = width // LANES
    per_tile = chunks // tiles
    side = side_of(lax.axis_index("cols"))
    for line in range(strip):
        for chunk in range(chunks):
            span = slice(chunk * LANES, (chunk + 1) * LANES)
            at = slice(LEAD + chunk, LEAD + chunk + 1)
            left_rows[at, :] = left_ref[line : line + 1, span].astype(jnp.float32)
            right_rows[at, :] = right_ref[line : line + 1, span].astype(jnp.float32)
        for pair in range(tiles // 2):
            tile = 2 * pair + (side if pair else 1 - side)
            put(pair, line, cut(left_rows, right_rows, LEAD + tile * per_tile))


def own_kernel(tiles, left_hbm, right_hbm, ranges_hbm, out_ref, start_ref, cap_ref, masks_ref, picks_ref, left_ref, right_ref, ranges_ref, left_rows, right_rows, sems):
    copies = [
        pltpu.make_async_copy(source, target, sems.at[i])
        for i, (source, target) in enumerate(
            [(ranges_hbm, ranges_ref), (left_hbm, left_ref), (right_hbm, right_ref)]
        )
    ]
    for copy in copies:
        copy.start()
    left_rows[...] = jnp.zeros_like(left_rows)
    right_rows[...] = jnp.zeros_like(right_rows)
    row16 = lax.broadcasted_iota(jnp.int32, (16, 2 * LANES), 0)
    owner16 = lax.broadcasted_iota(jnp.int32, (16, 2 * LANES), 1) // STEP
    window = jnp.where((row16 >= owner16) & (row16 < owner16 + 7), 1.0, 0.0)
    masks_ref[0] = window.astype(jnp.bfloat16)
    masks_ref[1] = jnp.where((row16 & 7) == owner16, 1.0, 0.0).astype(jnp.bfloat16)
    source = lax.broadcasted_iota(jnp.int32, picks_ref.shape, 0)
    owner = lax.broadcasted_iota(jnp.int32, picks_ref.shape, 1) // STEP
    picked = (source >= 10 * GROUP) & ((source & 7) == owner)
    picks_ref[...] = jnp.where(picked, 1.0, 0.0).astype(jnp.bfloat16)
    past = lax.broadcasted_iota(jnp.int32, cap_ref.shape, 0) - (
        lax.broadcasted_iota(jnp.int32, cap_ref.shape, 1) & (STEP - 1)
    )
    for copy in copies:
        copy.wait()
    tile = lax.axis_index("cols")
    start_ref[...] = jnp.full(start_ref.shape, ranges_ref[0, tile], jnp.int32)
    inside = (past >= MAXB * DB - DB * ranges_ref[1, tile]) & (past < MAXB * DB)
    cap_ref[...] = jnp.where(inside, FAR, -FAR)

    def put(pair, line, piece):
        out_ref[pair, line] = piece

    cut_all(tiles, left_ref, right_ref, left_rows, right_rows, put)


def cut_own(left, right, ranges, tiles):
    strip, width = left.shape
    rows = LEAD + width // LANES + 13
    return pl.pallas_call(
        functools.partial(own_kernel, tiles),
        out_shape=[
            jax.ShapeDtypeStruct((tiles // 2, strip, TILES, LANES), jnp.bfloat16),
            jax.ShapeDtypeStruct((8, LANES), jnp.int32),
            jax.ShapeDtypeStruct((MAXB * DB + STEP, LANES), jnp.float32),
            jax.ShapeDtypeStruct((2, 16, 2 * LANES), jnp.bfloat16),
            jax.ShapeDtypeStruct((14 * GROUP, 2 * LANES), jnp.bfloat16),
        ],
        in_specs=[HBM, HBM, HBM],
        out_specs=[VMEM] * 5,
        scratch_shapes=[
            pltpu.VMEM(left.shape, left.dtype),
            pltpu.VMEM(right.shape, right.dtype),
            pltpu.SMEM((2, tiles), jnp.int32),
            pltpu.VMEM((rows, LANES), jnp.float32),
            pltpu.VMEM((rows, LANES), jnp.float32),
            pltpu.SemaphoreType.DMA((3,)),
        ],
        compiler_params=pltpu.CompilerParams(vmem_limit_bytes=8 * 2**20),
        cost_estimate=pl.CostEstimate(flops=10**6, bytes_accessed=2**16, transcendentals=0),
    )(*[pltpu.with_memory_space_constraint(v, pltpu.HBM) for v in (left, right, ranges.T)])


def pair_kernel(bands, tiles, own_ref, left_ref, right_ref, out_ref, left_rows, right_rows):
    left_rows[...] = jnp.zeros_like(left_rows)
    right_rows[...] = jnp.zeros_like(right_rows)
    core = lax.rem(lax.axis_index("cols"), 2)
    order = chip_order(bands, tiles // 2)

    def put(pair, line, piece):
        mine = own_ref[pair, line]
        for band in range(bands):
            member = order.index(band * (tiles // 2) + pair)
            out_ref[member, core, line] = mine
            out_ref[member, 1 - core, line] = piece

    cut_all(tiles, left_ref, right_ref, left_rows, right_rows, put)


def cut_pair(own, left, right, bands, tiles):
    strip, width = left.shape
    rows = LEAD + width // LANES + 13
    return pl.pallas_call(
        functools.partial(pair_kernel, bands, tiles),
        out_shape=jax.ShapeDtypeStruct((bands * tiles // 2, 2, strip, TILES, LANES), jnp.bfloat16),
        in_specs=[VMEM, VMEM, VMEM],
        out_specs=VMEM,
        scratch_shapes=[pltpu.VMEM((rows, LANES), jnp.float32), pltpu.VMEM((rows, LANES), jnp.float32)],
        compiler_params=pltpu.CompilerParams(vmem_limit_bytes=8 * 2**20),
    )(own, left, right)


def ahead(values, by, axis):
    if by == 0:
        return values
    return pltpu.roll(values, values.shape[axis] - by, axis)


def column_sum(values):
    two = values + ahead(values, 1, 0)
    four = two + ahead(two, 2, 0)
    return (four + ahead(two, 4, 0) + ahead(values, 6, 0))[:GROUP]


def moments(shifted):
    shifted = [v.astype(jnp.float32) for v in shifted]
    total = column_sum(sum(shifted[1:], shifted[0]))
    squares = [v * v for v in shifted]
    mean = total * (1.0 / 49.0)
    spread = column_sum(sum(squares[1:], squares[0])) * (1.0 / 49.0) - mean * mean
    return total, mean, lax.rsqrt(jnp.maximum(spread, 0.01))


def parts(values):
    high = values.astype(jnp.bfloat16)
    rest = values - high.astype(jnp.float32)
    middle = rest.astype(jnp.bfloat16)
    low = (rest - middle.astype(jnp.float32)).astype(jnp.bfloat16)
    return [high, middle, low]


def tree_sum(values):
    while len(values) > 1:
        pairs = [a + b for a, b in zip(values[::2], values[1::2])]
        values = pairs + values[len(pairs) * 2 :]
    return values[0]


def fold(values):
    return functools.reduce(jnp.maximum, [values[i : i + 8] for i in range(0, values.shape[0], 8)])


def spread_out(values, lane_group):
    out = []
    for tile in range(values.shape[1] // LANES):
        here = values[:, tile * LANES : (tile + 1) * LANES]
        turned = [here] + [pltpu.roll(here, STEP * k, 1) for k in range(1, LANES // STEP)]
        for g in range(LANES // STEP):
            block = turned[0]
            for k in range(1, LANES // STEP):
                block = jnp.where(lane_group[(g + k) % (LANES // STEP)] > 0, turned[k], block)
            out.append(block)
    return out


def regroup(found):
    groups = LANES // STEP
    row = lax.broadcasted_iota(jnp.int32, (GROUP, LANES), 0)
    lane = lax.broadcasted_iota(jnp.int32, (GROUP, LANES), 1) // STEP
    halves = [found[:, h * LANES : (h + 1) * LANES] for h in range(2)]
    out = []
    for to in range(2):
        terms = []
        for half in range(2):
            for k in range(groups):
                turned = halves[half] if k == 0 else pltpu.roll(halves[half], STEP * k, 1)
                for up in sorted({(half - to) * groups - k, (half - to) * groups + (groups - k if k else 0)}):
                    chosen = (row // groups == half) & (row - (to * groups + lane) == up)
                    by = up % GROUP
                    terms.append(jnp.where(chosen, pltpu.roll(turned, by, 0) if by else turned, 0.0))
        out.append(tree_sum(terms))
    return jnp.concatenate(out, 1)


def score_kernel(order, lines_ref, start_ref, cap_ref, masks_ref, picks_ref, out_ref, rows):
    band_rows, tile_width = out_ref.shape
    reach = tile_width + MAXB * DB
    span = MAXB * DB + STEP
    window, only = masks_ref[0], masks_ref[1]
    lane16 = lax.broadcasted_iota(jnp.int32, (16, LANES), 1) // STEP
    lane_group = [jnp.where(lane16 == p, 1.0, 0.0) for p in range(LANES // STEP)]
    lane_group = [v.astype(jnp.bfloat16) for v in lane_group]
    always = (DB + STEP, MAXB * DB)
    height = lines_ref.shape[0]
    each = height // len(order)
    rows[: 3 * TILES] = jnp.zeros((3 * TILES, LANES), jnp.float32)
    rows[(height + 3) * TILES :] = jnp.zeros((6 * TILES, LANES), jnp.float32)
    for member, chip in enumerate(order):
        for line in range(each):
            at = (3 + chip * each + line) * TILES
            rows[at : at + TILES] = lines_ref[member * each + line].astype(jnp.float32)
    start = start_ref[0, 0]
    lane = lax.broadcasted_iota(jnp.int32, (16, LANES), 1)

    def moved(pieces, by):
        turned = [pltpu.roll(v, by, 1) for v in pieces]
        ahead_by = [jnp.where(lane < by, a, b) for a, b in zip(turned, turned[1:])]
        return jnp.concatenate(ahead_by, 1)

    for group in range(band_rows // GROUP):
        first = (lax.axis_index("rows") * band_rows + group * GROUP) * TILES
        tiles = [rows[pl.ds(first + t, 16, stride=TILES), :] for t in range(TILES)]
        left = jnp.concatenate(tiles[:LEFT_TILES], 1).astype(jnp.bfloat16)
        shifted_right = [moved(tiles[LEFT_TILES:], RIGHT_LEAD - 4 - j + start) for j in range(7)]
        shifted_left = [ahead(left, j, 1)[:, :tile_width] for j in range(7)]
        blank = jnp.zeros((16, reach), jnp.bfloat16)
        near_side = jnp.transpose(jnp.concatenate([v.astype(jnp.bfloat16) for v in shifted_right] + [blank], 0))
        _, right_mean, right_scale = moments(shifted_right)
        left_total, _, left_scale = moments(shifted_left)
        high, middle, low = [p.astype(jnp.float32) for p in parts(right_mean)]
        far_side = [high, high, middle, middle, low, low, high, middle, low, jnp.zeros_like(low)]
        far_side += [p.astype(jnp.float32) for p in parts(right_scale)] + [jnp.zeros_like(low)]
        far_side = jnp.transpose(jnp.concatenate(far_side, 0).astype(jnp.bfloat16))
        right_side = jnp.concatenate([near_side, far_side], 1)
        near = [spread_out(v, lane_group) for v in shifted_left]
        high, middle, low = [p.astype(jnp.float32) for p in parts(-left_total)]
        far = [jnp.concatenate(p, 0).astype(jnp.bfloat16) for p in ((high, middle), (low, low))]
        far = [spread_out(p, lane_group) for p in far]
        scale = jnp.dot(far_side, picks_ref[...], preferred_element_type=jnp.float32)
        none = jnp.zeros((16, 2 * LANES), jnp.bfloat16)
        none32 = jnp.zeros((32, 2 * LANES), jnp.bfloat16)
        found = []
        for block in range(tile_width // STEP):
            left_side = [jnp.concatenate([v[block]] * 2, 1) * window for v in near] + [none]
            two, last = [jnp.concatenate([a[block]] * 2, 1) * only for a in far]
            left_side += [two, two, two, last, last, none32]
            reached = slice(block * STEP, block * STEP + span)
            products = jnp.dot(
                right_side[reached], jnp.concatenate(left_side, 0), preferred_element_type=jnp.float32
            )
            halves = []
            for half in range(2):
                at = slice(half * LANES, (half + 1) * LANES)
                scaled = products[:, at] * scale[reached, at]
                kept = [
                    jnp.minimum(scaled[: always[0]], cap_ref[: always[0]]),
                    scaled[always[0] : always[1]],
                    jnp.minimum(scaled[always[1] :], cap_ref[always[1] :]),
                ]
                halves.append(jnp.max(functools.reduce(jnp.maximum, [fold(v) for v in kept]), axis=0, keepdims=True))
            found.append(jnp.concatenate(halves, 1))
        best = regroup(jnp.concatenate(found, 0)) * (left_scale * (1.0 / 49.0))
        out_ref[group * GROUP : (group + 1) * GROUP, :] = jnp.maximum(best, -2.0)


def score(lines, constants, order, band_rows, tile_width):
    return pl.pallas_call(
        functools.partial(score_kernel, order),
        out_shape=jax.ShapeDtypeStruct((band_rows, tile_width), jnp.float32),
        in_specs=[VMEM] * 5,
        out_specs=VMEM,
        scratch_shapes=[pltpu.VMEM(((lines.shape[0] + 9) * TILES, LANES), jnp.float32)],
        compiler_params=pltpu.CompilerParams(vmem_limit_bytes=16 * 2**20),
    )(lines, *constants)


def on_device(left_image, right_image, ranges):
    bands, tiles = lax.axis_size("rows"), lax.axis_size("cols")
    strip, width = left_image.shape
    swap = [(i, i ^ 1) for i in range(tiles)]
    left_other = lax.ppermute(left_image, "cols", swap)
    right_other = lax.ppermute(right_image, "cols", swap)
    own, *constants = cut_own(left_image, right_image, ranges, tiles)
    pieces = cut_pair(own, left_other, right_other, bands, tiles)
    order = chip_order(bands, tiles // 2)
    groups = [[2 * chip + (side if chip % (tiles // 2) else 1 - side) for chip in order] for side in range(2)]
    lines = lax.all_to_all(
        pieces, ("rows", "cols"), split_axis=0, concat_axis=0, tiled=True, axis_index_groups=groups
    )
    lines = lines.reshape(bands * tiles * strip, TILES, LANES)
    return score(lines, constants, order, strip * tiles, width // tiles)


def solution(mesh):
    return jax.shard_map(
        on_device,
        mesh=mesh,
        in_specs=(P(("rows", "cols"), None), P(("rows", "cols"), None), P()),
        out_specs=P("rows", "cols"),
        check_vma=False,
    )
```
